128 devices in a mesh: dp: 8 (over x_lo, y), grp: 16 (over x_hi, z, core).
Axes of the slice: x: 4 (x_hi: 2, x_lo: 2; x = x_hi * 2 + x_lo), y: 4, z: 4, core: 2. Of those that a mesh axis runs over, the one named last changes fastest.
Arguments:
- tokens: bfloat16 [64, 1024, 512], P('dp', 'grp'), may hold values from -6 to 6
- cotangent: bfloat16 [64, 1024, 512], P('dp', 'grp'), may hold values from -6 to 6
- w_qkv: bfloat16 [512, 1536], replicated, may hold values from -0.25 to 0.25
- w_out: bfloat16 [512, 512], replicated, may hold values from -1.5 to 1.5
- gain_attn: float32 [512], replicated, may hold values from 0.5 to 1.5
- gain_mix: float32 [512], replicated, may hold values from 0.5 to 1.5
- w_ctrl: bfloat16 [512, 16], replicated, may hold values from -0.125 to 0.125
- w_in: bfloat16 [16, 512, 2048], P('grp'), may hold values from -1.5 to 1.5
- w_back: bfloat16 [16, 2048, 512], P('grp'), may hold values from -1.5 to 1.5
- prefix: int32 [64], P('dp'), may hold values from 102 to 512
- group_ids: int32 [64, 1024], P('dp', 'grp'), may hold values from 0 to 1, as said below
Outputs:
- tokens_out: bfloat16 [64, 1024, 512], P('dp', 'grp')
- token_grad: float32 [64, 1024, 512], P('dp', 'grp')
- grad_qkv: float32 [512, 1536], replicated
- grad_out: float32 [512, 512], replicated
- grad_gain_attn: float32 [512], replicated
- grad_gain_mix: float32 [512], replicated
- grad_ctrl: float32 [512, 16], replicated
- grad_in: float32 [16, 512, 2048], P('grp')
- grad_back: float32 [16, 2048, 512], P('grp')
The draws below stay inside these ranges and needn't reach their ends.
Inputs may be any that keep to these rules, and one draw needn't show every extreme that they name: `group_ids`: in each sequence, every aligned block of 64 positions holds exactly 32 positions of each id.
All inputs are finite; a program needn't handle non-finite values.
Results may differ from the reference program's by a relative error of at most 0.02.
Values may be sent and summed in bfloat16 or wider, within the bound.
A program may use at most 128 MiB of HBM per device.

```python
import jax
import jax.numpy as jnp
from jax import lax

D = 512
HEADS = 8
HEAD_DIM = 64
EXPERTS = 16
FF = 2048
GROUP = 32
LEN = 1024
BLOCK = 64
SEQS = 64


def draw_group_ids(key, part):
    block_count = SEQS * LEN // BLOCK
    block_keys = jax.random.split(key, block_count)
    orders = jax.vmap(lambda block_key: jax.random.permutation(block_key, BLOCK))(block_keys)
    return (orders // GROUP).astype(jnp.int32).reshape(SEQS, LEN)


def plant(drawn, stream_key, smallest, high):
    shape = drawn.shape
    index_at = [jax.random.randint(jax.random.fold_in(stream_key, axis), (), 0, shape[axis]) for axis in range(len(shape))]
    drawn = drawn.at[tuple(index_at)].set(smallest)
    longest = shape.index(max(shape))
    index_at[longest] = (index_at[longest] + 1) % shape[longest]
    return drawn.at[tuple(index_at)].set(high)


def levels(key, extent, cuts, low, high):
    def one(position, blocks):
        steps = jax.random.uniform(jax.random.fold_in(jax.random.fold_in(key, 6), position), (blocks,), jnp.float32, low / len(cuts), high / len(cuts))
        return jnp.repeat(jnp.exp(steps), extent[position] // blocks).reshape((-1,) + (1,) * (len(extent) - position - 1))

    factor_of = one(*cuts[0])
    for cut in cuts[1:]:
        factor_of = factor_of * one(*cut)
    return factor_of


def normal_values(rng, shape, deviation, bound, cuts=(), held_as=jnp.bfloat16):
    loudness = levels(rng, shape, cuts, -0.22, 0.18) if cuts else 1.0
    result = jax.random.normal(rng, shape, jnp.float32) * deviation * loudness
    return jnp.minimum(jnp.maximum(result, -bound), bound).astype(held_as)


def setup_inputs(seed: int = 0) -> dict:
    arg_keys = jax.random.split(jax.random.key(seed), 12)
    return {
        "tokens": normal_values(arg_keys[0], (SEQS, LEN, D), 1.0, 6.0, ((0, 8), (1, 16))),
        "cotangent": normal_values(arg_keys[1], (SEQS, LEN, D), 1.0, 6.0, ((0, 8), (1, 16))),
        "w_qkv": normal_values(arg_keys[2], (D, 3 * D), D ** -0.5, 0.25),
        "w_out": normal_values(arg_keys[3], (D, D), (D * 32 // LEN) ** -0.5, 1.5),
        "gain_attn": jnp.clip(1.0 + 0.1 * jax.random.normal(arg_keys[4], (D,), jnp.float32), 0.5, 1.5),
        "gain_mix": jnp.clip(1.0 + 0.1 * jax.random.normal(arg_keys[5], (D,), jnp.float32), 0.5, 1.5),
        "w_ctrl": normal_values(arg_keys[6], (D, EXPERTS), (4 * D) ** -0.5, 0.125),
        "w_in": normal_values(arg_keys[7], (EXPERTS, D, FF), (D // GROUP) ** -0.5, 1.5, ((0, 16),)),
        "w_back": normal_values(arg_keys[8], (EXPERTS, FF, D), (FF * EXPERTS // (2 * GROUP * GROUP)) ** -0.5, 1.5, ((0, 16),)),
        "prefix": plant(jax.random.randint(arg_keys[9], (SEQS,), LEN // 10, LEN // 2 + 1), jax.random.fold_in(arg_keys[9], 1), LEN // 10, (LEN // 2 + 1) - 1).astype(jnp.int32),
        "group_ids": draw_group_ids(jax.random.fold_in(arg_keys[11], 71), 0),
    }


@jax.custom_vjp
def low(v):
    return lax.optimization_barrier(v.astype(jnp.bfloat16)).astype(jnp.float32)

@jax.custom_vjp
def low_back(v):
    return v

def low_keep(v):
    return (low(v), None)

def low_pass(kept, grad):
    return (grad,)

def back_keep(v):
    return (v, None)

def back_low(kept, grad):
    return (low(grad),)
low.defvjp(low_keep, low_pass)
low_back.defvjp(back_keep, back_low)
EPSILON = 1e-05
MASKED = -1e+30

def exact_product(form, left_side, right_side):
    return jnp.einsum(form, left_side, right_side, precision=lax.Precision.HIGHEST)

def layer_norm(seq_rows, gain_vec):
    row_mean = lax.optimization_barrier(jnp.mean(seq_rows, axis=-1, keepdims=True))
    centred = seq_rows - row_mean
    inv_std = lax.rsqrt(lax.optimization_barrier(jnp.mean(centred * centred, axis=-1, keepdims=True)) + EPSILON)
    return centred * inv_std * gain_vec

def block_forward(seq_rows, params, prefix_len, id_rows):
    w_qkv, w_out, gain_attn, gain_mix, w_ctrl, w_in, w_back = params
    length = seq_rows.shape[0]
    model_width = seq_rows.shape[1]
    attn_in = low(layer_norm(seq_rows, gain_attn))
    projected = low(low_back(exact_product('pd,de->pe', attn_in, w_qkv)))
    queries = projected[:, :model_width].reshape(length, HEADS, HEAD_DIM)
    keys_all = projected[:, model_width:2 * model_width].reshape(length, HEADS, HEAD_DIM)
    values_all = projected[:, 2 * model_width:].reshape(length, HEADS, HEAD_DIM)
    positions = jnp.arange(length, dtype=jnp.int32)
    visible = (positions[None, :] <= positions[:, None]) | (positions[None, :] < prefix_len)
    scores = low_back(exact_product('qhd,khd->hqk', queries, keys_all) * HEAD_DIM ** (-0.5))
    scores = jnp.where(visible[None], scores, MASKED)
    row_top = lax.optimization_barrier(jnp.max(scores, axis=-1, keepdims=True))
    exponent = jnp.exp(scores - row_top)
    attn_probs = exponent / lax.optimization_barrier(jnp.sum(exponent, axis=-1, keepdims=True))
    attn_mix = low(low_back(exact_product('hqk,khd->qhd', low(attn_probs), values_all).reshape(length, model_width)))
    resid = seq_rows + low_back(exact_product('pd,de->pe', attn_mix, w_out))
    mix_in = low(layer_norm(resid, gain_mix))
    logits = low_back(exact_product('pd,de->pe', mix_in, w_ctrl))
    blocks = length // BLOCK
    per_block = BLOCK // GROUP
    num_experts = w_ctrl.shape[1]
    member = (id_rows.reshape(blocks, BLOCK)[..., None] == jnp.arange(per_block, dtype=jnp.int32)).astype(jnp.float32)
    blocked = logits.reshape(blocks, BLOCK, num_experts)
    exp_mix = jnp.exp(blocked - lax.optimization_barrier(jnp.max(blocked, axis=1, keepdims=True)))
    totals = exact_product('nbg,nbe->nge', member, exp_mix)
    weights = exp_mix / exact_product('nbg,nge->nbe', member, totals)
    mix_coef = member[..., None] * low(weights)[:, :, None, :]
    mixed = low(low_back(exact_product('nbge,nbd->nged', mix_coef, mix_in.reshape(blocks, BLOCK, model_width))))
    mixed = mixed.reshape(blocks * per_block, num_experts, model_width)
    pre = low_back(exact_product('ged,edf->gef', mixed, w_in))
    hidden = low(low_back(jax.nn.silu(pre)))
    expert_out = low(low_back(exact_product('gef,efd->ged', hidden, w_back)))
    returned = expert_out.reshape(blocks, per_block, num_experts, model_width)
    branch = low_back(exact_product('nbge,nged->nbd', mix_coef, returned))
    return resid + branch.reshape(length, model_width)

def reference(tokens, cotangent, w_qkv, w_out, gain_attn, gain_mix, w_ctrl, w_in, w_back, prefix, group_ids):
    params = tuple((weight.astype(jnp.float32) for weight in (w_qkv, w_out, gain_attn, gain_mix, w_ctrl, w_in, w_back)))
    empty_grads = jax.tree.map(jnp.zeros_like, params)

    def one_sequence(running, inputs):
        seq_rows, grad_rows, prefix_len, id_rows = inputs

        def forward_only(rows_in, params_in):
            return block_forward(rows_in, params_in, prefix_len, id_rows)
        outputs, pullback = jax.vjp(forward_only, seq_rows.astype(jnp.float32), params)
        grad_input, grad_params = pullback(grad_rows.astype(jnp.float32))
        running = jax.tree.map(lambda left_side, right_side: left_side + right_side, running, grad_params)
        return (running, (outputs.astype(jnp.bfloat16), grad_input))
    totals, (tokens_out, token_grad) = lax.scan(one_sequence, empty_grads, (tokens, cotangent, prefix, group_ids))
    return (tokens_out, token_grad, totals[0], totals[1], totals[2], totals[3], totals[4], totals[5], totals[6])
```

```python
import functools

import jax
import jax.numpy as jnp
from jax import lax
from jax.experimental import pallas as pl
from jax.experimental.pallas import tpu as pltpu
from jax.sharding import PartitionSpec as P

HEADS = 8
HEAD_DIM = 64
GROUP = 32
BLOCK = 64
EPSILON = 1e-05
MASKED = -1e30
MESH = pl.DeviceIdType.MESH
F32 = jnp.float32
BF16 = jnp.bfloat16
SEMS = 176


def mm(a, b):
    return lax.dot_general(a, b, (((1,), (0,)), ((), ())), preferred_element_type=F32)


def mm_nt(a, b):
    return lax.dot_general(a, b, (((1,), (1,)), ((), ())), preferred_element_type=F32)


def mm_tn(a, b):
    return lax.dot_general(a, b, (((0,), (0,)), ((), ())), preferred_element_type=F32)


def unit_norm(x):
    centred = x - jnp.mean(x, axis=-1, keepdims=True)
    inv_std = lax.rsqrt(jnp.mean(centred * centred, axis=-1, keepdims=True) + EPSILON)
    return centred * inv_std, inv_std


def norm_back(up, unit, inv_std, gain):
    u = up * gain
    return inv_std * (
        u - jnp.mean(u, axis=-1, keepdims=True) - unit * jnp.mean(u * unit, axis=-1, keepdims=True)
    )


def block_kernel(
    ng, ndp, nx,
    tokens, cotangent, w_qkv, w_out, gain_attn, gain_mix, w_ctrl, w_in, w_back, prefix, group_ids,
    tokens_out, token_grad, reduced, small_out, grad_in, grad_back,
    send_sem, recv_sem, local_sem,
    x_full, cot, ids_send, ids_own, wq, wk, wv, wo, win, wback,
    attn_in, qs, ks, vs, probs, bias, linv, attn, attn_other, resid, mix_in, wc, weights, coef,
    rows_send, rows_all, back_send, back_recv, out_send, mixgrad, gresid, gbranch, gheads,
    acc_k, acc_v, act_q, act_k, act_v, part_send, part_recv, tgrad_send, pay, rs1, red1, rs2, red2, ag1,
    small_pay, small_rs1, small_sib, small_dp, small_fin, acc_b, acc_i,
):
    d, g = lax.axis_index("dp"), lax.axis_index("grp")
    nc, ny = ng // 2, ndp // nx
    c, p = g // 2, g % 2
    sib = g + 1 - 2 * p
    oth = 1 - p
    width = x_full.shape[3]
    half = width // 2
    length = ng * BLOCK
    own = nc * BLOCK
    ff = win.shape[1]
    q_rows = min(256, length // 2)
    n_q = length // q_rows
    per_q = q_rows // (2 * BLOCK)
    cols = ng * 2 * nc

    started, used = [], [0, 0]

    def number():
        used[0] += 1
        return used[0] - 1

    def send(n, src, dst, **device):
        copy = pltpu.make_async_remote_copy(
            src_ref=src, dst_ref=dst, send_sem=send_sem.at[n], recv_sem=recv_sem.at[n],
            device_id=device, device_id_type=MESH,
        )
        copy.start()
        started.append(copy)

    def arrived(n, dst):
        pltpu.make_async_remote_copy(
            src_ref=dst, dst_ref=dst, send_sem=send_sem.at[n], recv_sem=recv_sem.at[n],
            device_id={"grp": sib}, device_id_type=MESH,
        ).wait_recv()

    def local(src, dst):
        copy = pltpu.make_async_copy(src, dst, local_sem.at[used[1]])
        used[1] += 1
        copy.start()
        return copy

    def chip_at(k):
        return lax.rem(c + k, nc)

    def chip_from(k):
        return lax.rem(c + nc - k, nc)

    load_tokens = local(tokens.at[c], x_full.at[c, p])
    loads_qkv = [
        local(w_qkv.at[:, pl.ds(pl.multiple_of(part * width + p * half, 128), half)], dst)
        for part, dst in enumerate((wq, wk, wv))
    ]
    load_out = local(w_out, wo)
    load_cot = local(cotangent.at[c], cot.at[c])
    load_in = local(w_in.at[0], win)
    load_back = local(w_back.at[0], wback)
    barrier = pltpu.get_barrier_semaphore()
    for k in range(1, ng):
        pl.semaphore_signal(barrier, inc=1, device_id={"grp": lax.rem(g + k, ng)}, device_id_type=MESH)
    for k in range(1, ndp):
        pl.semaphore_signal(barrier, inc=1, device_id={"dp": lax.rem(d + k, ndp)}, device_id_type=MESH)
    for b in range(nc):
        ids_send[b] = jnp.zeros((8, 128), jnp.int32)
        ids_send[b, :, 0:BLOCK] = jnp.broadcast_to(group_ids[b : b + 1, :], (8, BLOCK))
    pl.semaphore_wait(barrier, ng + ndp - 2)

    n_tok = [number() for _ in range(nc)]
    n_fwd = [number() for _ in range(nc)]
    n_cot = [number() for _ in range(nc)]
    n_ids = [number() for _ in range(nc)]
    for k in range(1, nc):
        to = chip_at(k)
        send(n_tok[k], tokens.at[to], x_full.at[c, p], grp=to * 2 + p)
    for k in range(1, nc):
        to = chip_at(k)
        send(n_ids[k], ids_send.at[to], ids_own.at[c], grp=to * 2 + p)
    for k in range(1, nc):
        to = chip_at(k)
        send(n_cot[k], cotangent.at[to], cot.at[c], grp=to * 2 + p)
    ids_own[c] = ids_send[c]
    load_tokens.wait()
    send(n_fwd[0], x_full.at[c, p], x_full.at[c, p], grp=sib)

    prefix_len = prefix[c]
    hl = length // 2

    def mask_rows(b, carry):
        row = lax.broadcasted_iota(jnp.int32, (BLOCK, hl), 0) + b * BLOCK
        col = lax.broadcasted_iota(jnp.int32, (BLOCK, hl), 1)
        bias[pl.ds(pl.multiple_of(b * BLOCK, BLOCK), BLOCK), :] = jnp.where(
            (col <= row) | (col < prefix_len), 0.0, MASKED
        )
        return carry

    lax.fori_loop(0, hl // BLOCK, mask_rows, 0)
    spread = (
        lax.broadcasted_iota(jnp.int32, (ng, cols), 1) // (2 * nc)
        == lax.broadcasted_iota(jnp.int32, (ng, cols), 0)
    ).astype(F32)
    wc[...] = mm(w_ctrl[...].astype(F32), spread).astype(BF16)

    for k in range(1, nc):
        block = x_full.at[chip_from(k), p]
        arrived(n_tok[k], block)
        send(n_fwd[k], block, block, grp=sib)
    for load in loads_qkv:
        load.wait()

    gain_a = gain_attn[...]
    gain_m = gain_mix[...]

    def project(par):
        def rows(b, carry):
            unit, _ = unit_norm(x_full[b, par].astype(F32))
            attn_in[b, par] = (unit * gain_a).astype(BF16)
            return carry

        lax.fori_loop(0, nc, rows, 0)
        a = attn_in[:, par].reshape(own, width)
        qs[:, par] = (mm(a, wq[...]).astype(BF16) * BF16(HEAD_DIM**-0.5)).reshape(nc, BLOCK, half)
        ks[:, par] = mm(a, wk[...]).astype(BF16).reshape(nc, BLOCK, half)
        vs[:, par] = mm(a, wv[...]).astype(BF16).reshape(nc, BLOCK, half)

    project(p)
    for k in range(nc):
        arrived(n_fwd[k], x_full.at[chip_from(k), oth])
    project(oth)

    lane = lax.broadcasted_iota(jnp.int32, (1, 128), 1)
    low_lane = lane < HEAD_DIM
    keep_f = [jnp.where(low_lane, 1.0, 0.0), jnp.where(low_lane, 0.0, 1.0)]
    keep = [m.astype(BF16) for m in keep_f]
    causal = jnp.where(
        lax.broadcasted_iota(jnp.int32, (q_rows, q_rows), 1)
        <= lax.broadcasted_iota(jnp.int32, (q_rows, q_rows), 0),
        0.0,
        MASKED,
    )

    def key_range(i):
        return max(length // 2, (i + 1) * q_rows)

    def rows_of(ref, i, n, pair):
        return ref[i : i + n, :, :, pair * 128 : pair * 128 + 128].reshape(n * 2 * BLOCK, 128)

    n_mix = number()
    for i in range(n_q):
        extent = key_range(i)
        blocks = extent // (2 * BLOCK)
        for pair in range(2):
            q = rows_of(qs, i * per_q, per_q, pair)
            k_ = rows_of(ks, 0, blocks, pair)
            v_ = rows_of(vs, 0, blocks, pair)
            outs, invs = [], []
            for h in range(2):
                s = mm_nt(q * keep[h], k_)
                if (i + 1) * q_rows <= hl:
                    parts = [s + bias[i * q_rows : (i + 1) * q_rows, :]]
                else:
                    parts = [s[:, : extent - q_rows], s[:, extent - q_rows :] + causal]
                top = functools.reduce(
                    jnp.maximum, [jnp.max(part, axis=-1, keepdims=True) for part in parts]
                )
                at = 0
                for part in parts:
                    probs[pair * 2 + h, i * q_rows : (i + 1) * q_rows, at : at + part.shape[1]] = jnp.exp(part - top).astype(BF16)
                    at += part.shape[1]
                o = mm(
                    probs[pair * 2 + h, i * q_rows : (i + 1) * q_rows, :extent],
                    v_ * keep[h] + keep[1 - h],
                )
                inv = 1.0 / pltpu.roll(o, HEAD_DIM, 1)
                outs.append(o * inv)
                invs.append(inv)
            shape = (per_q, 2, BLOCK, 128)
            at = slice(pair * 128, pair * 128 + 128)
            attn[i * per_q : (i + 1) * per_q, :, :, at] = (
                jnp.where(low_lane, outs[0], outs[1]).astype(BF16).reshape(shape)
            )
            linv[i * per_q : (i + 1) * per_q, :, :, at] = jnp.where(
                low_lane, invs[0], invs[1]
            ).reshape(shape)
    send(n_mix, attn.at[:, oth], attn_other, grp=sib)
    load_out.wait()
    for k in range(1, nc):
        arrived(n_cot[k], cot.at[chip_from(k)])
        arrived(n_ids[k], ids_own.at[chip_from(k)])
    load_cot.wait()
    mixed_own = mm(attn[:, p].reshape(own, half), wo[p])
    arrived(n_mix, attn_other)
    resid[...] = (
        x_full[:, p].reshape(own, width).astype(F32)
        + mixed_own
        + mm(attn_other[...].reshape(own, half), wo[oth])
    )

    def block_rows(b):
        return pl.ds(pl.multiple_of(b * BLOCK, BLOCK), BLOCK)

    def mix_rows(b, carry):
        unit, _ = unit_norm(resid[block_rows(b), :])
        mix_in[block_rows(b), :] = (unit * gain_m).astype(BF16)
        return carry

    lax.fori_loop(0, nc, mix_rows, 0)
    weights[...] = mm(mix_in[...], wc[...])
    place = lax.broadcasted_iota(jnp.int32, (1, cols), 1) % (2 * nc)
    diagonal = lax.broadcasted_iota(jnp.int32, (BLOCK, 128), 0) == lax.broadcasted_iota(
        jnp.int32, (BLOCK, 128), 1
    )

    def member_rows(b, carry):
        ids = jnp.broadcast_to(ids_own[b, 0:1, :].astype(F32), (BLOCK, 128))
        id_col = jnp.sum(jnp.where(diagonal, ids, 0.0), axis=1, keepdims=True)
        member = (place - 2 * b).astype(F32) == id_col
        weights[block_rows(b), :] = jnp.where(member, weights[block_rows(b), :], MASKED)
        return carry

    lax.fori_loop(0, nc, member_rows, 0)
    top = jnp.max(weights[...], axis=0, keepdims=True)
    exponent = jnp.exp(weights[...] - top)
    w256 = exponent / jnp.sum(exponent, axis=0, keepdims=True)
    weights[...] = w256
    coef[...] = w256.astype(BF16)
    rows_send[0] = mm_tn(coef[...], mix_in[...]).astype(BF16).reshape(ng, 2 * nc, width)
    cot_rows = cot[...].reshape(own, width)
    rows_send[1] = mm_tn(coef[...], cot_rows).astype(BF16).reshape(ng, 2 * nc, width)

    n_rows = [number() for _ in range(ng)]
    for k in range(1, ng):
        to = lax.rem(g + k, ng)
        send(n_rows[k], rows_send.at[:, to], rows_all.at[d, :, g], grp=to)
    rows_all[d, :, g] = rows_send[:, g]
    load_in.wait()
    load_back.wait()
    for k in range(1, ng):
        arrived(n_rows[k], rows_all.at[d, :, lax.rem(g + ng - k, ng)])

    dx, dy = d // ny, d % ny
    n_m = [[number() for _ in range(ny)] for _ in range(nx)]
    n_g = [[number() for _ in range(ny)] for _ in range(nx)]
    x_to = (1 - dx) * ny + dy if nx == 2 else d

    def y_at(k, x):
        return x * ny + lax.rem(dy + k, ny)

    def y_from(k, x):
        return x * ny + lax.rem(dy + ny - k, ny)

    if nx == 2:
        send(n_m[1][0], rows_all.at[d, 0], rows_all.at[d, 0], dp=x_to)
    for k in range(1, ny):
        send(n_g[0][k], rows_all.at[d, 1], rows_all.at[d, 1], dp=y_at(k, dx))
        send(n_m[0][k], rows_all.at[d, 0], rows_all.at[d, 0], dp=y_at(k, dx))
    if nx == 2:
        send(n_g[1][0], rows_all.at[d, 1], rows_all.at[d, 1], dp=x_to)

    mixed = rows_all[d, 0].reshape(cols, width)
    gexp = rows_all[d, 1].reshape(cols, width)
    tile = min(512, ff)

    def expert_tile(f, mixed, gexp):
        at = pl.ds(pl.multiple_of(f * tile, tile), tile)
        w1, w2 = win[:, at], wback[at, :]
        pre = mm(mixed, w1)
        sig = jax.nn.sigmoid(pre)
        hidden = (pre * sig).astype(BF16)
        ghid = mm_nt(gexp, w2)
        gpre = (ghid * (sig * (1.0 + pre * (1.0 - sig)))).astype(BF16)
        return hidden, gpre, w1, w2

    e_out = g_mixed = None
    for f in range(ff // tile):
        hidden, gpre, w1, w2 = expert_tile(f, mixed, gexp)
        e_part, g_part = mm(hidden, w2), mm_nt(gpre, w1)
        e_out = e_part if e_out is None else e_out + e_part
        g_mixed = g_part if g_mixed is None else g_mixed + g_part
    back_send[0] = e_out.astype(BF16).reshape(ng, 2 * nc, width)
    back_send[1] = g_mixed.astype(BF16).reshape(ng, 2 * nc, width)
    n_back = [number() for _ in range(ng)]
    for k in range(1, ng):
        to = lax.rem(g + k, ng)
        send(n_back[k], back_send.at[:, to], back_recv.at[:, g], grp=to)
    back_recv[:, g] = back_send[:, g]

    if nx == 2:
        from_x = rows_all.at[x_to, 0]
        arrived(n_m[1][0], from_x)
        for k in range(1, ny):
            send(n_m[1][k], from_x, from_x, dp=y_at(k, dx))
    for k in range(1, ng):
        arrived(n_back[k], back_recv.at[:, lax.rem(g + ng - k, ng)])

    e_rows = back_recv[0].reshape(cols, width)
    g_rows = back_recv[1].reshape(cols, width)
    out_send[...] = (resid[...] + mm(coef[...], e_rows)).astype(BF16).reshape(nc, BLOCK, width)
    n_out = [number() for _ in range(nc)]
    for k in range(1, nc):
        to = chip_at(k)
        send(n_out[k], out_send.at[to], tokens_out.at[c], grp=to * 2 + p)
    keep_out = local(out_send.at[c], tokens_out.at[c])
    dots = mm_nt(cot_rows, e_rows) + mm_nt(mix_in[...], g_rows)
    w256 = weights[...]
    inner = jnp.sum(w256 * dots, axis=0, keepdims=True)
    glogit = (w256 * (dots - inner)).astype(BF16)
    mixgrad[...] = mm(coef[...], g_rows) + mm_nt(glogit, wc[...])
    ctrl = mm_tn(glogit, mix_in[...]).reshape(ng, 2 * nc, width).sum(axis=1)

    def resid_rows(b, total):
        unit, inv_std = unit_norm(resid[block_rows(b), :])
        up = mixgrad[block_rows(b), :]
        grad = cot[b].astype(F32) + norm_back(up, unit, inv_std, gain_m)
        gresid[block_rows(b), :] = grad
        gbranch[p, b] = grad.astype(BF16)
        return total + jnp.sum(up * unit, axis=0, keepdims=True)

    gain_m_part = lax.fori_loop(0, nc, resid_rows, jnp.zeros((1, width), F32))
    n_branch = number()
    send(n_branch, gbranch.at[p], gbranch.at[p], grp=sib)

    def head_grads(par):
        raw = mm_nt(gbranch[par].reshape(own, width), wo[p])
        scaled = (raw * linv[:, par].reshape(own, half)).astype(BF16)
        prod = scaled.astype(F32) * attn[:, par].reshape(own, half).astype(F32)
        for pair in range(2):
            at = slice(pair * 128, pair * 128 + 128)
            for h in range(2):
                delta = jnp.sum(prod[:, at] * keep_f[h], axis=1, keepdims=True)
                high = delta.astype(BF16).astype(F32)
                low = delta - high
                first = HEAD_DIM * (1 - h)
                extra = jnp.where(lane == first, -high, jnp.where(lane == first + 1, -low, 0.0))
                gheads[pair * 2 + h, :, par] = (
                    scaled[:, at] * keep[h] + extra.astype(BF16)
                ).reshape(nc, BLOCK, 128)

    head_grads(p)
    arrived(n_branch, gbranch.at[oth])
    head_grads(oth)

    if nx == 2:
        arrived(n_g[1][0], rows_all.at[x_to, 1])
        for k in range(1, ny):
            block = rows_all.at[y_from(k, dx), 1]
            arrived(n_g[0][k], block)
            send(n_g[1][k], block, block, dp=x_to)
    else:
        for k in range(1, ny):
            arrived(n_g[0][k], rows_all.at[y_from(k, dx), 1])

    acc_k[...] = jnp.zeros_like(acc_k)
    acc_v[...] = jnp.zeros_like(acc_v)
    for i in range(n_q):
        extent = key_range(i)
        blocks = extent // (2 * BLOCK)
        span = slice(i * q_rows, (i + 1) * q_rows)
        for pair in range(2):
            at = slice(pair * 128, pair * 128 + 128)
            q = rows_of(qs, i * per_q, per_q, pair)
            k_ = rows_of(ks, 0, blocks, pair)
            v_ = rows_of(vs, 0, blocks, pair)
            grads, dqs = [], []
            for h in range(2):
                up = gheads[pair * 2 + h, i * per_q : (i + 1) * per_q].reshape(q_rows, 128)
                dp = mm_nt(up, v_ * keep[h] + keep[1 - h]).astype(BF16)
                ds = probs[pair * 2 + h, span, :extent] * dp
                grads.append(up * keep[h])
                dqs.append(mm(ds, k_))
                part_k = mm_tn(ds, q * keep[h])
                part_v = mm_tn(probs[pair * 2 + h, span, :extent], grads[h])
                acc_k[:extent, at] += part_k
                acc_v[:extent, at] += part_v
            act_q[i * per_q : (i + 1) * per_q, :, :, at] = (
                (jnp.where(low_lane, dqs[0], dqs[1]) * HEAD_DIM**-0.5)
                .astype(BF16)
                .reshape(per_q, 2, BLOCK, 128)
            )
    act_k[...] = acc_k[...].astype(BF16).reshape(nc, 2, BLOCK, half)
    act_v[...] = acc_v[...].astype(BF16).reshape(nc, 2, BLOCK, half)

    def act_grad(par):
        return sum(
            mm_nt(act[:, par].reshape(own, half), w[...])
            for act, w in ((act_q, wq), (act_k, wk), (act_v, wv))
        )

    part_send[...] = act_grad(oth).astype(BF16).reshape(nc, BLOCK, width)
    n_part = number()
    send(n_part, part_send, part_recv, grp=sib)
    mixgrad[...] = act_grad(p)

    a = attn_in[...].reshape(length, width)
    for part, act in enumerate((act_q, act_k, act_v)):
        grad = mm_tn(a, act[...].reshape(length, half)).astype(BF16)
        pay[part * half : (part + 1) * half, :half] = grad[:half]
        pay[part * half : (part + 1) * half, half:] = grad[half:]
    pay[3 * half : 4 * half, :] = sum(
        mm_tn(attn[:, par].reshape(own, half), gbranch[par].reshape(own, width)) for par in range(2)
    ).astype(BF16)
    ra = 4 * half // nc
    rb = ra // ndp
    n_rs1 = [number() for _ in range(nc)]
    for k in range(1, nc):
        to = chip_at(k)
        send(n_rs1[k], pay.at[pl.ds(pl.multiple_of(to * ra, ra), ra)], rs1.at[c], grp=to * 2 + p)

    arrived(n_part, part_recv)

    def grad_rows(b, total):
        unit, inv_std = unit_norm(x_full[b, p].astype(F32))
        up = mixgrad[block_rows(b), :] + part_recv[b].astype(F32)
        grad = gresid[block_rows(b), :] + norm_back(up, unit, inv_std, gain_a)
        tgrad_send[b] = grad.astype(BF16)
        return total + jnp.sum(up * unit, axis=0, keepdims=True)

    gain_a_part = lax.fori_loop(0, nc, grad_rows, jnp.zeros((1, width), F32))
    n_tg = [number() for _ in range(nc)]
    for k in range(1, nc):
        to = chip_at(k)
        send(n_tg[k], tgrad_send.at[to], token_grad.at[c], grp=to * 2 + p)
    keep_tg = local(tgrad_send.at[c], token_grad.at[c])

    tiles = 8 // nc
    for j in range(8):
        r, l = j // 4, j % 4
        if ng >= 8 * (r + 1):
            small_pay[j // tiles, j % tiles] = ctrl[r * 8 : r * 8 + 8, l * 128 : l * 128 + 128]
        else:
            small_pay[j // tiles, j % tiles] = jnp.zeros((8, 128), F32)
            if ng > 8 * r:
                small_pay[j // tiles, j % tiles, : ng - 8 * r] = ctrl[r * 8 : ng, l * 128 : l * 128 + 128]
    for j in range(nc):
        for l in range(4):
            small_pay[j, tiles, l : l + 1] = gain_a_part[:, l * 128 : l * 128 + 128]
            small_pay[j, tiles, 4 + l : 5 + l] = gain_m_part[:, l * 128 : l * 128 + 128]
    n_s1 = [number() for _ in range(nc)]
    for k in range(1, nc):
        to = chip_at(k)
        send(n_s1[k], small_pay.at[to], small_rs1.at[c], grp=to * 2 + p)
    small_rs1[c] = small_pay[c]
    rs1[c] = pay[pl.ds(pl.multiple_of(c * ra, ra), ra), :]

    for k in range(1, nc):
        arrived(n_rs1[k], rs1.at[chip_from(k)])
    total = rs1[0].astype(F32)
    for j in range(1, nc):
        total = total + rs1[j].astype(F32)
    red1[...] = total.astype(BF16)
    n_rs2 = [number() for _ in range(ndp)]
    for k in range(1, ndp):
        to = lax.rem(d + k, ndp)
        send(n_rs2[k], red1.at[pl.ds(pl.multiple_of(to * rb, rb), rb)], rs2.at[d], dp=to)
    rs2[d] = red1[pl.ds(pl.multiple_of(d * rb, rb), rb), :]
    for k in range(1, nc):
        arrived(n_s1[k], small_rs1.at[chip_from(k)])
    small_sib[p] = small_rs1[...].sum(axis=0)
    n_ss = number()
    send(n_ss, small_sib.at[p], small_sib.at[p], grp=sib)

    if nx == 2:
        for k in range(1, ny):
            arrived(n_g[1][k], rows_all.at[y_from(k, 1 - dx), 1])
            arrived(n_m[1][k], rows_all.at[y_from(k, 1 - dx), 0])
    for k in range(1, ny):
        arrived(n_m[0][k], rows_all.at[y_from(k, dx), 0])

    for k in range(1, ndp):
        arrived(n_rs2[k], rs2.at[lax.rem(d + ndp - k, ndp)])
    total = rs2[0].astype(F32)
    for j in range(1, ndp):
        total = total + rs2[j].astype(F32)
    red2[...] = total.astype(BF16)
    n_ag1 = [number() for _ in range(ndp)]
    mine = ag1.at[pl.ds(pl.multiple_of(d * rb, rb), rb)]
    for k in range(1, ndp):
        send(n_ag1[k], red2, mine, dp=lax.rem(d + k, ndp))
    ag1[pl.ds(pl.multiple_of(d * rb, rb), rb), :] = red2[...]
    arrived(n_ss, small_sib.at[oth])
    small_dp[d] = small_sib[0] + small_sib[1]
    n_sd = [number() for _ in range(ndp)]
    for k in range(1, ndp):
        send(n_sd[k], small_dp.at[d], small_dp.at[d], dp=lax.rem(d + k, ndp))

    step = min(2, ndp)
    n_half = 2
    for f in range(ff // tile):
        if f == 1:
            for k in range(1, ndp):
                frm = lax.rem(d + ndp - k, ndp)
                arrived(n_ag1[k], ag1.at[pl.ds(pl.multiple_of(frm * rb, rb), rb)])
            n_ag2 = [number() for _ in range(nc)]
            n_ag3 = [number() for _ in range(nc)]
            place_c = reduced.at[p, pl.ds(pl.multiple_of(c * ra, ra), ra)]
            for k in range(1, nc):
                send(n_ag2[k], ag1, place_c, grp=chip_at(k) * 2 + p)
            send(n_ag3[0], ag1, place_c, grp=sib)
            keep_red = local(ag1, place_c)
            for k in range(1, ndp):
                arrived(n_sd[k], small_dp.at[lax.rem(d + ndp - k, ndp)])
            small_fin[...] = small_dp[...].sum(axis=0)
            n_sg = [number() for _ in range(nc)]
            for k in range(1, nc):
                send(n_sg[k], small_fin, small_out.at[c], grp=chip_at(k) * 2 + p)
            keep_small = local(small_fin, small_out.at[c])
        if f == ff // tile - 1:
            for k in range(1, nc):
                place_k = reduced.at[p, pl.ds(pl.multiple_of(chip_from(k) * ra, ra), ra)]
                arrived(n_ag2[k], place_k)
                send(n_ag3[k], place_k, place_k, grp=sib)
        slot = f % n_half

        def chunk(j, carry, f=f, slot=slot):
            m_rows = rows_all[pl.ds(j * step, step), 0].reshape(step * cols, width)
            g_rows = rows_all[pl.ds(j * step, step), 1].reshape(step * cols, width)
            hidden, gpre, _, _ = expert_tile(f, m_rows, g_rows)
            part_b, part_i = mm_tn(hidden, g_rows), mm_tn(m_rows, gpre)

            @pl.when(j == 0)
            def _():
                acc_b[slot] = part_b
                acc_i[slot] = part_i

            @pl.when(j > 0)
            def _():
                acc_b[slot] += part_b
                acc_i[slot] += part_i

            return carry

        if f >= n_half:
            stores[f - n_half][0].wait()
            stores[f - n_half][1].wait()
        else:
            stores = [] if f == 0 else stores
        lax.fori_loop(0, ndp // step, chunk, 0)
        stores.append(
            (
                local(acc_b.at[slot], grad_back.at[0, f * tile : (f + 1) * tile, :]),
                local(acc_i.at[slot], grad_in.at[0, :, f * tile : (f + 1) * tile]),
            )
        )

    for b, i in stores[-n_half:]:
        b.wait()
        i.wait()
    for k in range(1, nc):
        arrived(n_out[k], tokens_out.at[chip_from(k)])
        arrived(n_tg[k], token_grad.at[chip_from(k)])
        arrived(n_sg[k], small_out.at[chip_from(k)])
    for k in range(nc):
        arrived(n_ag3[k], reduced.at[oth, pl.ds(pl.multiple_of(chip_from(k) * ra, ra), ra)])
    for copy in (keep_out, keep_tg, keep_red, keep_small):
        copy.wait()
    for copy in started:
        copy.wait_send()


def on_device(
    ng, ndp, nx,
    tokens, cotangent, w_qkv, w_out, gain_attn, gain_mix, w_ctrl, w_in, w_back, prefix, group_ids,
):
    nc = ng // 2
    width = tokens.shape[2]
    half = width // 2
    length, own = ng * BLOCK, nc * BLOCK
    ff = w_in.shape[2]
    cols = ng * 2 * nc
    ra = 4 * half // nc
    tile = min(512, ff)
    tiles = 8 // nc
    vm = pltpu.VMEM
    anywhere = pl.BlockSpec(memory_space=pl.ANY)
    in_vmem = pl.BlockSpec(memory_space=pltpu.VMEM)
    in_smem = pl.BlockSpec(memory_space=pltpu.SMEM)
    scratch = [
        pltpu.SemaphoreType.DMA((SEMS,)),
        pltpu.SemaphoreType.DMA((SEMS,)),
        pltpu.SemaphoreType.DMA((32,)),
        vm((nc, 2, BLOCK, width), BF16),
        vm((nc, BLOCK, width), BF16),
        vm((nc, 8, 128), jnp.int32),
        vm((nc, 8, 128), jnp.int32),
        vm((width, half), BF16),
        vm((width, half), BF16),
        vm((width, half), BF16),
        vm((2, half, width), BF16),
        vm((width, ff), BF16),
        vm((ff, width), BF16),
        vm((nc, 2, BLOCK, width), BF16),
        vm((nc, 2, BLOCK, half), BF16),
        vm((nc, 2, BLOCK, half), BF16),
        vm((nc, 2, BLOCK, half), BF16),
        vm((4, length, length), BF16),
        vm((length // 2, length // 2), F32),
        vm((nc, 2, BLOCK, half), F32),
        vm((nc, 2, BLOCK, half), BF16),
        vm((nc, BLOCK, half), BF16),
        vm((own, width), F32),
        vm((own, width), BF16),
        vm((width, cols), BF16),
        vm((own, cols), F32),
        vm((own, cols), BF16),
        vm((2, ng, 2 * nc, width), BF16),
        vm((ndp, 2, ng, 2 * nc, width), BF16),
        vm((2, ng, 2 * nc, width), BF16),
        vm((2, ng, 2 * nc, width), BF16),
        vm((nc, BLOCK, width), BF16),
        vm((own, width), F32),
        vm((own, width), F32),
        vm((2, nc, BLOCK, width), BF16),
        vm((4, nc, 2, BLOCK, 128), BF16),
        vm((length, half), F32),
        vm((length, half), F32),
        vm((nc, 2, BLOCK, half), BF16),
        vm((nc, 2, BLOCK, half), BF16),
        vm((nc, 2, BLOCK, half), BF16),
        vm((nc, BLOCK, width), BF16),
        vm((nc, BLOCK, width), BF16),
        vm((nc, BLOCK, width), BF16),
        vm((4 * half, width), BF16),
        vm((nc, ra, width), BF16),
        vm((ra, width), BF16),
        vm((ndp, ra // ndp, width), BF16),
        vm((ra // ndp, width), BF16),
        vm((ra, width), BF16),
        vm((nc, tiles + 1, 8, 128), F32),
        vm((nc, tiles + 1, 8, 128), F32),
        vm((2, tiles + 1, 8, 128), F32),
        vm((ndp, tiles + 1, 8, 128), F32),
        vm((tiles + 1, 8, 128), F32),
        vm((2, tile, width), F32),
        vm((2, width, tile), F32),
    ]
    tokens_out, token_grad, reduced, small, grad_in, grad_back = pl.pallas_call(
        functools.partial(block_kernel, ng, ndp, nx),
        out_shape=[
            jax.ShapeDtypeStruct(tokens.shape, BF16),
            jax.ShapeDtypeStruct(tokens.shape, BF16),
            jax.ShapeDtypeStruct((2, 4 * half, width), BF16),
            jax.ShapeDtypeStruct((nc, tiles + 1, 8, 128), F32),
            jax.ShapeDtypeStruct(w_in.shape, F32),
            jax.ShapeDtypeStruct(w_back.shape, F32),
        ],
        in_specs=[anywhere] * 4 + [in_vmem] * 3 + [anywhere] * 2 + [in_smem, in_vmem],
        out_specs=[anywhere] * 6,
        scratch_shapes=scratch,
        compiler_params=pltpu.CompilerParams(
            collective_id=0, has_side_effects=True, vmem_limit_bytes=60 * 1024 * 1024
        ),
        name="of_tokens_block",
    )(
        tokens, cotangent, w_qkv, w_out.reshape(2, half, width), gain_attn.reshape(1, width),
        gain_mix.reshape(1, width), w_ctrl, w_in, w_back, prefix, group_ids,
    )
    halves = reduced.reshape(2, 4, half, 2, half)
    grad_qkv = halves[:, :3].transpose(3, 2, 1, 0, 4).reshape(width, 3 * width).astype(F32)
    grad_out = reduced[:, 3 * half :].reshape(width, width).astype(F32)
    ctrl_tiles = small[:, :tiles].reshape(2, 4, 8, 128).transpose(0, 2, 1, 3).reshape(16, width)
    grad_ctrl = ctrl_tiles[:ng].T
    grad_gain_attn = small[0, tiles, :4].reshape(width)
    grad_gain_mix = small[0, tiles, 4:].reshape(width)
    return (
        tokens_out,
        token_grad.astype(F32),
        grad_qkv,
        grad_out,
        grad_gain_attn,
        grad_gain_mix,
        grad_ctrl,
        grad_in,
        grad_back,
    )


def solution(mesh):
    ng, ndp = mesh.shape["grp"], mesh.shape["dp"]
    in_specs = (
        P("dp", "grp", None),
        P("dp", "grp", None),
        P(),
        P(),
        P(),
        P(),
        P(),
        P("grp", None, None),
        P("grp", None, None),
        P("dp"),
        P("dp", "grp"),
    )
    out_specs = (
        P("dp", "grp", None),
        P("dp", "grp", None),
        P(),
        P(),
        P(),
        P(),
        P(),
        P("grp", None, None),
        P("grp", None, None),
    )
    return jax.shard_map(
        functools.partial(on_device, ng, ndp, 2),
        mesh=mesh, in_specs=in_specs, out_specs=out_specs, check_vma=False,
    )
```

```python
import functools

import jax
import jax.numpy as jnp
from jax import lax
from jax.experimental import pallas as pl
from jax.experimental.pallas import tpu as pltpu
from jax.sharding import PartitionSpec as P

HEADS = 8
HEAD_DIM = 64
GROUP = 32
BLOCK = 64
EPSILON = 1e-05
MASKED = -1e30
MESH = pl.DeviceIdType.MESH
F32 = jnp.float32
BF16 = jnp.bfloat16
SEMS = 288


def mm(a, b):
    return lax.dot_general(a, b, (((1,), (0,)), ((), ())), preferred_element_type=F32)


def mm_nt(a, b):
    return lax.dot_general(a, b, (((1,), (1,)), ((), ())), preferred_element_type=F32)


def mm_tn(a, b):
    return lax.dot_general(a, b, (((0,), (0,)), ((), ())), preferred_element_type=F32)


def unit_norm(x):
    centred = x - jnp.mean(x, axis=-1, keepdims=True)
    inv_std = lax.rsqrt(jnp.mean(centred * centred, axis=-1, keepdims=True) + EPSILON)
    return centred * inv_std, inv_std


def norm_back(up, unit, inv_std, gain):
    u = up * gain
    return inv_std * (
        u - jnp.mean(u, axis=-1, keepdims=True) - unit * jnp.mean(u * unit, axis=-1, keepdims=True)
    )


def block_kernel(
    ng, ndp, nx,
    tokens, cotangent, w_qkv, w_out, gain_attn, gain_mix, w_ctrl, w_in, w_back, prefix, group_ids,
    tokens_out, token_grad, reduced, small_out, grad_in, grad_back,
    send_sem, recv_sem, local_sem,
    x_full, cot, ids_send, ids_own, wq, wk, wv, wo, win, wback,
    attn_in, qs, ks, vs, bias, linv, attn, attn_other, resid, mix_in, wc, weights, coef,
    rows_send, rows_all, back_send, back_recv, out_send, mixgrad, gresid, gbranch, gheads,
    acc_k, acc_v, act_q, act_k, act_v, part_send, part_recv, tgrad_send, pay, rs1, red1, rs2, red2, ag1,
    small_pay, small_rs1, small_sib, small_dp, small_fin, hid, gpr, out_b, out_i,
):
    d, g = lax.axis_index("dp"), lax.axis_index("grp")
    nc, ny = ng // 2, ndp // nx
    c, p = g // 2, g % 2
    sib = g + 1 - 2 * p
    oth = 1 - p
    width = x_full.shape[3]
    half = width // 2
    length = ng * BLOCK
    own = nc * BLOCK
    ff = win.shape[1]
    q_rows = min(256, length // 2)
    n_q = length // q_rows
    per_q = q_rows // (2 * BLOCK)
    cols = ng * 2 * nc

    started, used = [], [0, 0]

    def number():
        used[0] += 1
        return used[0] - 1

    def send(n, src, dst, **device):
        copy = pltpu.make_async_remote_copy(
            src_ref=src, dst_ref=dst, send_sem=send_sem.at[n], recv_sem=recv_sem.at[n],
            device_id=device, device_id_type=MESH,
        )
        copy.start()
        started.append(copy)

    def arrived(n, dst):
        pltpu.make_async_remote_copy(
            src_ref=dst, dst_ref=dst, send_sem=send_sem.at[n], recv_sem=recv_sem.at[n],
            device_id={"grp": sib}, device_id_type=MESH,
        ).wait_recv()

    def local(src, dst):
        copy = pltpu.make_async_copy(src, dst, local_sem.at[used[1]])
        used[1] += 1
        copy.start()
        return copy

    def chip_at(k):
        return lax.rem(c + k, nc)

    def chip_from(k):
        return lax.rem(c + nc - k, nc)

    load_tokens = local(tokens.at[c], x_full.at[c, p])
    loads_qkv = [
        local(w_qkv.at[:, pl.ds(pl.multiple_of(part * width + p * half, 128), half)], dst)
        for part, dst in enumerate((wq, wk, wv))
    ]
    load_out = local(w_out, wo)
    load_cot = local(cotangent.at[c], cot.at[c])
    load_in = local(w_in.at[0], win)
    load_back = local(w_back.at[0], wback)
    barrier = pltpu.get_barrier_semaphore()
    for k in range(1, ng):
        pl.semaphore_signal(barrier, inc=1, device_id={"grp": lax.rem(g + k, ng)}, device_id_type=MESH)
    for k in range(1, ndp):
        pl.semaphore_signal(barrier, inc=1, device_id={"dp": lax.rem(d + k, ndp)}, device_id_type=MESH)
    for b in range(nc):
        ids_send[b] = jnp.zeros((8, 128), jnp.int32)
        ids_send[b, :, 0:BLOCK] = jnp.broadcast_to(group_ids[b : b + 1, :], (8, BLOCK))
    nz = nc // 2
    dx, dy = d // ny, d % ny
    xh, z = c // nz, c % nz
    plane_a, plane_b = 2 * ndp, 2 * nc
    at_a, at_b = xh * ndp + d, dx * nc + c

    def device_a(a):
        return {"dp": a % ndp, "grp": (a // ndp * nz + z) * 2 + p}

    def device_b(b):
        return {"dp": b // nc * ny + dy, "grp": b % nc * 2 + p}

    for k in range(1, ndp):
        far = {"dp": lax.rem(d + k, ndp), "grp": ((1 - xh) * nz + z) * 2 + p}
        pl.semaphore_signal(barrier, inc=1, device_id=far, device_id_type=MESH)
    for k in range(1, nc):
        far = {"dp": (1 - dx) * ny + dy, "grp": chip_at(k) * 2 + p}
        pl.semaphore_signal(barrier, inc=1, device_id=far, device_id_type=MESH)
    pl.semaphore_wait(barrier, 2 * ndp + ng + nc - 4)

    n_tok = [number() for _ in range(nc)]
    n_fwd = [number() for _ in range(nc)]
    n_cot = [number() for _ in range(nc)]
    n_ids = [number() for _ in range(nc)]
    for k in range(1, nc):
        to = chip_at(k)
        send(n_tok[k], tokens.at[to], x_full.at[c, p], grp=to * 2 + p)
    for k in range(1, nc):
        to = chip_at(k)
        send(n_ids[k], ids_send.at[to], ids_own.at[c], grp=to * 2 + p)
    for k in range(1, nc):
        to = chip_at(k)
        send(n_cot[k], cotangent.at[to], cot.at[c], grp=to * 2 + p)
    ids_own[c] = ids_send[c]
    load_tokens.wait()
    send(n_fwd[0], x_full.at[c, p], x_full.at[c, p], grp=sib)

    prefix_len = prefix[c]
    hl = length // 2

    def mask_rows(b, carry):
        row = lax.broadcasted_iota(jnp.int32, (BLOCK, hl), 0) + b * BLOCK
        col = lax.broadcasted_iota(jnp.int32, (BLOCK, hl), 1)
        bias[pl.ds(pl.multiple_of(b * BLOCK, BLOCK), BLOCK), :] = jnp.where(
            (col <= row) | (col < prefix_len), 0.0, MASKED
        )
        return carry

    lax.fori_loop(0, hl // BLOCK, mask_rows, 0)
    spread = (
        lax.broadcasted_iota(jnp.int32, (ng, cols), 1) // (2 * nc)
        == lax.broadcasted_iota(jnp.int32, (ng, cols), 0)
    ).astype(F32)
    wc[...] = mm_tn(w_ctrl[...].astype(F32), spread).astype(BF16)

    for k in range(1, nc):
        block = x_full.at[chip_from(k), p]
        arrived(n_tok[k], block)
        send(n_fwd[k], block, block, grp=sib)
    for load in loads_qkv:
        load.wait()

    gain_a = gain_attn[...]
    gain_m = gain_mix[...]

    def project(par):
        def rows(b, carry):
            unit, _ = unit_norm(x_full[b, par].astype(F32))
            attn_in[b, par] = (unit * gain_a).astype(BF16)
            return carry

        lax.fori_loop(0, nc, rows, 0)
        a = attn_in[:, par].reshape(own, width)
        qs[:, par] = (mm(a, wq[...]).astype(BF16) * BF16(HEAD_DIM**-0.5)).reshape(nc, BLOCK, half)
        ks[:, par] = mm(a, wk[...]).astype(BF16).reshape(nc, BLOCK, half)
        vs[:, par] = mm(a, wv[...]).astype(BF16).reshape(nc, BLOCK, half)

    project(p)
    for k in range(nc):
        arrived(n_fwd[k], x_full.at[chip_from(k), oth])
    project(oth)

    lane = lax.broadcasted_iota(jnp.int32, (1, 128), 1)
    low_lane = lane < HEAD_DIM
    keep_f = [jnp.where(low_lane, 1.0, 0.0), jnp.where(low_lane, 0.0, 1.0)]
    keep = [m.astype(BF16) for m in keep_f]
    causal = jnp.where(
        lax.broadcasted_iota(jnp.int32, (q_rows, q_rows), 1)
        <= lax.broadcasted_iota(jnp.int32, (q_rows, q_rows), 0),
        0.0,
        MASKED,
    )

    def pieces(i):
        end = (i + 1) * q_rows
        return [(0, hl)] + ([(hl, end - hl)] if end > hl else [])

    def held(head, i, n):
        span = slice(n * length + i * q_rows, n * length + (i + 1) * q_rows)
        return hid.at[head, span, : pieces(i)[n][1]]

    def rows_of(ref, i, n, pair):
        return ref[i : i + n, :, :, pair * 128 : pair * 128 + 128].reshape(n * 2 * BLOCK, 128)

    n_mix = number()
    for i in range(n_q):
        for pair in range(2):
            q = rows_of(qs, i * per_q, per_q, pair)
            outs, invs = [], []
            for h in range(2):
                parts = []
                for start, size in pieces(i):
                    k_ = rows_of(ks, start // (2 * BLOCK), size // (2 * BLOCK), pair)
                    s = mm_nt(q * keep[h], k_)
                    if (i + 1) * q_rows <= hl:
                        s = s + bias[i * q_rows : (i + 1) * q_rows, :]
                    elif start == hl:
                        last = s[:, size - q_rows :] + causal
                        s = last if size == q_rows else jnp.concatenate([s[:, : size - q_rows], last], axis=1)
                    parts.append(s)
                top = functools.reduce(
                    jnp.maximum, [jnp.max(part, axis=-1, keepdims=True) for part in parts]
                )
                o = None
                for n, (start, size) in enumerate(pieces(i)):
                    low = jnp.exp(parts[n] - top).astype(BF16)
                    held(pair * 2 + h, i, n)[...] = low
                    v_ = rows_of(vs, start // (2 * BLOCK), size // (2 * BLOCK), pair)
                    term = mm(low, v_ * keep[h] + keep[1 - h])
                    o = term if o is None else o + term
                inv = 1.0 / pltpu.roll(o, HEAD_DIM, 1)
                outs.append(o * inv)
                invs.append(inv)
            shape = (per_q, 2, BLOCK, 128)
            at = slice(pair * 128, pair * 128 + 128)
            attn[i * per_q : (i + 1) * per_q, :, :, at] = (
                jnp.where(low_lane, outs[0], outs[1]).astype(BF16).reshape(shape)
            )
            linv[i * per_q : (i + 1) * per_q, :, :, at] = jnp.where(
                low_lane, invs[0], invs[1]
            ).reshape(shape)
    send(n_mix, attn.at[:, oth], attn_other, grp=sib)
    load_out.wait()
    for k in range(1, nc):
        arrived(n_cot[k], cot.at[chip_from(k)])
        arrived(n_ids[k], ids_own.at[chip_from(k)])
    load_cot.wait()
    mixed_own = mm(attn[:, p].reshape(own, half), wo[p])
    arrived(n_mix, attn_other)
    resid[...] = (
        x_full[:, p].reshape(own, width).astype(F32)
        + mixed_own
        + mm(attn_other[...].reshape(own, half), wo[oth])
    )

    def block_rows(b):
        return pl.ds(pl.multiple_of(b * BLOCK, BLOCK), BLOCK)

    def mix_rows(b, carry):
        unit, _ = unit_norm(resid[block_rows(b), :])
        mix_in[block_rows(b), :] = (unit * gain_m).astype(BF16)
        return carry

    lax.fori_loop(0, nc, mix_rows, 0)
    weights[...] = mm(mix_in[...], wc[...])
    place = lax.broadcasted_iota(jnp.int32, (1, cols), 1) % (2 * nc)
    diagonal = lax.broadcasted_iota(jnp.int32, (BLOCK, 128), 0) == lax.broadcasted_iota(
        jnp.int32, (BLOCK, 128), 1
    )

    def member_rows(b, carry):
        ids = jnp.broadcast_to(ids_own[b, 0:1, :].astype(F32), (BLOCK, 128))
        id_col = jnp.sum(jnp.where(diagonal, ids, 0.0), axis=1, keepdims=True)
        member = (place - 2 * b).astype(F32) == id_col
        weights[block_rows(b), :] = jnp.where(member, weights[block_rows(b), :], MASKED)
        return carry

    lax.fori_loop(0, nc, member_rows, 0)
    top = jnp.max(weights[...], axis=0, keepdims=True)
    exponent = jnp.exp(weights[...] - top)
    w256 = exponent / jnp.sum(exponent, axis=0, keepdims=True)
    weights[...] = w256
    coef[...] = w256.astype(BF16)
    cot_rows = cot[...].reshape(own, width)

    load_in.wait()
    load_back.wait()
    n_rows = [[number() for _ in range(ng)] for _ in range(2)]
    for kind, source in enumerate((mix_in[...], cot_rows)):
        rows_send[kind] = mm_tn(coef[...], source).astype(BF16).reshape(ng, 2 * nc, width)
        for k in range(1, ng):
            to = lax.rem(g + k, ng)
            send(n_rows[kind][k], rows_send.at[kind, to], rows_all.at[d, kind, g], grp=to)
        rows_all[d, kind, g] = rows_send[kind, g]

    def rows_arrived(kind):
        for k in range(1, ng):
            arrived(n_rows[kind][k], rows_all.at[d, kind, lax.rem(g + ng - k, ng)])

    rows_arrived(0)

    tile = min(512, ff)
    n_f = ff // tile
    n_back = [[number() for _ in range(ng)] for _ in range(2)]

    def send_back(kind, rows):
        back_send[kind] = rows.astype(BF16).reshape(ng, 2 * nc, width)
        for k in range(1, ng):
            to = lax.rem(g + k, ng)
            send(n_back[kind][k], back_send.at[kind, to], back_recv.at[kind, g], grp=to)
        back_recv[kind, g] = back_send[kind, g]

    def back_arrived(kind):
        for k in range(1, ng):
            arrived(n_back[kind][k], back_recv.at[kind, lax.rem(g + ng - k, ng)])

    def silu_and_slope(pre):
        sig = 0.5 + 0.5 * jnp.tanh(0.5 * pre)
        silu = pre * sig
        return silu, sig + silu * (1.0 - sig)

    mixed = rows_all[d, 0].reshape(cols, width)
    e_out, slopes = None, []
    for f in range(n_f):
        at = slice(f * tile, (f + 1) * tile)
        silu, slope = silu_and_slope(mm(mixed, win[:, at]))
        slopes.append(slope)
        part = mm(silu.astype(BF16), wback[at, :])
        e_out = part if e_out is None else e_out + part
    send_back(0, e_out)

    rows_arrived(1)
    gexp = rows_all[d, 1].reshape(cols, width)
    g_mixed = None
    for f in range(n_f):
        at = slice(f * tile, (f + 1) * tile)
        gpre = (mm_nt(gexp, wback[at, :]) * slopes[f]).astype(BF16)
        part = mm_nt(gpre, win[:, at])
        g_mixed = part if g_mixed is None else g_mixed + part
    send_back(1, g_mixed)

    n_m = [[number() for _ in range(ny)] for _ in range(nx)]
    n_g = [[number() for _ in range(ny)] for _ in range(nx)]
    x_to = (1 - dx) * ny + dy

    def y_at(k, x):
        return x * ny + lax.rem(dy + k, ny)

    def y_from(k, x):
        return x * ny + lax.rem(dy + ny - k, ny)

    send(n_m[1][0], rows_all.at[d, 0], rows_all.at[d, 0], dp=x_to)
    for k in range(1, ny):
        send(n_g[0][k], rows_all.at[d, 1], rows_all.at[d, 1], dp=y_at(k, dx))
        send(n_m[0][k], rows_all.at[d, 0], rows_all.at[d, 0], dp=y_at(k, dx))
    send(n_g[1][0], rows_all.at[d, 1], rows_all.at[d, 1], dp=x_to)

    back_arrived(0)
    e_rows = back_recv[0].reshape(cols, width)
    out_send[...] = (resid[...] + mm(coef[...], e_rows)).astype(BF16).reshape(nc, BLOCK, width)
    n_out = [number() for _ in range(nc)]
    for k in range(1, nc):
        to = chip_at(k)
        send(n_out[k], out_send.at[to], tokens_out.at[c], grp=to * 2 + p)
    keep_out = local(out_send.at[c], tokens_out.at[c])
    dots = mm_nt(cot_rows, e_rows)
    back_arrived(1)
    g_rows = back_recv[1].reshape(cols, width)
    dots = dots + mm_nt(mix_in[...], g_rows)
    w256 = weights[...]
    inner = jnp.sum(w256 * dots, axis=0, keepdims=True)
    glogit = (w256 * (dots - inner)).astype(BF16)
    mixgrad[...] = mm(coef[...], g_rows) + mm_nt(glogit, wc[...])
    ctrl = mm_tn(glogit, mix_in[...]).reshape(ng, 2 * nc, width).sum(axis=1)

    def resid_rows(b, total):
        unit, inv_std = unit_norm(resid[block_rows(b), :])
        up = mixgrad[block_rows(b), :]
        grad = cot[b].astype(F32) + norm_back(up, unit, inv_std, gain_m)
        gresid[block_rows(b), :] = grad
        gbranch[p, b] = grad.astype(BF16)
        return total + jnp.sum(up * unit, axis=0, keepdims=True)

    gain_m_part = lax.fori_loop(0, nc, resid_rows, jnp.zeros((1, width), F32))
    n_branch = number()
    send(n_branch, gbranch.at[p], gbranch.at[p], grp=sib)

    def head_grads(par):
        raw = mm_nt(gbranch[par].reshape(own, width), wo[p])
        scaled = (raw * linv[:, par].reshape(own, half)).astype(BF16)
        prod = scaled.astype(F32) * attn[:, par].reshape(own, half).astype(F32)
        for pair in range(2):
            at = slice(pair * 128, pair * 128 + 128)
            for h in range(2):
                delta = jnp.sum(prod[:, at] * keep_f[h], axis=1, keepdims=True)
                high = delta.astype(BF16).astype(F32)
                low = delta - high
                first = HEAD_DIM * (1 - h)
                extra = jnp.where(lane == first, -high, jnp.where(lane == first + 1, -low, 0.0))
                gheads[pair * 2 + h, :, par] = (
                    scaled[:, at] * keep[h] + extra.astype(BF16)
                ).reshape(nc, BLOCK, 128)

    head_grads(p)
    arrived(n_branch, gbranch.at[oth])
    head_grads(oth)

    from_x = rows_all.at[x_to, 0]
    arrived(n_m[1][0], from_x)
    for k in range(1, ny):
        send(n_m[1][k], from_x, from_x, dp=y_at(k, dx))

    def second_hop():
        arrived(n_g[1][0], rows_all.at[x_to, 1])
        for k in range(1, ny):
            block = rows_all.at[y_from(k, dx), 1]
            arrived(n_g[0][k], block)
            send(n_g[1][k], block, block, dp=x_to)

    acc_k[...] = jnp.zeros_like(acc_k)
    acc_v[...] = jnp.zeros_like(acc_v)
    for i in range(n_q):
        if i == n_q - 1:
            second_hop()
        for pair in range(2):
            at = slice(pair * 128, pair * 128 + 128)
            q = rows_of(qs, i * per_q, per_q, pair)
            dqs = []
            for h in range(2):
                up = gheads[pair * 2 + h, i * per_q : (i + 1) * per_q].reshape(q_rows, 128)
                up_only = up * keep[h]
                q_only = q * keep[h]
                dq = None
                for n, (start, size) in enumerate(pieces(i)):
                    k_ = rows_of(ks, start // (2 * BLOCK), size // (2 * BLOCK), pair)
                    v_ = rows_of(vs, start // (2 * BLOCK), size // (2 * BLOCK), pair)
                    prob = held(pair * 2 + h, i, n)[...]
                    ds = prob * mm_nt(up, v_ * keep[h] + keep[1 - h]).astype(BF16)
                    term = mm(ds, k_)
                    dq = term if dq is None else dq + term
                    acc_k[start : start + size, at] += mm_tn(ds, q_only)
                    acc_v[start : start + size, at] += mm_tn(prob, up_only)
                dqs.append(dq)
            act_q[i * per_q : (i + 1) * per_q, :, :, at] = (
                (jnp.where(low_lane, dqs[0], dqs[1]) * HEAD_DIM**-0.5)
                .astype(BF16)
                .reshape(per_q, 2, BLOCK, 128)
            )
    act_k[...] = acc_k[...].astype(BF16).reshape(nc, 2, BLOCK, half)
    act_v[...] = acc_v[...].astype(BF16).reshape(nc, 2, BLOCK, half)

    def act_grad(par):
        return sum(
            mm_nt(act[:, par].reshape(own, half), w[...])
            for act, w in ((act_q, wq), (act_k, wk), (act_v, wv))
        )

    part_send[...] = act_grad(oth).astype(BF16).reshape(nc, BLOCK, width)
    n_part = number()
    send(n_part, part_send, part_recv, grp=sib)
    mixgrad[...] = act_grad(p)

    a = attn_in[...].reshape(length, width)
    out_part = sum(
        mm_tn(attn[:, par].reshape(own, half), gbranch[par].reshape(own, width)) for par in range(2)
    ).astype(BF16)
    n_red = 2
    firsts = (nz, ny)
    planes = (plane_a, plane_b)
    here_1, here_2 = (z, dy), (at_a, at_b)
    device_2 = (device_a, device_b)

    def device_1(r, to):
        return {"grp": (xh * nz + to) * 2 + p} if r == 0 else {"dp": dx * ny + to}

    for part, act in enumerate((act_q, act_k, act_v)):
        grad = mm_tn(a, act[...].reshape(length, half)).astype(BF16)
        for r in range(n_red):
            n1, sub = firsts[r], planes[r] // 4
            rows = half // n1
            for j in range(n1):
                pay[r, j, part * sub : (part + 1) * sub] = grad[
                    r * half + j * rows : r * half + (j + 1) * rows
                ].reshape(sub, rows // sub, half)
    for r in range(n_red):
        n1, sub = firsts[r], planes[r] // 4
        rows = half // n1
        for j in range(n1):
            pay[r, j, 3 * sub : 4 * sub] = out_part[
                j * rows : (j + 1) * rows, r * half : (r + 1) * half
            ].reshape(sub, rows // sub, half)
    n_rs1 = [[number() for _ in range(firsts[r])] for r in range(n_red)]
    for k in range(1, max(firsts)):
        for r in range(n_red):
            if k < firsts[r]:
                to = lax.rem(here_1[r] + k, firsts[r])
                send(n_rs1[r][k], pay.at[r, to], rs1.at[r, here_1[r]], **device_1(r, to))

    arrived(n_part, part_recv)

    def grad_rows(b, total):
        unit, inv_std = unit_norm(x_full[b, p].astype(F32))
        up = mixgrad[block_rows(b), :] + part_recv[b].astype(F32)
        grad = gresid[block_rows(b), :] + norm_back(up, unit, inv_std, gain_a)
        tgrad_send[b] = grad.astype(BF16)
        return total + jnp.sum(up * unit, axis=0, keepdims=True)

    gain_a_part = lax.fori_loop(0, nc, grad_rows, jnp.zeros((1, width), F32))
    n_tg = [number() for _ in range(nc)]
    for k in range(1, nc):
        to = chip_at(k)
        send(n_tg[k], tgrad_send.at[to], token_grad.at[c], grp=to * 2 + p)
    keep_tg = local(tgrad_send.at[c], token_grad.at[c])

    tiles = 8 // nc
    for j in range(8):
        r, l = j // 4, j % 4
        if ng >= 8 * (r + 1):
            small_pay[j // tiles, j % tiles] = ctrl[r * 8 : r * 8 + 8, l * 128 : l * 128 + 128]
        else:
            small_pay[j // tiles, j % tiles] = jnp.zeros((8, 128), F32)
            if ng > 8 * r:
                small_pay[j // tiles, j % tiles, : ng - 8 * r] = ctrl[r * 8 : ng, l * 128 : l * 128 + 128]
    for j in range(nc):
        for l in range(4):
            small_pay[j, tiles, l : l + 1] = gain_a_part[:, l * 128 : l * 128 + 128]
            small_pay[j, tiles, 4 + l : 5 + l] = gain_m_part[:, l * 128 : l * 128 + 128]
    n_s1 = [number() for _ in range(nc)]
    for k in range(1, nc):
        to = chip_at(k)
        send(n_s1[k], small_pay.at[to], small_rs1.at[c], grp=to * 2 + p)
    small_rs1[c] = small_pay[c]

    def hidden_rows(x):
        def body(f, carry):
            at = pl.ds(pl.multiple_of(f * tile, tile), tile)
            m_rows = rows_all[pl.ds(x * ny, ny), 0].reshape(ny * cols, width)
            g_rows = rows_all[pl.ds(x * ny, ny), 1].reshape(ny * cols, width)
            rows = pl.ds(pl.multiple_of(x * ny * cols, ny * cols), ny * cols)
            silu, slope = silu_and_slope(mm(m_rows, win[:, at]))
            hid[f, rows, :] = silu.astype(BF16)
            gpr[f, rows, :] = (mm_nt(g_rows, wback[at, :]) * slope).astype(BF16)
            return carry

        lax.fori_loop(0, n_f, body, 0)

    stores = []

    def weight_grads(f):
        slot = f % 2
        if f >= 2:
            for copy in stores[f - 2]:
                copy.wait()
        m_rows = rows_all[:, 0].reshape(ndp * cols, width)
        g_rows = rows_all[:, 1].reshape(ndp * cols, width)
        out_b[slot] = mm_tn(hid[f], g_rows).astype(BF16)
        out_i[slot] = mm_tn(m_rows, gpr[f]).astype(BF16)
        stores.append(
            (
                local(out_b.at[slot], grad_back.at[0, f * tile : (f + 1) * tile, :]),
                local(out_i.at[slot], grad_in.at[0, :, f * tile : (f + 1) * tile]),
            )
        )

    for k in range(1, ny):
        arrived(n_m[0][k], rows_all.at[y_from(k, dx), 0])
    hidden_rows(dx)

    n_rs2 = [[number() for _ in range(planes[r])] for r in range(n_red)]
    for r in range(n_red):
        for k in range(1, firsts[r]):
            arrived(n_rs1[r][k], rs1.at[r, lax.rem(here_1[r] + firsts[r] - k, firsts[r])])
        rs1[r, here_1[r]] = pay[r, here_1[r]]
        total = rs1[r, 0].astype(F32)
        for j in range(1, firsts[r]):
            total = total + rs1[r, j].astype(F32)
        red1[r] = total.astype(BF16)
        for k in range(1, planes[r]):
            to = lax.rem(here_2[r] + k, planes[r])
            send(n_rs2[r][k], red1.at[r, to], rs2.at[r, here_2[r]], **device_2[r](to))
        rs2[r, here_2[r]] = red1[r, here_2[r]]
    for k in range(1, nc):
        arrived(n_s1[k], small_rs1.at[chip_from(k)])
    small_sib[p] = small_rs1[...].sum(axis=0)
    n_ss = number()
    send(n_ss, small_sib.at[p], small_sib.at[p], grp=sib)

    for k in range(1, ny):
        arrived(n_g[1][k], rows_all.at[y_from(k, 1 - dx), 1])
        arrived(n_m[1][k], rows_all.at[y_from(k, 1 - dx), 0])
    hidden_rows(1 - dx)

    n_ag1 = [[number() for _ in range(planes[r])] for r in range(n_red)]
    for r in range(n_red):
        for k in range(1, planes[r]):
            arrived(n_rs2[r][k], rs2.at[r, lax.rem(here_2[r] + planes[r] - k, planes[r])])
        total = rs2[r, 0].astype(F32)
        for j in range(1, planes[r]):
            total = total + rs2[r, j].astype(F32)
        red2[r] = total.astype(BF16)
        for k in range(1, planes[r]):
            to = lax.rem(here_2[r] + k, planes[r])
            send(n_ag1[r][k], red2.at[r], ag1.at[r, here_2[r]], **device_2[r](to))
        ag1[r, here_2[r]] = red2[r]
    arrived(n_ss, small_sib.at[oth])
    small_dp[d] = small_sib[0] + small_sib[1]
    n_sd = [number() for _ in range(ndp)]
    for k in range(1, ndp):
        send(n_sd[k], small_dp.at[d], small_dp.at[d], dp=lax.rem(d + k, ndp))

    for f in range(n_f // 2):
        weight_grads(f)

    n_ag2 = [[number() for _ in range(firsts[r])] for r in range(n_red)]
    n_ag3 = [[number() for _ in range(firsts[r])] for r in range(n_red)]
    keep_red = []
    for r in range(n_red):
        for k in range(1, planes[r]):
            arrived(n_ag1[r][k], ag1.at[r, lax.rem(here_2[r] + planes[r] - k, planes[r])])
        place = reduced.at[p, r, here_1[r]]
        for k in range(1, firsts[r]):
            to = lax.rem(here_1[r] + k, firsts[r])
            send(n_ag2[r][k], ag1.at[r], place, **device_1(r, to))
        send(n_ag3[r][0], ag1.at[r], place, grp=sib)
        keep_red.append(local(ag1.at[r], place))
    for k in range(1, ndp):
        arrived(n_sd[k], small_dp.at[lax.rem(d + ndp - k, ndp)])
    small_fin[...] = small_dp[...].sum(axis=0)
    n_sg = [number() for _ in range(nc)]
    for k in range(1, nc):
        send(n_sg[k], small_fin, small_out.at[c], grp=chip_at(k) * 2 + p)
    keep_small = local(small_fin, small_out.at[c])

    for f in range(n_f // 2, n_f):
        weight_grads(f)

    for k in range(1, max(firsts)):
        for r in range(n_red):
            if k < firsts[r]:
                place = reduced.at[p, r, lax.rem(here_1[r] + firsts[r] - k, firsts[r])]
                arrived(n_ag2[r][k], place)
                send(n_ag3[r][k], place, place, grp=sib)
    for pair in stores[-2:]:
        for copy in pair:
            copy.wait()
    for k in range(1, nc):
        arrived(n_out[k], tokens_out.at[chip_from(k)])
        arrived(n_tg[k], token_grad.at[chip_from(k)])
        arrived(n_sg[k], small_out.at[chip_from(k)])
    for r in range(n_red):
        for k in range(firsts[r]):
            arrived(n_ag3[r][k], reduced.at[oth, r, lax.rem(here_1[r] + firsts[r] - k, firsts[r])])
    for copy in [keep_out, keep_tg, keep_small] + keep_red:
        copy.wait()
    for copy in started:
        copy.wait_send()


def finish_kernel(
    tokens_out, token_grad, reduced, small, grad_in, grad_back,
    out_tokens, out_tgrad, out_qkv, out_out, out_gain_a, out_gain_m, out_ctrl, out_in, out_back,
):
    tiles = small.shape[1] - 1
    width = out_out.shape[2] * 2
    half = width // 2
    out_tokens[...] = tokens_out[...]
    out_tgrad[...] = token_grad[...].astype(F32)
    out_in[...] = grad_in[...].astype(F32)
    out_back[...] = grad_back[...].astype(F32)
    rows = out_qkv.shape[0]
    sub = reduced.shape[3] // 4
    for p in range(2):
        for part in range(3):
            at = part * width + p * half
            out_qkv[:, at : at + half] = (
                reduced[p, 0, 0, part * sub : (part + 1) * sub].reshape(rows, half).astype(F32)
            )
        out_out[p] = reduced[p, 0, 0, 3 * sub : 4 * sub].reshape(rows, half).astype(F32)
    for l in range(4):
        at = slice(l * 128, l * 128 + 128)
        out_gain_a[:, at] = small[0, tiles, l : l + 1]
        out_gain_m[:, at] = small[0, tiles, 4 + l : 5 + l]
    for j in range(8):
        out_ctrl[j // 4 * 8 : j // 4 * 8 + 8, j % 4 * 128 : j % 4 * 128 + 128] = small[j // tiles, j % tiles]


def on_device(
    ng, ndp, nx,
    tokens, cotangent, w_qkv, w_out, gain_attn, gain_mix, w_ctrl, w_in, w_back, prefix, group_ids,
):
    nc = ng // 2
    width = tokens.shape[2]
    half = width // 2
    length, own = ng * BLOCK, nc * BLOCK
    ff = w_in.shape[2]
    cols = ng * 2 * nc
    n1, plane = nc // 2, 2 * nc
    tile = min(512, ff)
    tiles = 8 // nc
    vm = pltpu.VMEM
    anywhere = pl.BlockSpec(memory_space=pl.ANY)
    in_vmem = pl.BlockSpec(memory_space=pltpu.VMEM)
    in_smem = pl.BlockSpec(memory_space=pltpu.SMEM)
    scratch = [
        pltpu.SemaphoreType.DMA((SEMS,)),
        pltpu.SemaphoreType.DMA((SEMS,)),
        pltpu.SemaphoreType.DMA((32,)),
        vm((nc, 2, BLOCK, width), BF16),
        vm((nc, BLOCK, width), BF16),
        vm((nc, 8, 128), jnp.int32),
        vm((nc, 8, 128), jnp.int32),
        vm((width, half), BF16),
        vm((width, half), BF16),
        vm((width, half), BF16),
        vm((2, half, width), BF16),
        vm((width, ff), BF16),
        vm((ff, width), BF16),
        vm((nc, 2, BLOCK, width), BF16),
        vm((nc, 2, BLOCK, half), BF16),
        vm((nc, 2, BLOCK, half), BF16),
        vm((nc, 2, BLOCK, half), BF16),
        vm((length // 2, length // 2), F32),
        vm((nc, 2, BLOCK, half), F32),
        vm((nc, 2, BLOCK, half), BF16),
        vm((nc, BLOCK, half), BF16),
        vm((own, width), F32),
        vm((own, width), BF16),
        vm((width, cols), BF16),
        vm((own, cols), F32),
        vm((own, cols), BF16),
        vm((2, ng, 2 * nc, width), BF16),
        vm((ndp, 2, ng, 2 * nc, width), BF16),
        vm((2, ng, 2 * nc, width), BF16),
        vm((2, ng, 2 * nc, width), BF16),
        vm((nc, BLOCK, width), BF16),
        vm((own, width), F32),
        vm((own, width), F32),
        vm((2, nc, BLOCK, width), BF16),
        vm((4, nc, 2, BLOCK, 128), BF16),
        vm((length, half), F32),
        vm((length, half), F32),
        vm((nc, 2, BLOCK, half), BF16),
        vm((nc, 2, BLOCK, half), BF16),
        vm((nc, 2, BLOCK, half), BF16),
        vm((nc, BLOCK, width), BF16),
        vm((nc, BLOCK, width), BF16),
        vm((nc, BLOCK, width), BF16),
        vm((2, n1, plane, 16, half), BF16),
        vm((2, n1, plane, 16, half), BF16),
        vm((2, plane, 16, half), BF16),
        vm((2, plane, 16, half), BF16),
        vm((2, 16, half), BF16),
        vm((2, plane, 16, half), BF16),
        vm((nc, tiles + 1, 8, 128), F32),
        vm((nc, tiles + 1, 8, 128), F32),
        vm((2, tiles + 1, 8, 128), F32),
        vm((ndp, tiles + 1, 8, 128), F32),
        vm((tiles + 1, 8, 128), F32),
        vm((ff // tile, ndp * cols, tile), BF16),
        vm((ff // tile, ndp * cols, tile), BF16),
        vm((2, tile, width), BF16),
        vm((2, width, tile), BF16),
    ]
    tokens_out, token_grad, reduced, small, grad_in, grad_back = pl.pallas_call(
        functools.partial(block_kernel, ng, ndp, nx),
        out_shape=[
            jax.ShapeDtypeStruct(tokens.shape, BF16),
            jax.ShapeDtypeStruct(tokens.shape, BF16),
            jax.ShapeDtypeStruct((2, 2, n1, plane, 16, half), BF16),
            jax.ShapeDtypeStruct((nc, tiles + 1, 8, 128), F32),
            jax.ShapeDtypeStruct(w_in.shape, BF16),
            jax.ShapeDtypeStruct(w_back.shape, BF16),
        ],
        in_specs=[anywhere] * 4 + [in_vmem] * 3 + [anywhere] * 2 + [in_smem, in_vmem],
        out_specs=[anywhere] * 6,
        scratch_shapes=scratch,
        compiler_params=pltpu.CompilerParams(
            collective_id=0, has_side_effects=True, vmem_limit_bytes=60 * 1024 * 1024
        ),
        name="of_tokens_block",
    )(
        tokens, cotangent, w_qkv, w_out.reshape(2, half, width), gain_attn.reshape(1, width),
        gain_mix.reshape(1, width), w_ctrl.T, w_in, w_back, prefix, group_ids,
    )
    steps = 2 * n1

    def whole(shape):
        return pl.BlockSpec(shape, lambda s: (0,) * len(shape))

    def split(shape, axis):
        block = tuple(n // steps if i == axis else n for i, n in enumerate(shape))
        return pl.BlockSpec(block, lambda s: tuple(s if i == axis else 0 for i in range(len(shape))))

    shapes = [
        (tokens.shape, BF16), (tokens.shape, F32), ((width, 3 * width), F32), ((2, half, width), F32),
        ((1, width), F32), ((1, width), F32), ((16, width), F32), (w_in.shape, F32), (w_back.shape, F32),
    ]
    tokens_out, token_grad, grad_qkv, grad_out, gain_a, gain_m, ctrl, grad_in, grad_back = pl.pallas_call(
        finish_kernel,
        grid=(steps,),
        out_shape=[jax.ShapeDtypeStruct(*shape) for shape in shapes],
        in_specs=[
            split(tokens.shape, 0),
            split(tokens.shape, 0),
            pl.BlockSpec((2, 1, 1, plane, 16, half), lambda s: (0, s // n1, s % n1, 0, 0, 0)),
            whole(small.shape),
            split(w_in.shape, 1),
            split(w_back.shape, 1),
        ],
        out_specs=[
            split(tokens.shape, 0),
            split(tokens.shape, 0),
            split((width, 3 * width), 0),
            pl.BlockSpec((2, half // n1, half), lambda s: (0, s % n1, s // n1)),
            whole((1, width)),
            whole((1, width)),
            whole((16, width)),
            split(w_in.shape, 1),
            split(w_back.shape, 1),
        ],
        name="finish",
    )(tokens_out, token_grad, reduced, small, grad_in, grad_back)
    return (
        tokens_out,
        token_grad,
        grad_qkv,
        grad_out.reshape(width, width),
        gain_a.reshape(width),
        gain_m.reshape(width),
        ctrl[:ng].T,
        grad_in,
        grad_back,
    )


def solution(mesh):
    ng, ndp = mesh.shape["grp"], mesh.shape["dp"]
    in_specs = (
        P("dp", "grp", None),
        P("dp", "grp", None),
        P(),
        P(),
        P(),
        P(),
        P(),
        P("grp", None, None),
        P("grp", None, None),
        P("dp"),
        P("dp", "grp"),
    )
    out_specs = (
        P("dp", "grp", None),
        P("dp", "grp", None),
        P(),
        P(),
        P(),
        P(),
        P(),
        P("grp", None, None),
        P("grp", None, None),
    )
    return jax.shard_map(
        functools.partial(on_device, ng, ndp, 2),
        mesh=mesh, in_specs=in_specs, out_specs=out_specs, check_vma=False,
    )
```

```python
import functools

import jax
import jax.numpy as jnp
from jax import lax
from jax.experimental import pallas as pl
from jax.experimental.pallas import tpu as pltpu
from jax.sharding import PartitionSpec as P

HEADS = 8
HEAD_DIM = 64
GROUP = 32
BLOCK = 64
EPSILON = 1e-05
MASKED = -1e30
MESH = pl.DeviceIdType.MESH
F32 = jnp.float32
BF16 = jnp.bfloat16
SEMS = 288


def mm(a, b):
    return lax.dot_general(a, b, (((1,), (0,)), ((), ())), preferred_element_type=F32)


def mm_nt(a, b):
    return lax.dot_general(a, b, (((1,), (1,)), ((), ())), preferred_element_type=F32)


def mm_tn(a, b):
    return lax.dot_general(a, b, (((0,), (0,)), ((), ())), preferred_element_type=F32)


def unit_norm(x):
    centred = x - jnp.mean(x, axis=-1, keepdims=True)
    inv_std = lax.rsqrt(jnp.mean(centred * centred, axis=-1, keepdims=True) + EPSILON)
    return centred * inv_std, inv_std


def norm_back(up, unit, inv_std, gain):
    u = up * gain
    return inv_std * (
        u - jnp.mean(u, axis=-1, keepdims=True) - unit * jnp.mean(u * unit, axis=-1, keepdims=True)
    )


def block_kernel(
    ng, ndp, nx,
    tokens, cotangent, w_qkv, w_out, gain_attn, gain_mix, w_ctrl, w_in, w_back, prefix, group_ids,
    tokens_out, token_grad, reduced, small_out, grad_in, grad_back,
    send_sem, recv_sem, local_sem,
    x_full, cot, ids_send, ids_own, wq, wk, wv, wo, win, wback,
    attn_in, qs, ks, vs, bias, linv, attn, attn_other, resid, mix_in, wc, weights, coef,
    rows_send, rows_all, back_send, back_recv, out_send, mixgrad, gresid, gbranch, gheads,
    acc_k, acc_v, act_q, act_k, act_v, part_send, part_recv, tgrad_send, pay, rs1, red1, rs2, red2, ag1,
    small_pay, small_rs1, small_sib, small_dp, small_fin, hid, gpr, out_b, out_i,
):
    d, g = lax.axis_index("dp"), lax.axis_index("grp")
    nc, ny = ng // 2, ndp // nx
    c, p = g // 2, g % 2
    sib = g + 1 - 2 * p
    oth = 1 - p
    width = x_full.shape[3]
    half = width // 2
    length = ng * BLOCK
    own = nc * BLOCK
    ff = win.shape[1]
    q_rows = min(256, length // 2)
    n_q = length // q_rows
    per_q = q_rows // (2 * BLOCK)
    cols = ng * 2 * nc

    started, in_loop, used = [], [], [0, 0]

    def number():
        used[0] += 1
        return used[0] - 1

    def send(n, src, dst, like=None, **device):
        copy = pltpu.make_async_remote_copy(
            src_ref=src, dst_ref=dst, send_sem=send_sem.at[n], recv_sem=recv_sem.at[n],
            device_id=device, device_id_type=MESH,
        )
        copy.start()
        if like is None:
            started.append(copy)
        else:
            in_loop.append((n, like))

    def arrived(n, dst):
        pltpu.make_async_remote_copy(
            src_ref=dst, dst_ref=dst, send_sem=send_sem.at[n], recv_sem=recv_sem.at[n],
            device_id={"grp": sib}, device_id_type=MESH,
        ).wait_recv()

    def local(src, dst):
        copy = pltpu.make_async_copy(src, dst, local_sem.at[used[1]])
        used[1] += 1
        copy.start()
        return copy

    def chip_at(k):
        return lax.rem(c + k, nc)

    def chip_from(k):
        return lax.rem(c + nc - k, nc)

    load_tokens = local(tokens.at[c], x_full.at[c, p])
    loads_qkv = [
        local(w_qkv.at[:, pl.ds(pl.multiple_of(part * width + p * half, 128), half)], dst)
        for part, dst in enumerate((wq, wk, wv))
    ]
    load_out = local(w_out, wo)
    load_cot = local(cotangent.at[c], cot.at[c])
    load_in = local(w_in.at[0], win)
    load_back = local(w_back.at[0], wback)
    barrier = pltpu.get_barrier_semaphore()
    for k in range(1, ng):
        pl.semaphore_signal(barrier, inc=1, device_id={"grp": lax.rem(g + k, ng)}, device_id_type=MESH)
    for k in range(1, ndp):
        pl.semaphore_signal(barrier, inc=1, device_id={"dp": lax.rem(d + k, ndp)}, device_id_type=MESH)
    for b in range(nc):
        ids_send[b] = jnp.zeros((8, 128), jnp.int32)
        ids_send[b, :, 0:BLOCK] = jnp.broadcast_to(group_ids[b : b + 1, :], (8, BLOCK))
    nz = nc // 2
    dx, dy = d // ny, d % ny
    xh, z = c // nz, c % nz
    plane_a, plane_b = 2 * ndp, 2 * nc
    at_a, at_b = xh * ndp + d, dx * nc + c

    def device_a(a):
        return {"dp": a % ndp, "grp": (a // ndp * nz + z) * 2 + p}

    def device_b(b):
        return {"dp": b // nc * ny + dy, "grp": b % nc * 2 + p}

    for k in range(1, ndp):
        far = {"dp": lax.rem(d + k, ndp), "grp": ((1 - xh) * nz + z) * 2 + p}
        pl.semaphore_signal(barrier, inc=1, device_id=far, device_id_type=MESH)
    for k in range(1, nc):
        far = {"dp": (1 - dx) * ny + dy, "grp": chip_at(k) * 2 + p}
        pl.semaphore_signal(barrier, inc=1, device_id=far, device_id_type=MESH)
    pl.semaphore_wait(barrier, 2 * ndp + ng + nc - 4)

    n_tok = [number() for _ in range(nc)]
    n_fwd = [number() for _ in range(nc)]
    n_cot = [number() for _ in range(nc)]
    n_ids = [number() for _ in range(nc)]
    for k in range(1, nc):
        to = chip_at(k)
        send(n_tok[k], tokens.at[to], x_full.at[c, p], grp=to * 2 + p)
    for k in range(1, nc):
        to = chip_at(k)
        send(n_ids[k], ids_send.at[to], ids_own.at[c], grp=to * 2 + p)
    ids_own[c] = ids_send[c]
    load_tokens.wait()
    send(n_fwd[0], x_full.at[c, p], x_full.at[c, p], grp=sib)

    prefix_len = prefix[c]
    hl = length // 2

    def mask_rows(b, carry):
        row = lax.broadcasted_iota(jnp.int32, (BLOCK, hl), 0) + b * BLOCK
        col = lax.broadcasted_iota(jnp.int32, (BLOCK, hl), 1)
        bias[pl.ds(pl.multiple_of(b * BLOCK, BLOCK), BLOCK), :] = jnp.where(
            (col <= row) | (col < prefix_len), 0.0, MASKED
        )
        return carry

    lax.fori_loop(0, hl // BLOCK, mask_rows, 0)
    spread = (
        lax.broadcasted_iota(jnp.int32, (ng, cols), 1) // (2 * nc)
        == lax.broadcasted_iota(jnp.int32, (ng, cols), 0)
    ).astype(F32)
    wc[...] = mm_tn(w_ctrl[...].astype(F32), spread).astype(BF16)

    for k in range(1, nc):
        block = x_full.at[chip_from(k), p]
        arrived(n_tok[k], block)
        send(n_fwd[k], block, block, grp=sib)
    for k in range(1, nc):
        to = chip_at(k)
        send(n_cot[k], cotangent.at[to], cot.at[c], grp=to * 2 + p)
    for load in loads_qkv:
        load.wait()

    gain_a = gain_attn[...]
    gain_m = gain_mix[...]

    def project(par):
        def rows(b, carry):
            unit, _ = unit_norm(x_full[b, par].astype(F32))
            attn_in[b, par] = (unit * gain_a).astype(BF16)
            return carry

        lax.fori_loop(0, nc, rows, 0)
        a = attn_in[:, par].reshape(own, width)
        qs[:, par] = (mm(a, wq[...]).astype(BF16) * BF16(HEAD_DIM**-0.5)).reshape(nc, BLOCK, half)
        ks[:, par] = mm(a, wk[...]).astype(BF16).reshape(nc, BLOCK, half)
        vs[:, par] = mm(a, wv[...]).astype(BF16).reshape(nc, BLOCK, half)

    project(p)
    for k in range(nc):
        arrived(n_fwd[k], x_full.at[chip_from(k), oth])
    project(oth)

    lane = lax.broadcasted_iota(jnp.int32, (1, 128), 1)
    low_lane = lane < HEAD_DIM
    keep_f = [jnp.where(low_lane, 1.0, 0.0), jnp.where(low_lane, 0.0, 1.0)]
    keep = [m.astype(BF16) for m in keep_f]
    causal = jnp.where(
        lax.broadcasted_iota(jnp.int32, (q_rows, q_rows), 1)
        <= lax.broadcasted_iota(jnp.int32, (q_rows, q_rows), 0),
        0.0,
        MASKED,
    )

    def pieces(i):
        end = (i + 1) * q_rows
        return [(0, hl)] + ([(hl, end - hl)] if end > hl else [])

    def held(head, i, n):
        span = slice(n * length + i * q_rows, n * length + (i + 1) * q_rows)
        return hid.at[head, span, : pieces(i)[n][1]]

    def rows_of(ref, i, n, pair):
        return ref[i : i + n, :, :, pair * 128 : pair * 128 + 128].reshape(n * 2 * BLOCK, 128)

    n_mix = number()
    for i in range(n_q):
        for pair in range(2):
            q = rows_of(qs, i * per_q, per_q, pair)
            outs, invs = [], []
            for h in range(2):
                parts = []
                for start, size in pieces(i):
                    k_ = rows_of(ks, start // (2 * BLOCK), size // (2 * BLOCK), pair)
                    s = mm_nt(q * keep[h], k_)
                    if (i + 1) * q_rows <= hl:
                        s = s + bias[i * q_rows : (i + 1) * q_rows, :]
                    elif start == hl:
                        last = s[:, size - q_rows :] + causal
                        s = last if size == q_rows else jnp.concatenate([s[:, : size - q_rows], last], axis=1)
                    parts.append(s)
                top = functools.reduce(
                    jnp.maximum, [jnp.max(part, axis=-1, keepdims=True) for part in parts]
                )
                o = None
                for n, (start, size) in enumerate(pieces(i)):
                    low = jnp.exp(parts[n] - top).astype(BF16)
                    held(pair * 2 + h, i, n)[...] = low
                    v_ = rows_of(vs, start // (2 * BLOCK), size // (2 * BLOCK), pair)
                    term = mm(low, v_ * keep[h] + keep[1 - h])
                    o = term if o is None else o + term
                inv = 1.0 / pltpu.roll(o, HEAD_DIM, 1)
                outs.append(o * inv)
                invs.append(inv)
            shape = (per_q, 2, BLOCK, 128)
            at = slice(pair * 128, pair * 128 + 128)
            attn[i * per_q : (i + 1) * per_q, :, :, at] = (
                jnp.where(low_lane, outs[0], outs[1]).astype(BF16).reshape(shape)
            )
            linv[i * per_q : (i + 1) * per_q, :, :, at] = jnp.where(
                low_lane, invs[0], invs[1]
            ).reshape(shape)
    send(n_mix, attn.at[:, oth], attn_other, grp=sib)
    load_out.wait()
    for k in range(1, nc):
        arrived(n_cot[k], cot.at[chip_from(k)])
        arrived(n_ids[k], ids_own.at[chip_from(k)])
    load_cot.wait()
    mixed_own = mm(attn[:, p].reshape(own, half), wo[p])
    arrived(n_mix, attn_other)
    resid[...] = (
        x_full[:, p].reshape(own, width).astype(F32)
        + mixed_own
        + mm(attn_other[...].reshape(own, half), wo[oth])
    )

    def block_rows(b):
        return pl.ds(pl.multiple_of(b * BLOCK, BLOCK), BLOCK)

    def mix_rows(b, carry):
        unit, _ = unit_norm(resid[block_rows(b), :])
        mix_in[block_rows(b), :] = (unit * gain_m).astype(BF16)
        return carry

    lax.fori_loop(0, nc, mix_rows, 0)
    weights[...] = mm(mix_in[...], wc[...])
    place = lax.broadcasted_iota(jnp.int32, (1, cols), 1) % (2 * nc)
    diagonal = lax.broadcasted_iota(jnp.int32, (BLOCK, 128), 0) == lax.broadcasted_iota(
        jnp.int32, (BLOCK, 128), 1
    )

    def member_rows(b, carry):
        ids = jnp.broadcast_to(ids_own[b, 0:1, :].astype(F32), (BLOCK, 128))
        id_col = jnp.sum(jnp.where(diagonal, ids, 0.0), axis=1, keepdims=True)
        member = (place - 2 * b).astype(F32) == id_col
        weights[block_rows(b), :] = jnp.where(member, weights[block_rows(b), :], MASKED)
        return carry

    lax.fori_loop(0, nc, member_rows, 0)
    top = jnp.max(weights[...], axis=0, keepdims=True)
    exponent = jnp.exp(weights[...] - top)
    w256 = exponent / jnp.sum(exponent, axis=0, keepdims=True)
    weights[...] = w256
    coef[...] = w256.astype(BF16)
    cot_rows = cot[...].reshape(own, width)

    load_in.wait()
    load_back.wait()
    n_rows = [[number() for _ in range(ng)] for _ in range(2)]
    n_m = [[number() for _ in range(ny)] for _ in range(nx)]
    n_g = [[number() for _ in range(ny)] for _ in range(nx)]
    x_to = (1 - dx) * ny + dy

    def y_at(k, x):
        return x * ny + lax.rem(dy + k, ny)

    def y_from(k, x):
        return x * ny + lax.rem(dy + ny - k, ny)

    def send_rows(kind):
        for k in range(1, ng):
            to = lax.rem(g + k, ng)
            send(n_rows[kind][k], rows_send.at[kind, to], rows_all.at[d, kind, g], grp=to)
        rows_all[d, kind, g] = rows_send[kind, g]

    def rows_arrived(kind):
        for k in range(1, ng):
            arrived(n_rows[kind][k], rows_all.at[d, kind, lax.rem(g + ng - k, ng)])

    rows_send[0] = mm_tn(coef[...], mix_in[...]).astype(BF16).reshape(ng, 2 * nc, width)
    send_rows(0)
    rows_send[1] = mm_tn(coef[...], cot_rows).astype(BF16).reshape(ng, 2 * nc, width)
    send_rows(1)
    rows_arrived(0)

    tile = min(512, ff)
    n_f = ff // tile
    n_back = [[number() for _ in range(ng)] for _ in range(2)]

    def send_back(kind, rows):
        back_send[kind] = rows.astype(BF16).reshape(ng, 2 * nc, width)
        for k in range(1, ng):
            to = lax.rem(g + k, ng)
            send(n_back[kind][k], back_send.at[kind, to], back_recv.at[kind, g], grp=to)
        back_recv[kind, g] = back_send[kind, g]

    def back_arrived(kind):
        for k in range(1, ng):
            arrived(n_back[kind][k], back_recv.at[kind, lax.rem(g + ng - k, ng)])

    def silu_and_slope(pre):
        sig = 0.5 + 0.5 * jnp.tanh(0.5 * pre)
        silu = pre * sig
        return silu, sig + silu * (1.0 - sig)

    mixed = rows_all[d, 0].reshape(cols, width)
    e_out, slopes = None, []
    for f in range(n_f):
        at = slice(f * tile, (f + 1) * tile)
        silu, slope = silu_and_slope(mm(mixed, win[:, at]))
        slopes.append(slope)
        part = mm(silu.astype(BF16), wback[at, :])
        e_out = part if e_out is None else e_out + part
    send_back(0, e_out)

    rows_arrived(1)
    gexp = rows_all[d, 1].reshape(cols, width)
    g_mixed = None
    for f in range(n_f):
        at = slice(f * tile, (f + 1) * tile)
        gpre = (mm_nt(gexp, wback[at, :]) * slopes[f]).astype(BF16)
        part = mm_nt(gpre, win[:, at])
        g_mixed = part if g_mixed is None else g_mixed + part
    send_back(1, g_mixed)

    send(n_m[1][0], rows_all.at[d, 0], rows_all.at[d, 0], dp=x_to)
    for k in range(1, ny):
        send(n_g[0][k], rows_all.at[d, 1], rows_all.at[d, 1], dp=y_at(k, dx))
        send(n_m[0][k], rows_all.at[d, 0], rows_all.at[d, 0], dp=y_at(k, dx))
    send(n_g[1][0], rows_all.at[d, 1], rows_all.at[d, 1], dp=x_to)

    back_arrived(0)
    e_rows = back_recv[0].reshape(cols, width)
    out_send[...] = (resid[...] + mm(coef[...], e_rows)).astype(BF16).reshape(nc, BLOCK, width)
    n_out = [number() for _ in range(nc)]
    for k in range(1, nc):
        to = chip_at(k)
        send(n_out[k], out_send.at[to], tokens_out.at[c], grp=to * 2 + p)
    keep_out = local(out_send.at[c], tokens_out.at[c])
    dots = mm_nt(cot_rows, e_rows)
    back_arrived(1)
    g_rows = back_recv[1].reshape(cols, width)
    dots = dots + mm_nt(mix_in[...], g_rows)
    w256 = weights[...]
    inner = jnp.sum(w256 * dots, axis=0, keepdims=True)
    glogit = (w256 * (dots - inner)).astype(BF16)
    mixgrad[...] = mm(coef[...], g_rows) + mm_nt(glogit, wc[...])
    ctrl = mm_tn(glogit, mix_in[...]).reshape(ng, 2 * nc, width).sum(axis=1)

    def resid_rows(b, total):
        unit, inv_std = unit_norm(resid[block_rows(b), :])
        up = mixgrad[block_rows(b), :]
        grad = cot[b].astype(F32) + norm_back(up, unit, inv_std, gain_m)
        gresid[block_rows(b), :] = grad
        gbranch[p, b] = grad.astype(BF16)
        return total + jnp.sum(up * unit, axis=0, keepdims=True)

    gain_m_part = lax.fori_loop(0, nc, resid_rows, jnp.zeros((1, width), F32))
    n_branch = number()
    send(n_branch, gbranch.at[p], gbranch.at[p], grp=sib)

    tiles = 8 // nc
    for j in range(8):
        r, l = j // 4, j % 4
        if ng >= 8 * (r + 1):
            small_pay[j // tiles, j % tiles] = ctrl[r * 8 : r * 8 + 8, l * 128 : l * 128 + 128]
        else:
            small_pay[j // tiles, j % tiles] = jnp.zeros((8, 128), F32)
            if ng > 8 * r:
                small_pay[j // tiles, j % tiles, : ng - 8 * r] = ctrl[r * 8 : ng, l * 128 : l * 128 + 128]
    for j in range(nc):
        small_pay[j, tiles] = jnp.zeros((8, 128), F32)
        for l in range(4):
            small_pay[j, tiles, l : l + 1] = gain_m_part[:, l * 128 : l * 128 + 128]
    n_s1 = [number() for _ in range(nc)]
    for k in range(1, nc):
        to = chip_at(k)
        send(n_s1[k], small_pay.at[to], small_rs1.at[c], grp=to * 2 + p)
    small_rs1[c] = small_pay[c]
    n_ss = number()
    n_sd = [number() for _ in range(ndp)]
    n_sg = [number() for _ in range(nc)]

    def small_step(step):
        if step == 0:
            for k in range(1, nc):
                arrived(n_s1[k], small_rs1.at[chip_from(k)])
            small_sib[p] = small_rs1[...].sum(axis=0)
            send(n_ss, small_sib.at[p], small_sib.at[p], grp=sib)
        elif step == 1:
            arrived(n_ss, small_sib.at[oth])
            small_dp[d] = small_sib[0] + small_sib[1]
            for k in range(1, ndp):
                send(n_sd[k], small_dp.at[d], small_dp.at[d], like=lambda: small_dp.at[0], dp=lax.rem(d + k, ndp))
        else:
            for k in range(1, ndp):
                arrived(n_sd[k], small_dp.at[lax.rem(d + ndp - k, ndp)])
            small_fin[...] = small_dp[...].sum(axis=0)
            for k in range(1, nc):
                send(n_sg[k], small_fin, small_out.at[c], grp=chip_at(k) * 2 + p)

    def head_grads(par):
        raw = mm_nt(gbranch[par].reshape(own, width), wo[p])
        scaled = (raw * linv[:, par].reshape(own, half)).astype(BF16)
        prod = scaled.astype(F32) * attn[:, par].reshape(own, half).astype(F32)
        for pair in range(2):
            at = slice(pair * 128, pair * 128 + 128)
            for h in range(2):
                delta = jnp.sum(prod[:, at] * keep_f[h], axis=1, keepdims=True)
                high = delta.astype(BF16).astype(F32)
                low = delta - high
                first = HEAD_DIM * (1 - h)
                extra = jnp.where(lane == first, -high, jnp.where(lane == first + 1, -low, 0.0))
                gheads[pair * 2 + h, :, par] = (
                    scaled[:, at] * keep[h] + extra.astype(BF16)
                ).reshape(nc, BLOCK, 128)

    head_grads(p)
    arrived(n_branch, gbranch.at[oth])
    head_grads(oth)


    def second_hop(k):
        block = rows_all.at[y_from(k, dx), 1]
        arrived(n_g[0][k], block)
        send(n_g[1][k], block, block, dp=x_to)

    acc_k[...] = jnp.zeros_like(acc_k)
    acc_v[...] = jnp.zeros_like(acc_v)
    for i in range(n_q):
        if i == n_q - 2:
            from_x = rows_all.at[x_to, 0]
            arrived(n_m[1][0], from_x)
            for k in range(1, ny):
                send(n_m[1][k], from_x, from_x, dp=y_at(k, dx))
        if i == n_q - 1:
            for k in range(1, ny):
                second_hop(k)
        for pair in range(2):
            at = slice(pair * 128, pair * 128 + 128)
            q = rows_of(qs, i * per_q, per_q, pair)
            dqs = []
            for h in range(2):
                up = gheads[pair * 2 + h, i * per_q : (i + 1) * per_q].reshape(q_rows, 128)
                up_only = up * keep[h]
                q_only = q * keep[h]
                dq = None
                for n, (start, size) in enumerate(pieces(i)):
                    k_ = rows_of(ks, start // (2 * BLOCK), size // (2 * BLOCK), pair)
                    v_ = rows_of(vs, start // (2 * BLOCK), size // (2 * BLOCK), pair)
                    prob = held(pair * 2 + h, i, n)[...]
                    ds = prob * mm_nt(up, v_ * keep[h] + keep[1 - h]).astype(BF16)
                    term = mm(ds, k_)
                    dq = term if dq is None else dq + term
                    acc_k[start : start + size, at] += mm_tn(ds, q_only)
                    acc_v[start : start + size, at] += mm_tn(prob, up_only)
                dqs.append(dq)
            act_q[i * per_q : (i + 1) * per_q, :, :, at] = (
                (jnp.where(low_lane, dqs[0], dqs[1]) * HEAD_DIM**-0.5)
                .astype(BF16)
                .reshape(per_q, 2, BLOCK, 128)
            )
    act_k[...] = acc_k[...].astype(BF16).reshape(nc, 2, BLOCK, half)
    act_v[...] = acc_v[...].astype(BF16).reshape(nc, 2, BLOCK, half)

    def act_grad(par):
        return sum(
            mm_nt(act[:, par].reshape(own, half), w[...])
            for act, w in ((act_q, wq), (act_k, wk), (act_v, wv))
        )

    part_send[...] = act_grad(oth).astype(BF16).reshape(nc, BLOCK, width)
    n_part = number()
    send(n_part, part_send, part_recv, grp=sib)
    mixgrad[...] = act_grad(p)

    a = attn_in[...].reshape(length, width)
    out_part = sum(
        mm_tn(attn[:, par].reshape(own, half), gbranch[par].reshape(own, width)) for par in range(2)
    ).astype(BF16)
    n_red = 2
    firsts = (nz, ny)
    planes = (plane_a, plane_b)
    here_1, here_2 = (z, dy), (at_a, at_b)
    device_2 = (device_a, device_b)

    def device_1(r, to):
        return {"grp": (xh * nz + to) * 2 + p} if r == 0 else {"dp": dx * ny + to}

    for part, act in enumerate((act_q, act_k, act_v)):
        grad = mm_tn(a, act[...].reshape(length, half)).astype(BF16)
        for r in range(n_red):
            n1, sub = firsts[r], planes[r] // 4
            rows = half // n1
            for j in range(n1):
                pay[r, j, part * sub : (part + 1) * sub] = grad[
                    r * half + j * rows : r * half + (j + 1) * rows
                ].reshape(sub, rows // sub, half)
    for r in range(n_red):
        n1, sub = firsts[r], planes[r] // 4
        rows = half // n1
        for j in range(n1):
            pay[r, j, 3 * sub : 4 * sub] = out_part[
                j * rows : (j + 1) * rows, r * half : (r + 1) * half
            ].reshape(sub, rows // sub, half)
    n_rs1 = [[number() for _ in range(firsts[r])] for r in range(n_red)]
    for k in range(1, max(firsts)):
        for r in range(n_red):
            if k < firsts[r]:
                to = lax.rem(here_1[r] + k, firsts[r])
                send(n_rs1[r][k], pay.at[r, to], rs1.at[r, here_1[r]], **device_1(r, to))

    arrived(n_part, part_recv)

    def grad_rows(b, carry):
        unit, inv_std = unit_norm(x_full[b, p].astype(F32))
        up = mixgrad[block_rows(b), :] + part_recv[b].astype(F32)
        grad = gresid[block_rows(b), :] + norm_back(up, unit, inv_std, gain_a)
        tgrad_send[b] = grad.astype(BF16)
        return carry

    lax.fori_loop(0, nc, grad_rows, 0)
    n_tg = [number() for _ in range(nc)]
    for k in range(1, nc):
        to = chip_at(k)
        send(n_tg[k], tgrad_send.at[to], token_grad.at[c], grp=to * 2 + p)
    keep_tg = local(tgrad_send.at[c], token_grad.at[c])

    n_rs2 = [[number() for _ in range(planes[r])] for r in range(n_red)]
    n_ag1 = [[number() for _ in range(planes[r])] for r in range(n_red)]
    n_ag2 = [[number() for _ in range(firsts[r])] for r in range(n_red)]
    n_ag3 = [[number() for _ in range(firsts[r])] for r in range(n_red)]

    def reduce_first():
        for r in range(n_red):
            for k in range(1, firsts[r]):
                arrived(n_rs1[r][k], rs1.at[r, lax.rem(here_1[r] + firsts[r] - k, firsts[r])])
            rs1[r, here_1[r]] = pay[r, here_1[r]]
            total = rs1[r, 0].astype(F32)
            for j in range(1, firsts[r]):
                total = total + rs1[r, j].astype(F32)
            red1[r] = total.astype(BF16)
            for k in range(1, planes[r]):
                to = lax.rem(here_2[r] + k, planes[r])
                send(n_rs2[r][k], red1.at[r, to], rs2.at[r, here_2[r]], like=lambda r=r: red1.at[r, 0], **device_2[r](to))
            rs2[r, here_2[r]] = red1[r, here_2[r]]

    def reduce_second():
        for r in range(n_red):
            for k in range(1, planes[r]):
                arrived(n_rs2[r][k], rs2.at[r, lax.rem(here_2[r] + planes[r] - k, planes[r])])
            total = rs2[r, 0].astype(F32)
            for j in range(1, planes[r]):
                total = total + rs2[r, j].astype(F32)
            red2[r] = total.astype(BF16)
            for k in range(1, planes[r]):
                to = lax.rem(here_2[r] + k, planes[r])
                send(n_ag1[r][k], red2.at[r], ag1.at[r, here_2[r]], like=lambda r=r: red2.at[r], **device_2[r](to))
            ag1[r, here_2[r]] = red2[r]

    def gather_first():
        for r in range(n_red):
            for k in range(1, planes[r]):
                arrived(n_ag1[r][k], ag1.at[r, lax.rem(here_2[r] + planes[r] - k, planes[r])])
            place = reduced.at[p, r, here_1[r]]
            for k in range(1, firsts[r]):
                to = lax.rem(here_1[r] + k, firsts[r])
                send(n_ag2[r][k], ag1.at[r], place, like=lambda r=r: ag1.at[r], **device_1(r, to))
            send(n_ag3[r][0], ag1.at[r], place, like=lambda r=r: ag1.at[r], grp=sib)
            keep_red(r).start()

    red_sem = used[1]
    store_sem = used[1] + n_red
    used[1] += n_red + 2 * n_f

    def keep_red(r):
        return pltpu.make_async_copy(ag1.at[r], reduced.at[p, r, here_1[r]], local_sem.at[red_sem + r])

    def hidden_rows(t, carry):
        @pl.when(t == n_f)
        def _():
            small_step(1)
            reduce_first()
            for k in range(1, ny):
                arrived(n_g[1][k], rows_all.at[y_from(k, 1 - dx), 1])
                arrived(n_m[1][k], rows_all.at[y_from(k, 1 - dx), 0])
            arrived(n_g[1][0], rows_all.at[x_to, 1])

        @pl.when(t == n_f + n_f // 2)
        def _():
            reduce_second()

        x = lax.rem(dx + t // n_f, 2)
        f = lax.rem(t, n_f)
        at = pl.ds(pl.multiple_of(f * tile, tile), tile)
        m_rows = rows_all[pl.ds(x * ny, ny), 0].reshape(ny * cols, width)
        g_rows = rows_all[pl.ds(x * ny, ny), 1].reshape(ny * cols, width)
        rows = pl.ds(pl.multiple_of(x * ny * cols, ny * cols), ny * cols)
        silu, slope = silu_and_slope(mm(m_rows, win[:, at]))
        hid[f, rows, :] = silu.astype(BF16)
        gpr[f, rows, :] = (mm_nt(g_rows, wback[at, :]) * slope).astype(BF16)
        return carry

    def stores(f):
        slot = lax.rem(f, 2)
        at = pl.ds(pl.multiple_of(f * tile, tile), tile)
        return (
            pltpu.make_async_copy(out_b.at[slot], grad_back.at[0, at, :], local_sem.at[store_sem + 2 * f]),
            pltpu.make_async_copy(out_i.at[slot], grad_in.at[0, :, at], local_sem.at[store_sem + 2 * f + 1]),
        )

    def weight_grads(f, carry):
        @pl.when(f == 1)
        def _():
            gather_first()

        @pl.when(f >= 2)
        def _():
            for copy in stores(f - 2):
                copy.wait()

        slot = lax.rem(f, 2)
        m_rows = rows_all[:, 0].reshape(ndp * cols, width)
        g_rows = rows_all[:, 1].reshape(ndp * cols, width)
        out_b[slot] = mm_tn(hid[f], g_rows).astype(BF16)
        out_i[slot] = mm_tn(m_rows, gpr[f]).astype(BF16)
        for copy in stores(f):
            copy.start()
        return carry

    for k in range(1, ny):
        arrived(n_m[0][k], rows_all.at[y_from(k, dx), 0])
    small_step(0)
    lax.fori_loop(0, 2 * n_f, hidden_rows, 0)
    small_step(2)
    keep_small = local(small_fin, small_out.at[c])
    lax.fori_loop(0, n_f, weight_grads, 0)
    for k in range(1, max(firsts)):
        for r in range(n_red):
            if k < firsts[r]:
                place = reduced.at[p, r, lax.rem(here_1[r] + firsts[r] - k, firsts[r])]
                arrived(n_ag2[r][k], place)
                send(n_ag3[r][k], place, place, grp=sib)
    for f in (n_f - 2, n_f - 1):
        for copy in stores(f):
            copy.wait()
    for k in range(1, nc):
        arrived(n_out[k], tokens_out.at[chip_from(k)])
        arrived(n_tg[k], token_grad.at[chip_from(k)])
        arrived(n_sg[k], small_out.at[chip_from(k)])
    for r in range(n_red):
        for k in range(firsts[r]):
            arrived(n_ag3[r][k], reduced.at[oth, r, lax.rem(here_1[r] + firsts[r] - k, firsts[r])])
    for copy in [keep_out, keep_tg, keep_small] + [keep_red(r) for r in range(n_red)]:
        copy.wait()
    for copy in started:
        copy.wait_send()
    for n, like in in_loop:
        ref = like()
        pltpu.make_async_remote_copy(
            src_ref=ref, dst_ref=ref, send_sem=send_sem.at[n], recv_sem=recv_sem.at[n],
            device_id={"grp": sib}, device_id_type=MESH,
        ).wait_send()


def finish_kernel(
    tokens_out, token_grad, reduced, small, grad_in, grad_back, w_qkv, gain_attn,
    out_tokens, out_tgrad, out_qkv, out_out, out_gain_a, out_gain_m, out_ctrl, out_in, out_back,
    sums,
):
    step, steps = pl.program_id(0), pl.num_programs(0)
    tiles = small.shape[1] - 1
    width = out_out.shape[2] * 2
    half = width // 2
    out_tokens[...] = tokens_out[...]
    out_tgrad[...] = token_grad[...].astype(F32)
    out_in[...] = grad_in[...].astype(F32)
    out_back[...] = grad_back[...].astype(F32)
    rows = out_qkv.shape[0]
    sub = reduced.shape[3] // 4
    dots = jnp.zeros((rows, 1), F32)
    for p in range(2):
        for part in range(3):
            at = slice(part * width + p * half, part * width + p * half + half)
            grad = reduced[p, 0, 0, part * sub : (part + 1) * sub].reshape(rows, half).astype(F32)
            out_qkv[:, at] = grad
            dots = dots + jnp.sum(grad * w_qkv[:, at].astype(F32), axis=1, keepdims=True)
        out_out[p] = reduced[p, 0, 0, 3 * sub : 4 * sub].reshape(rows, half).astype(F32)
    sums[pl.ds(pl.multiple_of(step * rows, rows), rows), :] = jnp.broadcast_to(dots, (rows, 128))

    @pl.when(step == steps - 1)
    def _():
        out_gain_a[...] = sums[...].T[0:1] / gain_attn[...]

    for l in range(4):
        out_gain_m[:, l * 128 : l * 128 + 128] = small[0, tiles, l : l + 1]
    for j in range(8):
        out_ctrl[j // 4 * 8 : j // 4 * 8 + 8, j % 4 * 128 : j % 4 * 128 + 128] = small[j // tiles, j % tiles]


def on_device(
    ng, ndp, nx,
    tokens, cotangent, w_qkv, w_out, gain_attn, gain_mix, w_ctrl, w_in, w_back, prefix, group_ids,
):
    nc = ng // 2
    width = tokens.shape[2]
    half = width // 2
    length, own = ng * BLOCK, nc * BLOCK
    ff = w_in.shape[2]
    cols = ng * 2 * nc
    n1, plane = nc // 2, 2 * nc
    tile = min(512, ff)
    tiles = 8 // nc
    vm = pltpu.VMEM
    anywhere = pl.BlockSpec(memory_space=pl.ANY)
    in_vmem = pl.BlockSpec(memory_space=pltpu.VMEM)
    in_smem = pl.BlockSpec(memory_space=pltpu.SMEM)
    scratch = [
        pltpu.SemaphoreType.DMA((SEMS,)),
        pltpu.SemaphoreType.DMA((SEMS,)),
        pltpu.SemaphoreType.DMA((48,)),
        vm((nc, 2, BLOCK, width), BF16),
        vm((nc, BLOCK, width), BF16),
        vm((nc, 8, 128), jnp.int32),
        vm((nc, 8, 128), jnp.int32),
        vm((width, half), BF16),
        vm((width, half), BF16),
        vm((width, half), BF16),
        vm((2, half, width), BF16),
        vm((width, ff), BF16),
        vm((ff, width), BF16),
        vm((nc, 2, BLOCK, width), BF16),
        vm((nc, 2, BLOCK, half), BF16),
        vm((nc, 2, BLOCK, half), BF16),
        vm((nc, 2, BLOCK, half), BF16),
        vm((length // 2, length // 2), F32),
        vm((nc, 2, BLOCK, half), F32),
        vm((nc, 2, BLOCK, half), BF16),
        vm((nc, BLOCK, half), BF16),
        vm((own, width), F32),
        vm((own, width), BF16),
        vm((width, cols), BF16),
        vm((own, cols), F32),
        vm((own, cols), BF16),
        vm((2, ng, 2 * nc, width), BF16),
        vm((ndp, 2, ng, 2 * nc, width), BF16),
        vm((2, ng, 2 * nc, width), BF16),
        vm((2, ng, 2 * nc, width), BF16),
        vm((nc, BLOCK, width), BF16),
        vm((own, width), F32),
        vm((own, width), F32),
        vm((2, nc, BLOCK, width), BF16),
        vm((4, nc, 2, BLOCK, 128), BF16),
        vm((length, half), F32),
        vm((length, half), F32),
        vm((nc, 2, BLOCK, half), BF16),
        vm((nc, 2, BLOCK, half), BF16),
        vm((nc, 2, BLOCK, half), BF16),
        vm((nc, BLOCK, width), BF16),
        vm((nc, BLOCK, width), BF16),
        vm((nc, BLOCK, width), BF16),
        vm((2, n1, plane, 16, half), BF16),
        vm((2, n1, plane, 16, half), BF16),
        vm((2, plane, 16, half), BF16),
        vm((2, plane, 16, half), BF16),
        vm((2, 16, half), BF16),
        vm((2, plane, 16, half), BF16),
        vm((nc, tiles + 1, 8, 128), F32),
        vm((nc, tiles + 1, 8, 128), F32),
        vm((2, tiles + 1, 8, 128), F32),
        vm((ndp, tiles + 1, 8, 128), F32),
        vm((tiles + 1, 8, 128), F32),
        vm((ff // tile, ndp * cols, tile), BF16),
        vm((ff // tile, ndp * cols, tile), BF16),
        vm((2, tile, width), BF16),
        vm((2, width, tile), BF16),
    ]
    tokens_out, token_grad, reduced, small, grad_in, grad_back = pl.pallas_call(
        functools.partial(block_kernel, ng, ndp, nx),
        out_shape=[
            jax.ShapeDtypeStruct(tokens.shape, BF16),
            jax.ShapeDtypeStruct(tokens.shape, BF16),
            jax.ShapeDtypeStruct((2, 2, n1, plane, 16, half), BF16),
            jax.ShapeDtypeStruct((nc, tiles + 1, 8, 128), F32),
            jax.ShapeDtypeStruct(w_in.shape, BF16),
            jax.ShapeDtypeStruct(w_back.shape, BF16),
        ],
        in_specs=[anywhere] * 4 + [in_vmem] * 3 + [anywhere] * 2 + [in_smem, in_vmem],
        out_specs=[anywhere] * 6,
        scratch_shapes=scratch,
        compiler_params=pltpu.CompilerParams(
            collective_id=0, has_side_effects=True, vmem_limit_bytes=60 * 1024 * 1024
        ),
        name="of_tokens_block",
    )(
        tokens, cotangent, w_qkv, w_out.reshape(2, half, width), gain_attn.reshape(1, width),
        gain_mix.reshape(1, width), w_ctrl.T, w_in, w_back, prefix, group_ids,
    )
    steps = 2 * n1

    def whole(shape):
        return pl.BlockSpec(shape, lambda s: (0,) * len(shape))

    def split(shape, axis):
        block = tuple(n // steps if i == axis else n for i, n in enumerate(shape))
        return pl.BlockSpec(block, lambda s: tuple(s if i == axis else 0 for i in range(len(shape))))

    shapes = [
        (tokens.shape, BF16), (tokens.shape, F32), ((width, 3 * width), F32), ((2, half, width), F32),
        ((1, width), F32), ((1, width), F32), ((16, width), F32), (w_in.shape, F32), (w_back.shape, F32),
    ]
    tokens_out, token_grad, grad_qkv, grad_out, gain_a, gain_m, ctrl, grad_in, grad_back = pl.pallas_call(
        finish_kernel,
        grid=(steps,),
        out_shape=[jax.ShapeDtypeStruct(*shape) for shape in shapes],
        in_specs=[
            split(tokens.shape, 0),
            split(tokens.shape, 0),
            pl.BlockSpec((2, 1, 1, plane, 16, half), lambda s: (0, s // n1, s % n1, 0, 0, 0)),
            whole(small.shape),
            split(w_in.shape, 1),
            split(w_back.shape, 1),
            split((width, 3 * width), 0),
            whole((1, width)),
        ],
        out_specs=[
            split(tokens.shape, 0),
            split(tokens.shape, 0),
            split((width, 3 * width), 0),
            pl.BlockSpec((2, half // n1, half), lambda s: (0, s % n1, s // n1)),
            whole((1, width)),
            whole((1, width)),
            whole((16, width)),
            split(w_in.shape, 1),
            split(w_back.shape, 1),
        ],
        scratch_shapes=[vm((width, 128), F32)],
        name="finish",
    )(tokens_out, token_grad, reduced, small, grad_in, grad_back, w_qkv, gain_attn.reshape(1, width))
    return (
        tokens_out,
        token_grad,
        grad_qkv,
        grad_out.reshape(width, width),
        gain_a.reshape(width),
        gain_m.reshape(width),
        ctrl[:ng].T,
        grad_in,
        grad_back,
    )


def solution(mesh):
    ng, ndp = mesh.shape["grp"], mesh.shape["dp"]
    in_specs = (
        P("dp", "grp", None),
        P("dp", "grp", None),
        P(),
        P(),
        P(),
        P(),
        P(),
        P("grp", None, None),
        P("grp", None, None),
        P("dp"),
        P("dp", "grp"),
    )
    out_specs = (
        P("dp", "grp", None),
        P("dp", "grp", None),
        P(),
        P(),
        P(),
        P(),
        P(),
        P("grp", None, None),
        P("grp", None, None),
    )
    return jax.shard_map(
        functools.partial(on_device, ng, ndp, 2),
        mesh=mesh, in_specs=in_specs, out_specs=out_specs, check_vma=False,
    )
```

```python
import functools

import jax
import jax.numpy as jnp
from jax import lax
from jax.experimental import pallas as pl
from jax.experimental.pallas import tpu as pltpu
from jax.sharding import PartitionSpec as P

HEADS = 8
HEAD_DIM = 64
GROUP = 32
BLOCK = 64
EPSILON = 1e-05
MASKED = -1e30
MESH = pl.DeviceIdType.MESH
F32 = jnp.float32
BF16 = jnp.bfloat16
SEMS = 288


def mm(a, b):
    return lax.dot_general(a, b, (((1,), (0,)), ((), ())), preferred_element_type=F32)


def mm_nt(a, b):
    return lax.dot_general(a, b, (((1,), (1,)), ((), ())), preferred_element_type=F32)


def mm_tn(a, b):
    return lax.dot_general(a, b, (((0,), (0,)), ((), ())), preferred_element_type=F32)


def unit_norm(x):
    centred = x - jnp.mean(x, axis=-1, keepdims=True)
    inv_std = lax.rsqrt(jnp.mean(centred * centred, axis=-1, keepdims=True) + EPSILON)
    return centred * inv_std, inv_std


def norm_back(up, unit, inv_std, gain):
    u = up * gain
    return inv_std * (
        u - jnp.mean(u, axis=-1, keepdims=True) - unit * jnp.mean(u * unit, axis=-1, keepdims=True)
    )


def block_kernel(
    ng, ndp, nx,
    tokens, cotangent, w_qkv, w_out, gain_attn, gain_mix, w_ctrl, w_in, w_back, prefix, group_ids,
    tokens_out, token_grad, reduced, small_out, grad_in, grad_back,
    send_sem, recv_sem, local_sem,
    x_full, cot, ids_send, ids_own, wq, wk, wv, wo, win, wback,
    attn_in, qs, ks, vs, bias, linv, attn, attn_other, resid, mix_in, wc, weights, coef,
    rows_send, rows_all, back_send, back_recv, out_send, mixgrad, gresid, gbranch, gheads,
    acc_k, acc_v, act_q, act_k, act_v, part_send, part_recv, tgrad_send, pay, rs1, red1, rs2, red2, ag1,
    small_pay, small_rs1, small_sib, small_dp, small_fin, hid, gpr, out_b, out_i,
):
    d, g = lax.axis_index("dp"), lax.axis_index("grp")
    nc, ny = ng // 2, ndp // nx
    c, p = g // 2, g % 2
    sib = g + 1 - 2 * p
    oth = 1 - p
    width = x_full.shape[3]
    half = width // 2
    length = ng * BLOCK
    own = nc * BLOCK
    ff = win.shape[1]
    q_rows = min(256, length // 2)
    n_q = length // q_rows
    per_q = q_rows // (2 * BLOCK)
    cols = ng * 2 * nc

    started, in_loop, used = [], [], [0, 0]

    def number():
        used[0] += 1
        return used[0] - 1

    def send(n, src, dst, like=None, **device):
        copy = pltpu.make_async_remote_copy(
            src_ref=src, dst_ref=dst, send_sem=send_sem.at[n], recv_sem=recv_sem.at[n],
            device_id=device, device_id_type=MESH,
        )
        copy.start()
        if like is None:
            started.append(copy)
        else:
            in_loop.append((n, like))

    def arrived(n, dst):
        pltpu.make_async_remote_copy(
            src_ref=dst, dst_ref=dst, send_sem=send_sem.at[n], recv_sem=recv_sem.at[n],
            device_id={"grp": sib}, device_id_type=MESH,
        ).wait_recv()

    def local(src, dst):
        copy = pltpu.make_async_copy(src, dst, local_sem.at[used[1]])
        used[1] += 1
        copy.start()
        return copy

    def chip_at(k):
        return lax.rem(c + k, nc)

    def chip_from(k):
        return lax.rem(c + nc - k, nc)

    load_tokens = local(tokens.at[c], x_full.at[c, p])
    loads_qkv = [
        local(w_qkv.at[:, pl.ds(pl.multiple_of(part * width + p * half, 128), half)], dst)
        for part, dst in enumerate((wq, wk, wv))
    ]
    load_out = local(w_out, wo)
    load_cot = local(cotangent.at[c], cot.at[c])
    load_in = local(w_in.at[0], win)
    load_back = local(w_back.at[0], wback)
    barrier = pltpu.get_barrier_semaphore()
    for k in range(1, ng):
        pl.semaphore_signal(barrier, inc=1, device_id={"grp": lax.rem(g + k, ng)}, device_id_type=MESH)
    for k in range(1, ndp):
        pl.semaphore_signal(barrier, inc=1, device_id={"dp": lax.rem(d + k, ndp)}, device_id_type=MESH)
    for b in range(nc):
        ids_send[b] = jnp.zeros((8, 128), jnp.int32)
        ids_send[b, :, 0:BLOCK] = jnp.broadcast_to(group_ids[b : b + 1, :], (8, BLOCK))
    nz = nc // 2
    dx, dy = d // ny, d % ny
    xh, z = c // nz, c % nz
    plane_a, plane_b = 2 * ndp, 2 * nc
    at_a, at_b = xh * ndp + d, dx * nc + c

    def device_a(a):
        return {"dp": a % ndp, "grp": (a // ndp * nz + z) * 2 + p}

    def device_b(b):
        return {"dp": b // nc * ny + dy, "grp": b % nc * 2 + p}

    for k in range(1, ndp):
        far = {"dp": lax.rem(d + k, ndp), "grp": ((1 - xh) * nz + z) * 2 + p}
        pl.semaphore_signal(barrier, inc=1, device_id=far, device_id_type=MESH)
    for k in range(1, nc):
        far = {"dp": (1 - dx) * ny + dy, "grp": chip_at(k) * 2 + p}
        pl.semaphore_signal(barrier, inc=1, device_id=far, device_id_type=MESH)
    pl.semaphore_wait(barrier, 2 * ndp + ng + nc - 4)

    n_tok = [number() for _ in range(nc)]
    n_fwd = [number() for _ in range(nc)]
    n_cot = [number() for _ in range(nc)]
    n_ids = [number() for _ in range(nc)]
    for k in range(1, nc):
        to = chip_at(k)
        send(n_tok[k], tokens.at[to], x_full.at[c, p], grp=to * 2 + p)
    for k in range(1, nc):
        to = chip_at(k)
        send(n_ids[k], ids_send.at[to], ids_own.at[c], grp=to * 2 + p)
    ids_own[c] = ids_send[c]
    load_tokens.wait()
    send(n_fwd[0], x_full.at[c, p], x_full.at[c, p], grp=sib)

    prefix_len = prefix[c]
    hl = length // 2

    def mask_rows(b, carry):
        row = lax.broadcasted_iota(jnp.int32, (BLOCK, hl), 0) + b * BLOCK
        col = lax.broadcasted_iota(jnp.int32, (BLOCK, hl), 1)
        bias[pl.ds(pl.multiple_of(b * BLOCK, BLOCK), BLOCK), :] = jnp.where(
            (col <= row) | (col < prefix_len), 0.0, MASKED
        )
        return carry

    lax.fori_loop(0, hl // BLOCK, mask_rows, 0)
    spread = (
        lax.broadcasted_iota(jnp.int32, (ng, cols), 1) // (2 * nc)
        == lax.broadcasted_iota(jnp.int32, (ng, cols), 0)
    ).astype(F32)
    wc[...] = mm_tn(w_ctrl[...].astype(F32), spread).astype(BF16)

    for k in range(1, nc):
        block = x_full.at[chip_from(k), p]
        arrived(n_tok[k], block)
        send(n_fwd[k], block, block, grp=sib)
    for k in range(1, nc):
        to = chip_at(k)
        send(n_cot[k], cotangent.at[to], cot.at[c], grp=to * 2 + p)
    for load in loads_qkv:
        load.wait()

    gain_a = gain_attn[...]
    gain_m = gain_mix[...]

    def project(par):
        def rows(b, carry):
            unit, _ = unit_norm(x_full[b, par].astype(F32))
            attn_in[b, par] = (unit * gain_a).astype(BF16)
            return carry

        lax.fori_loop(0, nc, rows, 0)
        a = attn_in[:, par].reshape(own, width)
        qs[:, par] = (mm(a, wq[...]).astype(BF16) * BF16(HEAD_DIM**-0.5)).reshape(nc, BLOCK, half)
        ks[:, par] = mm(a, wk[...]).astype(BF16).reshape(nc, BLOCK, half)
        vs[:, par] = mm(a, wv[...]).astype(BF16).reshape(nc, BLOCK, half)

    project(p)
    for k in range(nc):
        arrived(n_fwd[k], x_full.at[chip_from(k), oth])
    project(oth)

    lane = lax.broadcasted_iota(jnp.int32, (1, 128), 1)
    low_lane = lane < HEAD_DIM
    keep_f = [jnp.where(low_lane, 1.0, 0.0), jnp.where(low_lane, 0.0, 1.0)]
    keep = [m.astype(BF16) for m in keep_f]
    causal = jnp.where(
        lax.broadcasted_iota(jnp.int32, (q_rows, q_rows), 1)
        <= lax.broadcasted_iota(jnp.int32, (q_rows, q_rows), 0),
        0.0,
        MASKED,
    )

    def pieces(i):
        end = (i + 1) * q_rows
        return [(0, hl)] + ([(hl, end - hl)] if end > hl else [])

    def held(head, i, n):
        span = slice(n * length + i * q_rows, n * length + (i + 1) * q_rows)
        return hid.at[head, span, : pieces(i)[n][1]]

    def rows_of(ref, i, n, pair):
        return ref[i : i + n, :, :, pair * 128 : pair * 128 + 128].reshape(n * 2 * BLOCK, 128)

    n_mix = number()
    for i in range(n_q):
        for pair in range(2):
            q = rows_of(qs, i * per_q, per_q, pair)
            outs, invs = [], []
            for h in range(2):
                parts = []
                for start, size in pieces(i):
                    k_ = rows_of(ks, start // (2 * BLOCK), size // (2 * BLOCK), pair)
                    s = mm_nt(q * keep[h], k_)
                    if (i + 1) * q_rows <= hl:
                        s = s + bias[i * q_rows : (i + 1) * q_rows, :]
                    elif start == hl:
                        last = s[:, size - q_rows :] + causal
                        s = last if size == q_rows else jnp.concatenate([s[:, : size - q_rows], last], axis=1)
                    parts.append(s)
                top = functools.reduce(
                    jnp.maximum, [jnp.max(part, axis=-1, keepdims=True) for part in parts]
                )
                o = None
                for n, (start, size) in enumerate(pieces(i)):
                    low = jnp.exp(parts[n] - top).astype(BF16)
                    held(pair * 2 + h, i, n)[...] = low
                    v_ = rows_of(vs, start // (2 * BLOCK), size // (2 * BLOCK), pair)
                    term = mm(low, v_ * keep[h] + keep[1 - h])
                    o = term if o is None else o + term
                inv = 1.0 / pltpu.roll(o, HEAD_DIM, 1)
                outs.append(o * inv)
                invs.append(inv)
            shape = (per_q, 2, BLOCK, 128)
            at = slice(pair * 128, pair * 128 + 128)
            attn[i * per_q : (i + 1) * per_q, :, :, at] = (
                jnp.where(low_lane, outs[0], outs[1]).astype(BF16).reshape(shape)
            )
            linv[i * per_q : (i + 1) * per_q, :, :, at] = jnp.where(
                low_lane, invs[0], invs[1]
            ).reshape(shape)
    send(n_mix, attn.at[:, oth], attn_other, grp=sib)
    load_out.wait()
    for k in range(1, nc):
        arrived(n_cot[k], cot.at[chip_from(k)])
        arrived(n_ids[k], ids_own.at[chip_from(k)])
    load_cot.wait()
    mixed_own = mm(attn[:, p].reshape(own, half), wo[p])
    arrived(n_mix, attn_other)
    resid[...] = (
        x_full[:, p].reshape(own, width).astype(F32)
        + mixed_own
        + mm(attn_other[...].reshape(own, half), wo[oth])
    )

    def block_rows(b):
        return pl.ds(pl.multiple_of(b * BLOCK, BLOCK), BLOCK)

    def mix_rows(b, carry):
        unit, _ = unit_norm(resid[block_rows(b), :])
        mix_in[block_rows(b), :] = (unit * gain_m).astype(BF16)
        return carry

    lax.fori_loop(0, nc, mix_rows, 0)
    weights[...] = mm(mix_in[...], wc[...])
    place = lax.broadcasted_iota(jnp.int32, (1, cols), 1) % (2 * nc)
    diagonal = lax.broadcasted_iota(jnp.int32, (BLOCK, 128), 0) == lax.broadcasted_iota(
        jnp.int32, (BLOCK, 128), 1
    )

    def member_rows(b, carry):
        ids = jnp.broadcast_to(ids_own[b, 0:1, :].astype(F32), (BLOCK, 128))
        id_col = jnp.sum(jnp.where(diagonal, ids, 0.0), axis=1, keepdims=True)
        member = (place - 2 * b).astype(F32) == id_col
        weights[block_rows(b), :] = jnp.where(member, weights[block_rows(b), :], MASKED)
        return carry

    lax.fori_loop(0, nc, member_rows, 0)
    top = jnp.max(weights[...], axis=0, keepdims=True)
    exponent = jnp.exp(weights[...] - top)
    w256 = exponent / jnp.sum(exponent, axis=0, keepdims=True)
    weights[...] = w256
    coef[...] = w256.astype(BF16)
    cot_rows = cot[...].reshape(own, width)

    load_in.wait()
    load_back.wait()
    n_rows = [[number() for _ in range(ng)] for _ in range(2)]
    n_m = [[number() for _ in range(ny)] for _ in range(nx)]
    n_g = [[number() for _ in range(ny)] for _ in range(nx)]
    x_to = (1 - dx) * ny + dy

    def y_at(k, x):
        return x * ny + lax.rem(dy + k, ny)

    def y_from(k, x):
        return x * ny + lax.rem(dy + ny - k, ny)

    def send_rows(kind):
        for k in range(1, ng):
            to = lax.rem(g + k, ng)
            send(n_rows[kind][k], rows_send.at[kind, to], rows_all.at[d, kind, g], grp=to)
        rows_all[d, kind, g] = rows_send[kind, g]

    def rows_arrived(kind):
        for k in range(1, ng):
            arrived(n_rows[kind][k], rows_all.at[d, kind, lax.rem(g + ng - k, ng)])

    rows_send[0] = mm_tn(coef[...], mix_in[...]).astype(BF16).reshape(ng, 2 * nc, width)
    send_rows(0)
    rows_send[1] = mm_tn(coef[...], cot_rows).astype(BF16).reshape(ng, 2 * nc, width)
    send_rows(1)
    rows_arrived(0)

    tile = min(512, ff)
    n_f = ff // tile
    n_back = [[number() for _ in range(ng)] for _ in range(2)]

    def send_back(kind, rows):
        back_send[kind] = rows.astype(BF16).reshape(ng, 2 * nc, width)
        for k in range(1, ng):
            to = lax.rem(g + k, ng)
            send(n_back[kind][k], back_send.at[kind, to], back_recv.at[kind, g], grp=to)
        back_recv[kind, g] = back_send[kind, g]

    def back_arrived(kind):
        for k in range(1, ng):
            arrived(n_back[kind][k], back_recv.at[kind, lax.rem(g + ng - k, ng)])

    def silu_and_slope(pre):
        sig = 0.5 + 0.5 * jnp.tanh(0.5 * pre)
        silu = pre * sig
        return silu, sig + silu * (1.0 - sig)

    mixed = rows_all[d, 0].reshape(cols, width)
    e_out, slopes = None, []
    for f in range(n_f):
        at = slice(f * tile, (f + 1) * tile)
        silu, slope = silu_and_slope(mm(mixed, win[:, at]))
        slopes.append(slope)
        part = mm(silu.astype(BF16), wback[at, :])
        e_out = part if e_out is None else e_out + part
    send_back(0, e_out)

    rows_arrived(1)
    gexp = rows_all[d, 1].reshape(cols, width)
    g_mixed = None
    for f in range(n_f):
        at = slice(f * tile, (f + 1) * tile)
        gpre = (mm_nt(gexp, wback[at, :]) * slopes[f]).astype(BF16)
        part = mm_nt(gpre, win[:, at])
        g_mixed = part if g_mixed is None else g_mixed + part
    send_back(1, g_mixed)

    send(n_m[1][0], rows_all.at[d, 0], rows_all.at[d, 0], dp=x_to)
    for k in range(1, ny):
        send(n_g[0][k], rows_all.at[d, 1], rows_all.at[d, 1], dp=y_at(k, dx))
        send(n_m[0][k], rows_all.at[d, 0], rows_all.at[d, 0], dp=y_at(k, dx))
    send(n_g[1][0], rows_all.at[d, 1], rows_all.at[d, 1], dp=x_to)

    back_arrived(0)
    e_rows = back_recv[0].reshape(cols, width)
    out_send[...] = (resid[...] + mm(coef[...], e_rows)).astype(BF16).reshape(nc, BLOCK, width)
    n_out = [number() for _ in range(nc)]
    for k in range(1, nc):
        to = chip_at(k)
        send(n_out[k], out_send.at[to], tokens_out.at[c], grp=to * 2 + p)
    keep_out = local(out_send.at[c], tokens_out.at[c])
    dots = mm_nt(cot_rows, e_rows)
    back_arrived(1)
    g_rows = back_recv[1].reshape(cols, width)
    dots = dots + mm_nt(mix_in[...], g_rows)
    w256 = weights[...]
    inner = jnp.sum(w256 * dots, axis=0, keepdims=True)
    glogit = (w256 * (dots - inner)).astype(BF16)
    mixgrad[...] = mm(coef[...], g_rows) + mm_nt(glogit, wc[...])
    ctrl = mm_tn(glogit, mix_in[...]).reshape(ng, 2 * nc, width).sum(axis=1)

    def resid_rows(b, total):
        unit, inv_std = unit_norm(resid[block_rows(b), :])
        up = mixgrad[block_rows(b), :]
        grad = cot[b].astype(F32) + norm_back(up, unit, inv_std, gain_m)
        gresid[block_rows(b), :] = grad
        gbranch[p, b] = grad.astype(BF16)
        return total + jnp.sum(up * unit, axis=0, keepdims=True)

    gain_m_part = lax.fori_loop(0, nc, resid_rows, jnp.zeros((1, width), F32))
    n_branch = number()
    send(n_branch, gbranch.at[p], gbranch.at[p], grp=sib)

    tiles = 8 // nc
    for j in range(8):
        r, l = j // 4, j % 4
        if ng >= 8 * (r + 1):
            small_pay[j // tiles, j % tiles] = ctrl[r * 8 : r * 8 + 8, l * 128 : l * 128 + 128]
        else:
            small_pay[j // tiles, j % tiles] = jnp.zeros((8, 128), F32)
            if ng > 8 * r:
                small_pay[j // tiles, j % tiles, : ng - 8 * r] = ctrl[r * 8 : ng, l * 128 : l * 128 + 128]
    for j in range(nc):
        small_pay[j, tiles] = jnp.zeros((8, 128), F32)
        for l in range(4):
            small_pay[j, tiles, l : l + 1] = gain_m_part[:, l * 128 : l * 128 + 128]
    n_s1 = [number() for _ in range(nc)]
    for k in range(1, nc):
        to = chip_at(k)
        send(n_s1[k], small_pay.at[to], small_rs1.at[c], grp=to * 2 + p)
    small_rs1[c] = small_pay[c]
    n_ss = number()
    n_sd = [number() for _ in range(ndp)]
    n_sg = [number() for _ in range(nc)]

    def small_step(step):
        if step == 0:
            for k in range(1, nc):
                arrived(n_s1[k], small_rs1.at[chip_from(k)])
            small_sib[p] = small_rs1[...].sum(axis=0)
            send(n_ss, small_sib.at[p], small_sib.at[p], grp=sib)
        elif step == 1:
            arrived(n_ss, small_sib.at[oth])
            small_dp[d] = small_sib[0] + small_sib[1]
            for k in range(1, ndp):
                send(n_sd[k], small_dp.at[d], small_dp.at[d], like=lambda: small_dp.at[0], dp=lax.rem(d + k, ndp))
        else:
            for k in range(1, ndp):
                arrived(n_sd[k], small_dp.at[lax.rem(d + ndp - k, ndp)])
            small_fin[...] = small_dp[...].sum(axis=0)
            for k in range(1, nc):
                send(n_sg[k], small_fin, small_out.at[c], grp=chip_at(k) * 2 + p)

    def head_grads(par):
        raw = mm_nt(gbranch[par].reshape(own, width), wo[p])
        scaled = (raw * linv[:, par].reshape(own, half)).astype(BF16)
        prod = scaled.astype(F32) * attn[:, par].reshape(own, half).astype(F32)
        for pair in range(2):
            at = slice(pair * 128, pair * 128 + 128)
            for h in range(2):
                delta = jnp.sum(prod[:, at] * keep_f[h], axis=1, keepdims=True)
                high = delta.astype(BF16).astype(F32)
                low = delta - high
                first = HEAD_DIM * (1 - h)
                extra = jnp.where(lane == first, -high, jnp.where(lane == first + 1, -low, 0.0))
                gheads[pair * 2 + h, :, par] = (
                    scaled[:, at] * keep[h] + extra.astype(BF16)
                ).reshape(nc, BLOCK, 128)

    head_grads(p)
    arrived(n_branch, gbranch.at[oth])
    head_grads(oth)


    def second_hop(k):
        block = rows_all.at[y_from(k, dx), 1]
        arrived(n_g[0][k], block)
        send(n_g[1][k], block, block, dp=x_to)

    acc_k[...] = jnp.zeros_like(acc_k)
    acc_v[...] = jnp.zeros_like(acc_v)
    for i in range(n_q):
        if i == n_q - 2:
            from_x = rows_all.at[x_to, 0]
            arrived(n_m[1][0], from_x)
            for k in range(1, ny):
                send(n_m[1][k], from_x, from_x, dp=y_at(k, dx))
        if i == n_q - 1:
            for k in range(1, ny):
                second_hop(k)
        for pair in range(2):
            at = slice(pair * 128, pair * 128 + 128)
            q = rows_of(qs, i * per_q, per_q, pair)
            dqs = []
            for h in range(2):
                up = gheads[pair * 2 + h, i * per_q : (i + 1) * per_q].reshape(q_rows, 128)
                up_only = up * keep[h]
                q_only = q * keep[h]
                dq = None
                for n, (start, size) in enumerate(pieces(i)):
                    k_ = rows_of(ks, start // (2 * BLOCK), size // (2 * BLOCK), pair)
                    v_ = rows_of(vs, start // (2 * BLOCK), size // (2 * BLOCK), pair)
                    prob = held(pair * 2 + h, i, n)[...]
                    ds = prob * mm_nt(up, v_ * keep[h] + keep[1 - h]).astype(BF16)
                    term = mm(ds, k_)
                    dq = term if dq is None else dq + term
                    acc_k[start : start + size, at] += mm_tn(ds, q_only)
                    acc_v[start : start + size, at] += mm_tn(prob, up_only)
                dqs.append(dq)
            act_q[i * per_q : (i + 1) * per_q, :, :, at] = (
                (jnp.where(low_lane, dqs[0], dqs[1]) * HEAD_DIM**-0.5)
                .astype(BF16)
                .reshape(per_q, 2, BLOCK, 128)
            )
    act_k[...] = acc_k[...].astype(BF16).reshape(nc, 2, BLOCK, half)
    act_v[...] = acc_v[...].astype(BF16).reshape(nc, 2, BLOCK, half)

    def act_grad(par):
        return sum(
            mm_nt(act[:, par].reshape(own, half), w[...])
            for act, w in ((act_q, wq), (act_k, wk), (act_v, wv))
        )

    part_send[...] = act_grad(oth).astype(BF16).reshape(nc, BLOCK, width)
    n_part = number()
    send(n_part, part_send, part_recv, grp=sib)
    mixgrad[...] = act_grad(p)

    a = attn_in[...].reshape(length, width)
    out_part = sum(
        mm_tn(attn[:, par].reshape(own, half), gbranch[par].reshape(own, width)) for par in range(2)
    ).astype(BF16)
    n_red = 2
    firsts = (nz, ny)
    planes = (plane_a, plane_b)
    here_1, here_2 = (z, dy), (at_a, at_b)
    device_2 = (device_a, device_b)

    def device_1(r, to):
        return {"grp": (xh * nz + to) * 2 + p} if r == 0 else {"dp": dx * ny + to}

    for part, act in enumerate((act_q, act_k, act_v)):
        grad = mm_tn(a, act[...].reshape(length, half)).astype(BF16)
        for r in range(n_red):
            n1, sub = firsts[r], planes[r] // 4
            rows = half // n1
            for j in range(n1):
                pay[r, j, part * sub : (part + 1) * sub] = grad[
                    r * half + j * rows : r * half + (j + 1) * rows
                ].reshape(sub, rows // sub, half)
    for r in range(n_red):
        n1, sub = firsts[r], planes[r] // 4
        rows = half // n1
        for j in range(n1):
            pay[r, j, 3 * sub : 4 * sub] = out_part[
                j * rows : (j + 1) * rows, r * half : (r + 1) * half
            ].reshape(sub, rows // sub, half)
    n_rs1 = [[number() for _ in range(firsts[r])] for r in range(n_red)]
    for k in range(1, max(firsts)):
        for r in range(n_red):
            if k < firsts[r]:
                to = lax.rem(here_1[r] + k, firsts[r])
                send(n_rs1[r][k], pay.at[r, to], rs1.at[r, here_1[r]], **device_1(r, to))

    arrived(n_part, part_recv)

    def grad_rows(b, carry):
        unit, inv_std = unit_norm(x_full[b, p].astype(F32))
        up = mixgrad[block_rows(b), :] + part_recv[b].astype(F32)
        grad = gresid[block_rows(b), :] + norm_back(up, unit, inv_std, gain_a)
        tgrad_send[b] = grad.astype(BF16)
        return carry

    lax.fori_loop(0, nc, grad_rows, 0)
    n_tg = [number() for _ in range(nc)]
    for k in range(1, nc):
        to = chip_at(k)
        send(n_tg[k], tgrad_send.at[to], token_grad.at[c], grp=to * 2 + p)
    keep_tg = local(tgrad_send.at[c], token_grad.at[c])

    n_rs2 = [[number() for _ in range(planes[r])] for r in range(n_red)]
    n_ag1 = [[number() for _ in range(planes[r])] for r in range(n_red)]
    n_ag2 = [[number() for _ in range(firsts[r])] for r in range(n_red)]
    n_ag3 = [[number() for _ in range(firsts[r])] for r in range(n_red)]

    def reduce_first():
        for r in range(n_red):
            for k in range(1, firsts[r]):
                arrived(n_rs1[r][k], rs1.at[r, lax.rem(here_1[r] + firsts[r] - k, firsts[r])])
            rs1[r, here_1[r]] = pay[r, here_1[r]]
            total = rs1[r, 0].astype(F32)
            for j in range(1, firsts[r]):
                total = total + rs1[r, j].astype(F32)
            red1[r] = total.astype(BF16)
            for k in range(1, planes[r]):
                to = lax.rem(here_2[r] + k, planes[r])
                send(n_rs2[r][k], red1.at[r, to], rs2.at[r, here_2[r]], like=lambda r=r: red1.at[r, 0], **device_2[r](to))
            rs2[r, here_2[r]] = red1[r, here_2[r]]

    def reduce_second():
        for r in range(n_red):
            for k in range(1, planes[r]):
                arrived(n_rs2[r][k], rs2.at[r, lax.rem(here_2[r] + planes[r] - k, planes[r])])
            total = rs2[r, 0].astype(F32)
            for j in range(1, planes[r]):
                total = total + rs2[r, j].astype(F32)
            red2[r] = total.astype(BF16)
            for k in range(1, planes[r]):
                to = lax.rem(here_2[r] + k, planes[r])
                send(n_ag1[r][k], red2.at[r], ag1.at[r, here_2[r]], like=lambda r=r: red2.at[r], **device_2[r](to))
            ag1[r, here_2[r]] = red2[r]

    def gather_first():
        for r in range(n_red):
            for k in range(1, planes[r]):
                arrived(n_ag1[r][k], ag1.at[r, lax.rem(here_2[r] + planes[r] - k, planes[r])])
            place = reduced.at[p, r, here_1[r]]
            for k in range(1, firsts[r]):
                to = lax.rem(here_1[r] + k, firsts[r])
                send(n_ag2[r][k], ag1.at[r], place, like=lambda r=r: ag1.at[r], **device_1(r, to))
            send(n_ag3[r][0], ag1.at[r], place, like=lambda r=r: ag1.at[r], grp=sib)
            keep_red(r).start()

    red_sem = used[1]
    store_sem = used[1] + n_red
    used[1] += n_red + 2 * n_f

    def keep_red(r):
        return pltpu.make_async_copy(ag1.at[r], reduced.at[p, r, here_1[r]], local_sem.at[red_sem + r])

    def hidden_rows(t, carry):
        @pl.when(t == n_f)
        def _():
            small_step(1)
            reduce_first()
            for k in range(1, ny):
                arrived(n_g[1][k], rows_all.at[y_from(k, 1 - dx), 1])
                arrived(n_m[1][k], rows_all.at[y_from(k, 1 - dx), 0])
            arrived(n_g[1][0], rows_all.at[x_to, 1])

        @pl.when(t == n_f + n_f // 2)
        def _():
            reduce_second()

        x = lax.rem(dx + t // n_f, 2)
        f = lax.rem(t, n_f)
        at = pl.ds(pl.multiple_of(f * tile, tile), tile)
        m_rows = rows_all[pl.ds(x * ny, ny), 0].reshape(ny * cols, width)
        g_rows = rows_all[pl.ds(x * ny, ny), 1].reshape(ny * cols, width)
        rows = pl.ds(pl.multiple_of(x * ny * cols, ny * cols), ny * cols)
        silu, slope = silu_and_slope(mm(m_rows, win[:, at]))
        hid[f, rows, :] = silu.astype(BF16)
        gpr[f, rows, :] = (mm_nt(g_rows, wback[at, :]) * slope).astype(BF16)
        return carry

    def stores(f):
        slot = lax.rem(f, 2)
        at = pl.ds(pl.multiple_of(f * tile, tile), tile)
        return (
            pltpu.make_async_copy(out_b.at[slot], grad_back.at[0, at, :], local_sem.at[store_sem + 2 * f]),
            pltpu.make_async_copy(out_i.at[slot], grad_in.at[0, :, at], local_sem.at[store_sem + 2 * f + 1]),
        )

    def weight_grads(f, carry):
        @pl.when(f == 1)
        def _():
            gather_first()

        @pl.when(f >= 2)
        def _():
            for copy in stores(f - 2):
                copy.wait()

        slot = lax.rem(f, 2)
        m_rows = rows_all[:, 0].reshape(ndp * cols, width)
        g_rows = rows_all[:, 1].reshape(ndp * cols, width)
        out_b[slot] = mm_tn(hid[f], g_rows).astype(BF16)
        out_i[slot] = mm_tn(m_rows, gpr[f]).astype(BF16)
        for copy in stores(f):
            copy.start()
        return carry

    for k in range(1, ny):
        arrived(n_m[0][k], rows_all.at[y_from(k, dx), 0])
    small_step(0)
    lax.fori_loop(0, 2 * n_f, hidden_rows, 0)
    small_step(2)
    keep_small = local(small_fin, small_out.at[c])
    lax.fori_loop(0, n_f, weight_grads, 0)
    for k in range(1, max(firsts)):
        for r in range(n_red):
            if k < firsts[r]:
                place = reduced.at[p, r, lax.rem(here_1[r] + firsts[r] - k, firsts[r])]
                arrived(n_ag2[r][k], place)
                send(n_ag3[r][k], place, place, grp=sib)
    for f in (n_f - 2, n_f - 1):
        for copy in stores(f):
            copy.wait()
    for k in range(1, nc):
        arrived(n_out[k], tokens_out.at[chip_from(k)])
        arrived(n_tg[k], token_grad.at[chip_from(k)])
        arrived(n_sg[k], small_out.at[chip_from(k)])
    for r in range(n_red):
        for k in range(firsts[r]):
            arrived(n_ag3[r][k], reduced.at[oth, r, lax.rem(here_1[r] + firsts[r] - k, firsts[r])])
    for copy in [keep_out, keep_tg, keep_small] + [keep_red(r) for r in range(n_red)]:
        copy.wait()
    for copy in started:
        copy.wait_send()
    for n, like in in_loop:
        ref = like()
        pltpu.make_async_remote_copy(
            src_ref=ref, dst_ref=ref, send_sem=send_sem.at[n], recv_sem=recv_sem.at[n],
            device_id={"grp": sib}, device_id_type=MESH,
        ).wait_send()


def finish_kernel(
    tokens_out, token_grad, reduced, small, grad_in, grad_back, w_qkv, gain_attn,
    out_tokens, out_tgrad, out_qkv, out_out, out_gain_a, out_gain_m, out_ctrl, out_in, out_back,
    sums,
):
    step, steps = pl.program_id(0), pl.num_programs(0)
    tiles = small.shape[1] - 1
    width = out_out.shape[2]
    half = width // 2
    out_tokens[...] = tokens_out[...]
    out_tgrad[...] = token_grad[...].astype(F32)
    out_in[...] = grad_in[...].astype(F32)
    out_back[...] = grad_back[...].astype(F32)
    chunks, sub = reduced.shape[2], reduced.shape[3] // 4
    rows = out_qkv.shape[1] // chunks
    for r in range(2):
        for j in range(chunks):
            here = slice(j * rows, (j + 1) * rows)
            dots = jnp.zeros((rows, half), F32)
            for p in range(2):
                for part in range(3):
                    at = slice(part * width + p * half, part * width + p * half + half)
                    grad = reduced[p, r, j, part * sub : (part + 1) * sub].reshape(rows, half).astype(F32)
                    out_qkv[r, here, at] = grad
                    dots = dots + grad * w_qkv[r, here, at].astype(F32)
                out_out[p, here, r * half : (r + 1) * half] = (
                    reduced[p, r, j, 3 * sub : 4 * sub].reshape(rows, half).astype(F32)
                )
            first = r * half + (step * chunks + j) * rows
            sums[pl.ds(pl.multiple_of(first, rows), rows), :] = jnp.broadcast_to(
                jnp.sum(dots, axis=1, keepdims=True), (rows, 128)
            )

    @pl.when(step == steps - 1)
    def _():
        out_gain_a[...] = sums[...].T[0:1] / gain_attn[...]

    for l in range(4):
        out_gain_m[:, l * 128 : l * 128 + 128] = small[0, tiles, l : l + 1]
    for j in range(8):
        out_ctrl[j // 4 * 8 : j // 4 * 8 + 8, j % 4 * 128 : j % 4 * 128 + 128] = small[j // tiles, j % tiles]


def on_device(
    ng, ndp, nx,
    tokens, cotangent, w_qkv, w_out, gain_attn, gain_mix, w_ctrl, w_in, w_back, prefix, group_ids,
):
    nc = ng // 2
    width = tokens.shape[2]
    half = width // 2
    length, own = ng * BLOCK, nc * BLOCK
    ff = w_in.shape[2]
    cols = ng * 2 * nc
    n1, plane = nc // 2, 2 * nc
    tile = min(512, ff)
    tiles = 8 // nc
    vm = pltpu.VMEM
    anywhere = pl.BlockSpec(memory_space=pl.ANY)
    in_vmem = pl.BlockSpec(memory_space=pltpu.VMEM)
    in_smem = pl.BlockSpec(memory_space=pltpu.SMEM)
    scratch = [
        pltpu.SemaphoreType.DMA((SEMS,)),
        pltpu.SemaphoreType.DMA((SEMS,)),
        pltpu.SemaphoreType.DMA((48,)),
        vm((nc, 2, BLOCK, width), BF16),
        vm((nc, BLOCK, width), BF16),
        vm((nc, 8, 128), jnp.int32),
        vm((nc, 8, 128), jnp.int32),
        vm((width, half), BF16),
        vm((width, half), BF16),
        vm((width, half), BF16),
        vm((2, half, width), BF16),
        vm((width, ff), BF16),
        vm((ff, width), BF16),
        vm((nc, 2, BLOCK, width), BF16),
        vm((nc, 2, BLOCK, half), BF16),
        vm((nc, 2, BLOCK, half), BF16),
        vm((nc, 2, BLOCK, half), BF16),
        vm((length // 2, length // 2), F32),
        vm((nc, 2, BLOCK, half), F32),
        vm((nc, 2, BLOCK, half), BF16),
        vm((nc, BLOCK, half), BF16),
        vm((own, width), F32),
        vm((own, width), BF16),
        vm((width, cols), BF16),
        vm((own, cols), F32),
        vm((own, cols), BF16),
        vm((2, ng, 2 * nc, width), BF16),
        vm((ndp, 2, ng, 2 * nc, width), BF16),
        vm((2, ng, 2 * nc, width), BF16),
        vm((2, ng, 2 * nc, width), BF16),
        vm((nc, BLOCK, width), BF16),
        vm((own, width), F32),
        vm((own, width), F32),
        vm((2, nc, BLOCK, width), BF16),
        vm((4, nc, 2, BLOCK, 128), BF16),
        vm((length, half), F32),
        vm((length, half), F32),
        vm((nc, 2, BLOCK, half), BF16),
        vm((nc, 2, BLOCK, half), BF16),
        vm((nc, 2, BLOCK, half), BF16),
        vm((nc, BLOCK, width), BF16),
        vm((nc, BLOCK, width), BF16),
        vm((nc, BLOCK, width), BF16),
        vm((2, n1, plane, 16, half), BF16),
        vm((2, n1, plane, 16, half), BF16),
        vm((2, plane, 16, half), BF16),
        vm((2, plane, 16, half), BF16),
        vm((2, 16, half), BF16),
        vm((2, plane, 16, half), BF16),
        vm((nc, tiles + 1, 8, 128), F32),
        vm((nc, tiles + 1, 8, 128), F32),
        vm((2, tiles + 1, 8, 128), F32),
        vm((ndp, tiles + 1, 8, 128), F32),
        vm((tiles + 1, 8, 128), F32),
        vm((ff // tile, ndp * cols, tile), BF16),
        vm((ff // tile, ndp * cols, tile), BF16),
        vm((2, tile, width), BF16),
        vm((2, width, tile), BF16),
    ]
    tokens_out, token_grad, reduced, small, grad_in, grad_back = pl.pallas_call(
        functools.partial(block_kernel, ng, ndp, nx),
        out_shape=[
            jax.ShapeDtypeStruct(tokens.shape, BF16),
            jax.ShapeDtypeStruct(tokens.shape, BF16),
            jax.ShapeDtypeStruct((2, 2, n1, plane, 16, half), BF16),
            jax.ShapeDtypeStruct((nc, tiles + 1, 8, 128), F32),
            jax.ShapeDtypeStruct(w_in.shape, BF16),
            jax.ShapeDtypeStruct(w_back.shape, BF16),
        ],
        in_specs=[anywhere] * 4 + [in_vmem] * 3 + [anywhere] * 2 + [in_smem, in_vmem],
        out_specs=[anywhere] * 6,
        scratch_shapes=scratch,
        compiler_params=pltpu.CompilerParams(
            collective_id=0, has_side_effects=True, vmem_limit_bytes=60 * 1024 * 1024
        ),
        name="of_tokens_block",
    )(
        tokens, cotangent, w_qkv, w_out.reshape(2, half, width), gain_attn.reshape(1, width),
        gain_mix.reshape(1, width), w_ctrl.T, w_in, w_back, prefix, group_ids,
    )
    steps = n1 // 2

    def whole(shape):
        return pl.BlockSpec(shape, lambda s: (0,) * len(shape))

    def split(shape, axis):
        block = tuple(n // steps if i == axis else n for i, n in enumerate(shape))
        return pl.BlockSpec(block, lambda s: tuple(s if i == axis else 0 for i in range(len(shape))))

    shapes = [
        (tokens.shape, BF16), (tokens.shape, F32), ((2, half, 3 * width), F32), ((2, half, width), F32),
        ((1, width), F32), ((1, width), F32), ((16, width), F32), (w_in.shape, F32), (w_back.shape, F32),
    ]
    tokens_out, token_grad, grad_qkv, grad_out, gain_a, gain_m, ctrl, grad_in, grad_back = pl.pallas_call(
        finish_kernel,
        grid=(steps,),
        out_shape=[jax.ShapeDtypeStruct(*shape) for shape in shapes],
        in_specs=[
            split(tokens.shape, 0),
            split(tokens.shape, 0),
            pl.BlockSpec((2, 2, n1 // steps, plane, 16, half), lambda s: (0, 0, s, 0, 0, 0)),
            whole(small.shape),
            split(w_in.shape, 1),
            split(w_back.shape, 1),
            split((2, half, 3 * width), 1),
            whole((1, width)),
        ],
        out_specs=[
            split(tokens.shape, 0),
            split(tokens.shape, 0),
            split((2, half, 3 * width), 1),
            split((2, half, width), 1),
            whole((1, width)),
            whole((1, width)),
            whole((16, width)),
            split(w_in.shape, 1),
            split(w_back.shape, 1),
        ],
        scratch_shapes=[vm((width, 128), F32)],
        compiler_params=pltpu.CompilerParams(vmem_limit_bytes=60 * 1024 * 1024),
        name="finish",
    )(
        tokens_out, token_grad, reduced, small, grad_in, grad_back,
        w_qkv.reshape(2, half, 3 * width), gain_attn.reshape(1, width),
    )
    return (
        tokens_out,
        token_grad,
        grad_qkv.reshape(width, 3 * width),
        grad_out.reshape(width, width),
        gain_a.reshape(width),
        gain_m.reshape(width),
        ctrl[:ng].T,
        grad_in,
        grad_back,
    )


def solution(mesh):
    ng, ndp = mesh.shape["grp"], mesh.shape["dp"]
    in_specs = (
        P("dp", "grp", None),
        P("dp", "grp", None),
        P(),
        P(),
        P(),
        P(),
        P(),
        P("grp", None, None),
        P("grp", None, None),
        P("dp"),
        P("dp", "grp"),
    )
    out_specs = (
        P("dp", "grp", None),
        P("dp", "grp", None),
        P(),
        P(),
        P(),
        P(),
        P(),
        P("grp", None, None),
        P("grp", None, None),
    )
    return jax.shard_map(
        functools.partial(on_device, ng, ndp, 2),
        mesh=mesh, in_specs=in_specs, out_specs=out_specs, check_vma=False,
    )
```

```python
import functools

import jax
import jax.numpy as jnp
from jax import lax
from jax.experimental import pallas as pl
from jax.experimental.pallas import tpu as pltpu
from jax.sharding import PartitionSpec as P

HEADS = 8
HEAD_DIM = 64
GROUP = 32
BLOCK = 64
EPSILON = 1e-05
MASKED = -1e30
MESH = pl.DeviceIdType.MESH
F32 = jnp.float32
BF16 = jnp.bfloat16
SEMS = 288


def mm(a, b):
    return lax.dot_general(a, b, (((1,), (0,)), ((), ())), preferred_element_type=F32)


def mm_nt(a, b):
    return lax.dot_general(a, b, (((1,), (1,)), ((), ())), preferred_element_type=F32)


def mm_tn(a, b):
    return lax.dot_general(a, b, (((0,), (0,)), ((), ())), preferred_element_type=F32)


def unit_norm(x):
    centred = x - jnp.mean(x, axis=-1, keepdims=True)
    inv_std = lax.rsqrt(jnp.mean(centred * centred, axis=-1, keepdims=True) + EPSILON)
    return centred * inv_std, inv_std


def norm_back(up, unit, inv_std, gain):
    u = up * gain
    return inv_std * (
        u - jnp.mean(u, axis=-1, keepdims=True) - unit * jnp.mean(u * unit, axis=-1, keepdims=True)
    )


def block_kernel(
    ng, ndp, nx,
    tokens, cotangent, w_qkv, w_out, gain_attn, gain_mix, w_ctrl, w_in, w_back, prefix, group_ids,
    tokens_out, token_grad, reduced, small_out, grad_in, grad_back,
    send_sem, recv_sem, local_sem,
    x_full, cot, ids_send, ids_own, wq, wk, wv, wo, win, wback,
    attn_in, qs, ks, vs, bias, linv, attn, attn_other, resid, mix_in, wc, weights, coef,
    rows_send, rows_all, back_send, back_recv, out_send, mixgrad, gresid, gbranch, gheads,
    acc_k, acc_v, act_q, act_k, act_v, part_send, part_recv, tgrad_send, pay, rs1, red1, rs2, red2, ag1,
    small_pay, small_rs1, small_sib, small_dp, small_fin, hid, gpr, out_b, out_i,
):
    d, g = lax.axis_index("dp"), lax.axis_index("grp")
    nc, ny = ng // 2, ndp // nx
    c, p = g // 2, g % 2
    sib = g + 1 - 2 * p
    oth = 1 - p
    width = x_full.shape[3]
    half = width // 2
    length = ng * BLOCK
    own = nc * BLOCK
    ff = win.shape[1]
    q_rows = min(256, length // 2)
    n_q = length // q_rows
    per_q = q_rows // (2 * BLOCK)
    cols = ng * 2 * nc

    started, in_loop, used = [], [], [0, 0]

    def number():
        used[0] += 1
        return used[0] - 1

    def send(n, src, dst, like=None, **device):
        copy = pltpu.make_async_remote_copy(
            src_ref=src, dst_ref=dst, send_sem=send_sem.at[n], recv_sem=recv_sem.at[n],
            device_id=device, device_id_type=MESH,
        )
        copy.start()
        if like is None:
            started.append(copy)
        else:
            in_loop.append((n, like))

    def arrived(n, dst):
        pltpu.make_async_remote_copy(
            src_ref=dst, dst_ref=dst, send_sem=send_sem.at[n], recv_sem=recv_sem.at[n],
            device_id={"grp": sib}, device_id_type=MESH,
        ).wait_recv()

    def local(src, dst):
        copy = pltpu.make_async_copy(src, dst, local_sem.at[used[1]])
        used[1] += 1
        copy.start()
        return copy

    def chip_at(k):
        return lax.rem(c + k, nc)

    def chip_from(k):
        return lax.rem(c + nc - k, nc)

    load_tokens = local(tokens.at[c], x_full.at[c, p])
    loads_qkv = [
        local(w_qkv.at[:, pl.ds(pl.multiple_of(part * width + p * half, 128), half)], dst)
        for part, dst in enumerate((wq, wk, wv))
    ]
    load_out = local(w_out, wo)
    load_cot = local(cotangent.at[c], cot.at[c])
    load_in = local(w_in.at[0], win)
    load_back = local(w_back.at[0], wback)
    barrier = pltpu.get_barrier_semaphore()
    for k in range(1, ng):
        pl.semaphore_signal(barrier, inc=1, device_id={"grp": lax.rem(g + k, ng)}, device_id_type=MESH)
    for k in range(1, ndp):
        pl.semaphore_signal(barrier, inc=1, device_id={"dp": lax.rem(d + k, ndp)}, device_id_type=MESH)
    for b in range(nc):
        ids_send[b] = jnp.zeros((8, 128), jnp.int32)
        ids_send[b, :, 0:BLOCK] = jnp.broadcast_to(group_ids[b : b + 1, :], (8, BLOCK))
    nz = nc // 2
    dx, dy = d // ny, d % ny
    xh, z = c // nz, c % nz
    plane_a, plane_b = 2 * ndp, 2 * nc
    at_a, at_b = xh * ndp + d, dx * nc + c

    def device_a(a):
        return {"dp": a % ndp, "grp": (a // ndp * nz + z) * 2 + p}

    def device_b(b):
        return {"dp": b // nc * ny + dy, "grp": b % nc * 2 + p}

    for k in range(1, ndp):
        far = {"dp": lax.rem(d + k, ndp), "grp": ((1 - xh) * nz + z) * 2 + p}
        pl.semaphore_signal(barrier, inc=1, device_id=far, device_id_type=MESH)
    for k in range(1, nc):
        far = {"dp": (1 - dx) * ny + dy, "grp": chip_at(k) * 2 + p}
        pl.semaphore_signal(barrier, inc=1, device_id=far, device_id_type=MESH)
    pl.semaphore_wait(barrier, 2 * ndp + ng + nc - 4)

    n_tok = [number() for _ in range(nc)]
    n_fwd = [number() for _ in range(nc)]
    n_cot = [number() for _ in range(nc)]
    n_ids = [number() for _ in range(nc)]
    for k in range(1, nc):
        to = chip_at(k)
        send(n_tok[k], tokens.at[to], x_full.at[c, p], grp=to * 2 + p)
    for k in range(1, nc):
        to = chip_at(k)
        send(n_ids[k], ids_send.at[to], ids_own.at[c], grp=to * 2 + p)
    ids_own[c] = ids_send[c]
    load_tokens.wait()
    send(n_fwd[0], x_full.at[c, p], x_full.at[c, p], grp=sib)

    prefix_len = prefix[c]
    hl = length // 2

    def mask_rows(b, carry):
        row = lax.broadcasted_iota(jnp.int32, (BLOCK, hl), 0) + b * BLOCK
        col = lax.broadcasted_iota(jnp.int32, (BLOCK, hl), 1)
        bias[pl.ds(pl.multiple_of(b * BLOCK, BLOCK), BLOCK), :] = jnp.where(
            (col <= row) | (col < prefix_len), 0.0, MASKED
        )
        return carry

    lax.fori_loop(0, hl // BLOCK, mask_rows, 0)
    spread = (
        lax.broadcasted_iota(jnp.int32, (ng, cols), 1) // (2 * nc)
        == lax.broadcasted_iota(jnp.int32, (ng, cols), 0)
    ).astype(F32)
    wc[...] = mm_tn(w_ctrl[...].astype(F32), spread).astype(BF16)

    for k in range(1, nc):
        block = x_full.at[chip_from(k), p]
        arrived(n_tok[k], block)
        send(n_fwd[k], block, block, grp=sib)
    for k in range(1, nc):
        to = chip_at(k)
        send(n_cot[k], cotangent.at[to], cot.at[c], grp=to * 2 + p)
    for load in loads_qkv:
        load.wait()

    gain_a = gain_attn[...]
    gain_m = gain_mix[...]

    def project(par):
        def rows(b, carry):
            unit, _ = unit_norm(x_full[b, par].astype(F32))
            attn_in[b, par] = (unit * gain_a).astype(BF16)
            return carry

        lax.fori_loop(0, nc, rows, 0)
        a = attn_in[:, par].reshape(own, width)
        qs[:, par] = (mm(a, wq[...]).astype(BF16) * BF16(HEAD_DIM**-0.5)).reshape(nc, BLOCK, half)
        ks[:, par] = mm(a, wk[...]).astype(BF16).reshape(nc, BLOCK, half)
        vs[:, par] = mm(a, wv[...]).astype(BF16).reshape(nc, BLOCK, half)

    project(p)
    for k in range(nc):
        arrived(n_fwd[k], x_full.at[chip_from(k), oth])
    project(oth)

    lane = lax.broadcasted_iota(jnp.int32, (1, 128), 1)
    low_lane = lane < HEAD_DIM
    keep_f = [jnp.where(low_lane, 1.0, 0.0), jnp.where(low_lane, 0.0, 1.0)]
    keep = [m.astype(BF16) for m in keep_f]
    causal = jnp.where(
        lax.broadcasted_iota(jnp.int32, (q_rows, q_rows), 1)
        <= lax.broadcasted_iota(jnp.int32, (q_rows, q_rows), 0),
        0.0,
        MASKED,
    )

    def pieces(i):
        end = (i + 1) * q_rows
        return [(0, hl)] + ([(hl, end - hl)] if end > hl else [])

    def held(head, i, n):
        span = slice(n * length + i * q_rows, n * length + (i + 1) * q_rows)
        return hid.at[head, span, : pieces(i)[n][1]]

    def rows_of(ref, i, n, pair):
        return ref[i : i + n, :, :, pair * 128 : pair * 128 + 128].reshape(n * 2 * BLOCK, 128)

    n_mix = number()
    for i in range(n_q):
        for pair in range(2):
            q = rows_of(qs, i * per_q, per_q, pair)
            outs, invs = [], []
            for h in range(2):
                parts = []
                for start, size in pieces(i):
                    k_ = rows_of(ks, start // (2 * BLOCK), size // (2 * BLOCK), pair)
                    s = mm_nt(q * keep[h], k_)
                    if (i + 1) * q_rows <= hl:
                        s = s + bias[i * q_rows : (i + 1) * q_rows, :]
                    elif start == hl:
                        last = s[:, size - q_rows :] + causal
                        s = last if size == q_rows else jnp.concatenate([s[:, : size - q_rows], last], axis=1)
                    parts.append(s)
                top = functools.reduce(
                    jnp.maximum, [jnp.max(part, axis=-1, keepdims=True) for part in parts]
                )
                o = None
                for n, (start, size) in enumerate(pieces(i)):
                    low = jnp.exp(parts[n] - top).astype(BF16)
                    held(pair * 2 + h, i, n)[...] = low
                    v_ = rows_of(vs, start // (2 * BLOCK), size // (2 * BLOCK), pair)
                    term = mm(low, v_ * keep[h] + keep[1 - h])
                    o = term if o is None else o + term
                inv = 1.0 / pltpu.roll(o, HEAD_DIM, 1)
                outs.append(o * inv)
                invs.append(inv)
            shape = (per_q, 2, BLOCK, 128)
            at = slice(pair * 128, pair * 128 + 128)
            attn[i * per_q : (i + 1) * per_q, :, :, at] = (
                jnp.where(low_lane, outs[0], outs[1]).astype(BF16).reshape(shape)
            )
            linv[i * per_q : (i + 1) * per_q, :, :, at] = jnp.where(
                low_lane, invs[0], invs[1]
            ).reshape(shape)
    send(n_mix, attn.at[:, oth], attn_other, grp=sib)
    load_out.wait()
    for k in range(1, nc):
        arrived(n_cot[k], cot.at[chip_from(k)])
        arrived(n_ids[k], ids_own.at[chip_from(k)])
    load_cot.wait()
    mixed_own = mm(attn[:, p].reshape(own, half), wo[p])
    arrived(n_mix, attn_other)
    resid[...] = (
        x_full[:, p].reshape(own, width).astype(F32)
        + mixed_own
        + mm(attn_other[...].reshape(own, half), wo[oth])
    )

    def block_rows(b):
        return pl.ds(pl.multiple_of(b * BLOCK, BLOCK), BLOCK)

    def mix_rows(b, carry):
        unit, _ = unit_norm(resid[block_rows(b), :])
        mix_in[block_rows(b), :] = (unit * gain_m).astype(BF16)
        return carry

    lax.fori_loop(0, nc, mix_rows, 0)
    weights[...] = mm(mix_in[...], wc[...])
    place = lax.broadcasted_iota(jnp.int32, (1, cols), 1) % (2 * nc)
    diagonal = lax.broadcasted_iota(jnp.int32, (BLOCK, 128), 0) == lax.broadcasted_iota(
        jnp.int32, (BLOCK, 128), 1
    )

    def member_rows(b, carry):
        ids = jnp.broadcast_to(ids_own[b, 0:1, :].astype(F32), (BLOCK, 128))
        id_col = jnp.sum(jnp.where(diagonal, ids, 0.0), axis=1, keepdims=True)
        member = (place - 2 * b).astype(F32) == id_col
        weights[block_rows(b), :] = jnp.where(member, weights[block_rows(b), :], MASKED)
        return carry

    lax.fori_loop(0, nc, member_rows, 0)
    top = jnp.max(weights[...], axis=0, keepdims=True)
    exponent = jnp.exp(weights[...] - top)
    w256 = exponent / jnp.sum(exponent, axis=0, keepdims=True)
    weights[...] = w256
    coef[...] = w256.astype(BF16)
    cot_rows = cot[...].reshape(own, width)

    load_in.wait()
    load_back.wait()
    n_rows = [[number() for _ in range(ng)] for _ in range(2)]
    n_m = [[number() for _ in range(ny)] for _ in range(nx)]
    n_g = [[number() for _ in range(ny)] for _ in range(nx)]
    x_to = (1 - dx) * ny + dy

    def y_at(k, x):
        return x * ny + lax.rem(dy + k, ny)

    def y_from(k, x):
        return x * ny + lax.rem(dy + ny - k, ny)

    def send_rows(kind):
        for k in range(1, ng):
            to = lax.rem(g + k, ng)
            send(n_rows[kind][k], rows_send.at[kind, to], rows_all.at[d, kind, g], grp=to)
        rows_all[d, kind, g] = rows_send[kind, g]

    def rows_arrived(kind):
        for k in range(1, ng):
            arrived(n_rows[kind][k], rows_all.at[d, kind, lax.rem(g + ng - k, ng)])

    rows_send[0] = mm_tn(coef[...], mix_in[...]).astype(BF16).reshape(ng, 2 * nc, width)
    send_rows(0)
    rows_send[1] = mm_tn(coef[...], cot_rows).astype(BF16).reshape(ng, 2 * nc, width)
    send_rows(1)
    rows_arrived(0)

    tile = min(512, ff)
    n_f = ff // tile
    n_back = [[number() for _ in range(ng)] for _ in range(2)]

    def send_back(kind, rows):
        back_send[kind] = rows.astype(BF16).reshape(ng, 2 * nc, width)
        for k in range(1, ng):
            to = lax.rem(g + k, ng)
            send(n_back[kind][k], back_send.at[kind, to], back_recv.at[kind, g], grp=to)
        back_recv[kind, g] = back_send[kind, g]

    def back_arrived(kind):
        for k in range(1, ng):
            arrived(n_back[kind][k], back_recv.at[kind, lax.rem(g + ng - k, ng)])

    def silu_and_slope(pre):
        sig = 0.5 + 0.5 * jnp.tanh(0.5 * pre)
        silu = pre * sig
        return silu, sig + silu * (1.0 - sig)

    mixed = rows_all[d, 0].reshape(cols, width)
    e_out, slopes = None, []
    for f in range(n_f):
        at = slice(f * tile, (f + 1) * tile)
        silu, slope = silu_and_slope(mm(mixed, win[:, at]))
        slopes.append(slope)
        part = mm(silu.astype(BF16), wback[at, :])
        e_out = part if e_out is None else e_out + part
    send_back(0, e_out)

    rows_arrived(1)
    gexp = rows_all[d, 1].reshape(cols, width)
    g_mixed = None
    for f in range(n_f):
        at = slice(f * tile, (f + 1) * tile)
        gpre = (mm_nt(gexp, wback[at, :]) * slopes[f]).astype(BF16)
        part = mm_nt(gpre, win[:, at])
        g_mixed = part if g_mixed is None else g_mixed + part
    send_back(1, g_mixed)

    send(n_m[1][0], rows_all.at[d, 0], rows_all.at[d, 0], dp=x_to)
    for k in range(1, ny):
        send(n_g[0][k], rows_all.at[d, 1], rows_all.at[d, 1], dp=y_at(k, dx))
        send(n_m[0][k], rows_all.at[d, 0], rows_all.at[d, 0], dp=y_at(k, dx))
    send(n_g[1][0], rows_all.at[d, 1], rows_all.at[d, 1], dp=x_to)

    back_arrived(0)
    e_rows = back_recv[0].reshape(cols, width)
    out_send[...] = (resid[...] + mm(coef[...], e_rows)).astype(BF16).reshape(nc, BLOCK, width)
    n_out = [number() for _ in range(nc)]
    for k in range(1, nc):
        to = chip_at(k)
        send(n_out[k], out_send.at[to], tokens_out.at[c], grp=to * 2 + p)
    keep_out = local(out_send.at[c], tokens_out.at[c])
    dots = mm_nt(cot_rows, e_rows)
    back_arrived(1)
    g_rows = back_recv[1].reshape(cols, width)
    dots = dots + mm_nt(mix_in[...], g_rows)
    w256 = weights[...]
    inner = jnp.sum(w256 * dots, axis=0, keepdims=True)
    glogit = (w256 * (dots - inner)).astype(BF16)
    mixgrad[...] = mm(coef[...], g_rows) + mm_nt(glogit, wc[...])
    ctrl = mm_tn(glogit, mix_in[...]).reshape(ng, 2 * nc, width).sum(axis=1)

    def resid_rows(b, total):
        unit, inv_std = unit_norm(resid[block_rows(b), :])
        up = mixgrad[block_rows(b), :]
        grad = cot[b].astype(F32) + norm_back(up, unit, inv_std, gain_m)
        gresid[block_rows(b), :] = grad
        gbranch[p, b] = grad.astype(BF16)
        return total + jnp.sum(up * unit, axis=0, keepdims=True)

    gain_m_part = lax.fori_loop(0, nc, resid_rows, jnp.zeros((1, width), F32))
    n_branch = number()
    send(n_branch, gbranch.at[p], gbranch.at[p], grp=sib)

    tiles = 8 // nc
    for j in range(8):
        r, l = j // 4, j % 4
        if ng >= 8 * (r + 1):
            small_pay[j // tiles, j % tiles] = ctrl[r * 8 : r * 8 + 8, l * 128 : l * 128 + 128]
        else:
            small_pay[j // tiles, j % tiles] = jnp.zeros((8, 128), F32)
            if ng > 8 * r:
                small_pay[j // tiles, j % tiles, : ng - 8 * r] = ctrl[r * 8 : ng, l * 128 : l * 128 + 128]
    for j in range(nc):
        small_pay[j, tiles] = jnp.zeros((8, 128), F32)
        for l in range(4):
            small_pay[j, tiles, l : l + 1] = gain_m_part[:, l * 128 : l * 128 + 128]
    n_s1 = [number() for _ in range(nc)]
    for k in range(1, nc):
        to = chip_at(k)
        send(n_s1[k], small_pay.at[to], small_rs1.at[c], grp=to * 2 + p)
    small_rs1[c] = small_pay[c]
    n_ss = number()
    n_sd = [number() for _ in range(ndp)]
    n_sg = [number() for _ in range(nc)]

    def small_step(step):
        if step == 0:
            for k in range(1, nc):
                arrived(n_s1[k], small_rs1.at[chip_from(k)])
            small_sib[p] = small_rs1[...].sum(axis=0)
            send(n_ss, small_sib.at[p], small_sib.at[p], grp=sib)
        elif step == 1:
            arrived(n_ss, small_sib.at[oth])
            small_dp[d] = small_sib[0] + small_sib[1]
            for k in range(1, ndp):
                send(n_sd[k], small_dp.at[d], small_dp.at[d], like=lambda: small_dp.at[0], dp=lax.rem(d + k, ndp))
        else:
            for k in range(1, ndp):
                arrived(n_sd[k], small_dp.at[lax.rem(d + ndp - k, ndp)])
            small_fin[...] = small_dp[...].sum(axis=0)
            for k in range(1, nc):
                send(n_sg[k], small_fin, small_out.at[c], grp=chip_at(k) * 2 + p)

    def head_grads(par):
        raw = mm_nt(gbranch[par].reshape(own, width), wo[p])
        scaled = (raw * linv[:, par].reshape(own, half)).astype(BF16)
        prod = scaled.astype(F32) * attn[:, par].reshape(own, half).astype(F32)
        for pair in range(2):
            at = slice(pair * 128, pair * 128 + 128)
            for h in range(2):
                delta = jnp.sum(prod[:, at] * keep_f[h], axis=1, keepdims=True)
                high = delta.astype(BF16).astype(F32)
                low = delta - high
                first = HEAD_DIM * (1 - h)
                extra = jnp.where(lane == first, -high, jnp.where(lane == first + 1, -low, 0.0))
                gheads[pair * 2 + h, :, par] = (
                    scaled[:, at] * keep[h] + extra.astype(BF16)
                ).reshape(nc, BLOCK, 128)

    head_grads(p)
    arrived(n_branch, gbranch.at[oth])
    head_grads(oth)


    def second_hop(k):
        block = rows_all.at[y_from(k, dx), 1]
        arrived(n_g[0][k], block)
        send(n_g[1][k], block, block, dp=x_to)

    acc_k[...] = jnp.zeros_like(acc_k)
    acc_v[...] = jnp.zeros_like(acc_v)
    for i in range(n_q):
        if i == n_q - 2:
            from_x = rows_all.at[x_to, 0]
            arrived(n_m[1][0], from_x)
            for k in range(1, ny):
                send(n_m[1][k], from_x, from_x, dp=y_at(k, dx))
        if i == n_q - 1:
            for k in range(1, ny):
                second_hop(k)
        for pair in range(2):
            at = slice(pair * 128, pair * 128 + 128)
            q = rows_of(qs, i * per_q, per_q, pair)
            dqs = []
            for h in range(2):
                up = gheads[pair * 2 + h, i * per_q : (i + 1) * per_q].reshape(q_rows, 128)
                up_only = up * keep[h]
                q_only = q * keep[h]
                dq = None
                for n, (start, size) in enumerate(pieces(i)):
                    k_ = rows_of(ks, start // (2 * BLOCK), size // (2 * BLOCK), pair)
                    v_ = rows_of(vs, start // (2 * BLOCK), size // (2 * BLOCK), pair)
                    prob = held(pair * 2 + h, i, n)[...]
                    ds = prob * mm_nt(up, v_ * keep[h] + keep[1 - h]).astype(BF16)
                    term = mm(ds, k_)
                    dq = term if dq is None else dq + term
                    acc_k[start : start + size, at] += mm_tn(ds, q_only)
                    acc_v[start : start + size, at] += mm_tn(prob, up_only)
                dqs.append(dq)
            act_q[i * per_q : (i + 1) * per_q, :, :, at] = (
                (jnp.where(low_lane, dqs[0], dqs[1]) * HEAD_DIM**-0.5)
                .astype(BF16)
                .reshape(per_q, 2, BLOCK, 128)
            )
    act_k[...] = acc_k[...].astype(BF16).reshape(nc, 2, BLOCK, half)
    act_v[...] = acc_v[...].astype(BF16).reshape(nc, 2, BLOCK, half)

    def act_grad(par):
        return sum(
            mm_nt(act[:, par].reshape(own, half), w[...])
            for act, w in ((act_q, wq), (act_k, wk), (act_v, wv))
        )

    part_send[...] = act_grad(oth).astype(BF16).reshape(nc, BLOCK, width)
    n_part = number()
    send(n_part, part_send, part_recv, grp=sib)
    mixgrad[...] = act_grad(p)

    a = attn_in[...].reshape(length, width)
    out_part = sum(
        mm_tn(attn[:, par].reshape(own, half), gbranch[par].reshape(own, width)) for par in range(2)
    ).astype(BF16)
    n_red = 2
    firsts = (nz, ny)
    planes = (plane_a, plane_b)
    here_1, here_2 = (z, dy), (at_a, at_b)
    device_2 = (device_a, device_b)

    def device_1(r, to):
        return {"grp": (xh * nz + to) * 2 + p} if r == 0 else {"dp": dx * ny + to}

    for part, act in enumerate((act_q, act_k, act_v)):
        grad = mm_tn(a, act[...].reshape(length, half)).astype(BF16)
        for r in range(n_red):
            n1, sub = firsts[r], planes[r] // 4
            rows = half // n1
            for j in range(n1):
                pay[r, j, part * sub : (part + 1) * sub] = grad[
                    r * half + j * rows : r * half + (j + 1) * rows
                ].reshape(sub, rows // sub, half)
    for r in range(n_red):
        n1, sub = firsts[r], planes[r] // 4
        rows = half // n1
        for j in range(n1):
            pay[r, j, 3 * sub : 4 * sub] = out_part[
                j * rows : (j + 1) * rows, r * half : (r + 1) * half
            ].reshape(sub, rows // sub, half)
    n_rs1 = [[number() for _ in range(firsts[r])] for r in range(n_red)]
    for k in range(1, max(firsts)):
        for r in range(n_red):
            if k < firsts[r]:
                to = lax.rem(here_1[r] + k, firsts[r])
                send(n_rs1[r][k], pay.at[r, to], rs1.at[r, here_1[r]], **device_1(r, to))

    arrived(n_part, part_recv)

    def grad_rows(b, carry):
        unit, inv_std = unit_norm(x_full[b, p].astype(F32))
        up = mixgrad[block_rows(b), :] + part_recv[b].astype(F32)
        grad = gresid[block_rows(b), :] + norm_back(up, unit, inv_std, gain_a)
        tgrad_send[b] = grad.astype(BF16)
        return carry

    lax.fori_loop(0, nc, grad_rows, 0)
    n_tg = [number() for _ in range(nc)]
    for k in range(1, nc):
        to = chip_at(k)
        send(n_tg[k], tgrad_send.at[to], token_grad.at[c], grp=to * 2 + p)
    keep_tg = local(tgrad_send.at[c], token_grad.at[c])

    n_rs2 = [[number() for _ in range(planes[r])] for r in range(n_red)]
    n_ag1 = [[number() for _ in range(planes[r])] for r in range(n_red)]
    n_ag2 = [[number() for _ in range(firsts[r])] for r in range(n_red)]
    n_ag3 = [[number() for _ in range(firsts[r])] for r in range(n_red)]

    def reduce_first():
        for r in range(n_red):
            for k in range(1, firsts[r]):
                arrived(n_rs1[r][k], rs1.at[r, lax.rem(here_1[r] + firsts[r] - k, firsts[r])])
            rs1[r, here_1[r]] = pay[r, here_1[r]]
            total = rs1[r, 0].astype(F32)
            for j in range(1, firsts[r]):
                total = total + rs1[r, j].astype(F32)
            red1[r] = total.astype(BF16)
            for k in range(1, planes[r]):
                to = lax.rem(here_2[r] + k, planes[r])
                send(n_rs2[r][k], red1.at[r, to], rs2.at[r, here_2[r]], like=lambda r=r: red1.at[r, 0], **device_2[r](to))
            rs2[r, here_2[r]] = red1[r, here_2[r]]

    def reduce_second():
        for r in range(n_red):
            for k in range(1, planes[r]):
                arrived(n_rs2[r][k], rs2.at[r, lax.rem(here_2[r] + planes[r] - k, planes[r])])
            total = rs2[r, 0].astype(F32)
            for j in range(1, planes[r]):
                total = total + rs2[r, j].astype(F32)
            red2[r] = total.astype(BF16)
            for k in range(1, planes[r]):
                to = lax.rem(here_2[r] + k, planes[r])
                send(n_ag1[r][k], red2.at[r], ag1.at[r, here_2[r]], like=lambda r=r: red2.at[r], **device_2[r](to))
            ag1[r, here_2[r]] = red2[r]

    def gather_first():
        for r in range(n_red):
            for k in range(1, planes[r]):
                arrived(n_ag1[r][k], ag1.at[r, lax.rem(here_2[r] + planes[r] - k, planes[r])])
            place = reduced.at[p, r, here_1[r]]
            for k in range(1, firsts[r]):
                to = lax.rem(here_1[r] + k, firsts[r])
                send(n_ag2[r][k], ag1.at[r], place, like=lambda r=r: ag1.at[r], **device_1(r, to))
            send(n_ag3[r][0], ag1.at[r], place, like=lambda r=r: ag1.at[r], grp=sib)
            keep_red(r).start()

    red_sem = used[1]
    store_sem = used[1] + n_red
    used[1] += n_red + 2 * n_f

    def keep_red(r):
        return pltpu.make_async_copy(ag1.at[r], reduced.at[p, r, here_1[r]], local_sem.at[red_sem + r])

    def hidden_rows(t, carry):
        @pl.when(t == n_f)
        def _():
            small_step(1)
            reduce_first()
            for k in range(1, ny):
                arrived(n_g[1][k], rows_all.at[y_from(k, 1 - dx), 1])
                arrived(n_m[1][k], rows_all.at[y_from(k, 1 - dx), 0])
            arrived(n_g[1][0], rows_all.at[x_to, 1])

        @pl.when(t == n_f + n_f // 2 + 1)
        def _():
            reduce_second()

        x = lax.rem(dx + t // n_f, 2)
        f = lax.rem(t, n_f)
        at = pl.ds(pl.multiple_of(f * tile, tile), tile)
        m_rows = rows_all[pl.ds(x * ny, ny), 0].reshape(ny * cols, width)
        g_rows = rows_all[pl.ds(x * ny, ny), 1].reshape(ny * cols, width)
        rows = pl.ds(pl.multiple_of(x * ny * cols, ny * cols), ny * cols)
        silu, slope = silu_and_slope(mm(m_rows, win[:, at]))
        hid[f, rows, :] = silu.astype(BF16)
        gpr[f, rows, :] = (mm_nt(g_rows, wback[at, :]) * slope).astype(BF16)
        return carry

    def stores(f):
        slot = lax.rem(f, 2)
        at = pl.ds(pl.multiple_of(f * tile, tile), tile)
        return (
            pltpu.make_async_copy(out_b.at[slot], grad_back.at[0, at, :], local_sem.at[store_sem + 2 * f]),
            pltpu.make_async_copy(out_i.at[slot], grad_in.at[0, :, at], local_sem.at[store_sem + 2 * f + 1]),
        )

    def weight_grads(f, carry):
        @pl.when(f == 1)
        def _():
            gather_first()

        @pl.when(f >= 2)
        def _():
            for copy in stores(f - 2):
                copy.wait()

        slot = lax.rem(f, 2)
        m_rows = rows_all[:, 0].reshape(ndp * cols, width)
        g_rows = rows_all[:, 1].reshape(ndp * cols, width)
        out_b[slot] = mm_tn(hid[f], g_rows).astype(BF16)
        out_i[slot] = mm_tn(m_rows, gpr[f]).astype(BF16)
        for copy in stores(f):
            copy.start()
        return carry

    for k in range(1, ny):
        arrived(n_m[0][k], rows_all.at[y_from(k, dx), 0])
    small_step(0)
    lax.fori_loop(0, 2 * n_f, hidden_rows, 0)
    small_step(2)
    keep_small = local(small_fin, small_out.at[c])
    lax.fori_loop(0, n_f, weight_grads, 0)
    for k in range(1, max(firsts)):
        for r in range(n_red):
            if k < firsts[r]:
                place = reduced.at[p, r, lax.rem(here_1[r] + firsts[r] - k, firsts[r])]
                arrived(n_ag2[r][k], place)
                send(n_ag3[r][k], place, place, grp=sib)
    for f in (n_f - 2, n_f - 1):
        for copy in stores(f):
            copy.wait()
    for k in range(1, nc):
        arrived(n_out[k], tokens_out.at[chip_from(k)])
        arrived(n_tg[k], token_grad.at[chip_from(k)])
        arrived(n_sg[k], small_out.at[chip_from(k)])
    for r in range(n_red):
        for k in range(firsts[r]):
            arrived(n_ag3[r][k], reduced.at[oth, r, lax.rem(here_1[r] + firsts[r] - k, firsts[r])])
    for copy in [keep_out, keep_tg, keep_small] + [keep_red(r) for r in range(n_red)]:
        copy.wait()
    for copy in started:
        copy.wait_send()
    for n, like in in_loop:
        ref = like()
        pltpu.make_async_remote_copy(
            src_ref=ref, dst_ref=ref, send_sem=send_sem.at[n], recv_sem=recv_sem.at[n],
            device_id={"grp": sib}, device_id_type=MESH,
        ).wait_send()


def finish_kernel(
    tokens_out, token_grad, reduced, small, grad_in, grad_back, w_qkv, gain_attn,
    out_tokens, out_tgrad, out_qkv, out_out, out_gain_a, out_gain_m, out_ctrl, out_in, out_back,
    sums,
):
    step, steps = pl.program_id(0), pl.num_programs(0)
    tiles = small.shape[1] - 1
    width = out_out.shape[2]
    half = width // 2
    out_tokens[...] = tokens_out[...]
    out_tgrad[...] = token_grad[...].astype(F32)
    out_in[...] = grad_in[...].astype(F32)
    out_back[...] = grad_back[...].astype(F32)
    chunks, sub = reduced.shape[2], reduced.shape[3] // 4
    rows = out_qkv.shape[1] // chunks
    for r in range(2):
        for j in range(chunks):
            here = slice(j * rows, (j + 1) * rows)
            dots = jnp.zeros((rows, half), F32)
            for p in range(2):
                for part in range(3):
                    at = slice(part * width + p * half, part * width + p * half + half)
                    grad = reduced[p, r, j, part * sub : (part + 1) * sub].reshape(rows, half).astype(F32)
                    out_qkv[r, here, at] = grad
                    dots = dots + grad * w_qkv[r, here, at].astype(F32)
                out_out[p, here, r * half : (r + 1) * half] = (
                    reduced[p, r, j, 3 * sub : 4 * sub].reshape(rows, half).astype(F32)
                )
            first = r * half + (step * chunks + j) * rows
            sums[pl.ds(pl.multiple_of(first, rows), rows), :] = jnp.broadcast_to(
                jnp.sum(dots, axis=1, keepdims=True), (rows, 128)
            )

    @pl.when(step == steps - 1)
    def _():
        out_gain_a[...] = sums[...].T[0:1] / gain_attn[...]

    for l in range(4):
        out_gain_m[:, l * 128 : l * 128 + 128] = small[0, tiles, l : l + 1]
    for j in range(8):
        out_ctrl[j // 4 * 8 : j // 4 * 8 + 8, j % 4 * 128 : j % 4 * 128 + 128] = small[j // tiles, j % tiles]


def on_device(
    ng, ndp, nx,
    tokens, cotangent, w_qkv, w_out, gain_attn, gain_mix, w_ctrl, w_in, w_back, prefix, group_ids,
):
    nc = ng // 2
    width = tokens.shape[2]
    half = width // 2
    length, own = ng * BLOCK, nc * BLOCK
    ff = w_in.shape[2]
    cols = ng * 2 * nc
    n1, plane = nc // 2, 2 * nc
    tile = min(512, ff)
    tiles = 8 // nc
    vm = pltpu.VMEM
    anywhere = pl.BlockSpec(memory_space=pl.ANY)
    in_vmem = pl.BlockSpec(memory_space=pltpu.VMEM)
    in_smem = pl.BlockSpec(memory_space=pltpu.SMEM)
    scratch = [
        pltpu.SemaphoreType.DMA((SEMS,)),
        pltpu.SemaphoreType.DMA((SEMS,)),
        pltpu.SemaphoreType.DMA((48,)),
        vm((nc, 2, BLOCK, width), BF16),
        vm((nc, BLOCK, width), BF16),
        vm((nc, 8, 128), jnp.int32),
        vm((nc, 8, 128), jnp.int32),
        vm((width, half), BF16),
        vm((width, half), BF16),
        vm((width, half), BF16),
        vm((2, half, width), BF16),
        vm((width, ff), BF16),
        vm((ff, width), BF16),
        vm((nc, 2, BLOCK, width), BF16),
        vm((nc, 2, BLOCK, half), BF16),
        vm((nc, 2, BLOCK, half), BF16),
        vm((nc, 2, BLOCK, half), BF16),
        vm((length // 2, length // 2), F32),
        vm((nc, 2, BLOCK, half), F32),
        vm((nc, 2, BLOCK, half), BF16),
        vm((nc, BLOCK, half), BF16),
        vm((own, width), F32),
        vm((own, width), BF16),
        vm((width, cols), BF16),
        vm((own, cols), F32),
        vm((own, cols), BF16),
        vm((2, ng, 2 * nc, width), BF16),
        vm((ndp, 2, ng, 2 * nc, width), BF16),
        vm((2, ng, 2 * nc, width), BF16),
        vm((2, ng, 2 * nc, width), BF16),
        vm((nc, BLOCK, width), BF16),
        vm((own, width), F32),
        vm((own, width), F32),
        vm((2, nc, BLOCK, width), BF16),
        vm((4, nc, 2, BLOCK, 128), BF16),
        vm((length, half), F32),
        vm((length, half), F32),
        vm((nc, 2, BLOCK, half), BF16),
        vm((nc, 2, BLOCK, half), BF16),
        vm((nc, 2, BLOCK, half), BF16),
        vm((nc, BLOCK, width), BF16),
        vm((nc, BLOCK, width), BF16),
        vm((nc, BLOCK, width), BF16),
        vm((2, n1, plane, 16, half), BF16),
        vm((2, n1, plane, 16, half), BF16),
        vm((2, plane, 16, half), BF16),
        vm((2, plane, 16, half), BF16),
        vm((2, 16, half), BF16),
        vm((2, plane, 16, half), BF16),
        vm((nc, tiles + 1, 8, 128), F32),
        vm((nc, tiles + 1, 8, 128), F32),
        vm((2, tiles + 1, 8, 128), F32),
        vm((ndp, tiles + 1, 8, 128), F32),
        vm((tiles + 1, 8, 128), F32),
        vm((ff // tile, ndp * cols, tile), BF16),
        vm((ff // tile, ndp * cols, tile), BF16),
        vm((2, tile, width), BF16),
        vm((2, width, tile), BF16),
    ]
    tokens_out, token_grad, reduced, small, grad_in, grad_back = pl.pallas_call(
        functools.partial(block_kernel, ng, ndp, nx),
        out_shape=[
            jax.ShapeDtypeStruct(tokens.shape, BF16),
            jax.ShapeDtypeStruct(tokens.shape, BF16),
            jax.ShapeDtypeStruct((2, 2, n1, plane, 16, half), BF16),
            jax.ShapeDtypeStruct((nc, tiles + 1, 8, 128), F32),
            jax.ShapeDtypeStruct(w_in.shape, BF16),
            jax.ShapeDtypeStruct(w_back.shape, BF16),
        ],
        in_specs=[anywhere] * 4 + [in_vmem] * 3 + [anywhere] * 2 + [in_smem, in_vmem],
        out_specs=[anywhere] * 6,
        scratch_shapes=scratch,
        compiler_params=pltpu.CompilerParams(
            collective_id=0, has_side_effects=True, vmem_limit_bytes=60 * 1024 * 1024
        ),
        name="of_tokens_block",
    )(
        tokens, cotangent, w_qkv, w_out.reshape(2, half, width), gain_attn.reshape(1, width),
        gain_mix.reshape(1, width), w_ctrl.T, w_in, w_back, prefix, group_ids,
    )
    steps = n1 // 2

    def whole(shape):
        return pl.BlockSpec(shape, lambda s: (0,) * len(shape))

    def split(shape, axis):
        block = tuple(n // steps if i == axis else n for i, n in enumerate(shape))
        return pl.BlockSpec(block, lambda s: tuple(s if i == axis else 0 for i in range(len(shape))))

    shapes = [
        (tokens.shape, BF16), (tokens.shape, F32), ((2, half, 3 * width), F32), ((2, half, width), F32),
        ((1, width), F32), ((1, width), F32), ((16, width), F32), (w_in.shape, F32), (w_back.shape, F32),
    ]
    tokens_out, token_grad, grad_qkv, grad_out, gain_a, gain_m, ctrl, grad_in, grad_back = pl.pallas_call(
        finish_kernel,
        grid=(steps,),
        out_shape=[jax.ShapeDtypeStruct(*shape) for shape in shapes],
        in_specs=[
            split(tokens.shape, 0),
            split(tokens.shape, 0),
            pl.BlockSpec((2, 2, n1 // steps, plane, 16, half), lambda s: (0, 0, s, 0, 0, 0)),
            whole(small.shape),
            split(w_in.shape, 1),
            split(w_back.shape, 1),
            split((2, half, 3 * width), 1),
            whole((1, width)),
        ],
        out_specs=[
            split(tokens.shape, 0),
            split(tokens.shape, 0),
            split((2, half, 3 * width), 1),
            split((2, half, width), 1),
            whole((1, width)),
            whole((1, width)),
            whole((16, width)),
            split(w_in.shape, 1),
            split(w_back.shape, 1),
        ],
        scratch_shapes=[vm((width, 128), F32)],
        compiler_params=pltpu.CompilerParams(vmem_limit_bytes=60 * 1024 * 1024),
        name="finish",
    )(
        tokens_out, token_grad, reduced, small, grad_in, grad_back,
        w_qkv.reshape(2, half, 3 * width), gain_attn.reshape(1, width),
    )
    return (
        tokens_out,
        token_grad,
        grad_qkv.reshape(width, 3 * width),
        grad_out.reshape(width, width),
        gain_a.reshape(width),
        gain_m.reshape(width),
        ctrl[:ng].T,
        grad_in,
        grad_back,
    )


def solution(mesh):
    ng, ndp = mesh.shape["grp"], mesh.shape["dp"]
    in_specs = (
        P("dp", "grp", None),
        P("dp", "grp", None),
        P(),
        P(),
        P(),
        P(),
        P(),
        P("grp", None, None),
        P("grp", None, None),
        P("dp"),
        P("dp", "grp"),
    )
    out_specs = (
        P("dp", "grp", None),
        P("dp", "grp", None),
        P(),
        P(),
        P(),
        P(),
        P(),
        P("grp", None, None),
        P("grp", None, None),
    )
    return jax.shard_map(
        functools.partial(on_device, ng, ndp, 2),
        mesh=mesh, in_specs=in_specs, out_specs=out_specs, check_vma=False,
    )
```
